32 devices in a mesh: section: 2 (over y), dp: 4 (over z), mp: 4 (over x, core).
Axes of the slice: x: 2, y: 2, z: 4, core: 2. Of those that a mesh axis runs over, the one named last changes fastest.
Arguments:
- conv_input: bfloat16 [4, 64, 2, 13, 13, 384], P(None, 'dp', None, None, None, 'mp'), may hold values from -6 to 6
- group_ids: int32 [4], replicated, may hold values from 0 to 1, as said below
- conv_weight: bfloat16 [2, 3456, 256], P(None, 'dp', 'mp'), may hold values from -0.21875 to 0.21875
- conv_bias: float32 [2, 256], P(None, 'mp'), may hold values from -3 to 3
- conv_stitch: float32 [2, 2, 256], P(None, None, 'mp'), may hold values from 0.1 to 1
- fc_weight: bfloat16 [2, 9216, 4096], P(None, 'dp', 'mp'), may hold values from -0.125 to 0.125
- fc_bias: float32 [2, 4096], P(None, 'mp'), may hold values from -3 to 3
- fc_stitch: float32 [2, 2, 4096], P(None, None, 'mp'), may hold values from 0.1 to 1
- cotangent: bfloat16 [4, 64, 2, 4096], P(None, None, None, 'mp'), may hold values from -6 to 6
Outputs:
- outputs: bfloat16 [4, 64, 2, 4096], P(None, 'dp', 'section', 'mp')
- input_grad: bfloat16 [4, 64, 2, 13, 13, 384], P(None, 'dp', 'section', None, None, 'mp')
- conv_weight_grad: float32 [2, 3456, 256], P('section', 'dp', 'mp')
- conv_bias_grad: float32 [2, 256], P('section', 'mp')
- conv_stitch_grad: float32 [2, 2, 256], P('section', None, 'mp')
- fc_weight_grad: float32 [2, 9216, 4096], P('section', 'dp', 'mp')
- fc_bias_grad: float32 [2, 4096], P('section', 'mp')
- fc_stitch_grad: float32 [2, 2, 4096], P('section', None, 'mp')
The draws below stay inside these ranges and needn't reach their ends.
Inputs may be any that keep to these rules, and one draw needn't show every extreme that they name: `group_ids`: exactly one micro-batch has group 1; the others have group 0.
All inputs are finite; a program needn't handle non-finite values.
Results may differ from the reference program's by a relative error of at most 0.012.
Values may be sent and summed in bfloat16 or wider, within the bound.
No kernel may reach another device: no remote copies, remote signals or barrier semaphores. Data moves between devices by JAX's collectives and lax.ppermute only.
A program may use at most 576 MiB of HBM per device.

```python
import jax
import jax.numpy as jnp
from jax import lax

CIN = 384
COUT = 256
HIDDEN_SIZE = 4096
MAP = 13
MAP_LOW = 11
MB = 4
POOL = 6
POOL_LOW = 5
FEATS = 9216
MB_IMAGES = 64


def draw_group_ids(key, part):
    key = jax.random.fold_in(key, 11)
    order = jax.random.permutation(key, MB)
    return (order < MB // 3).astype(jnp.int32)


def block_scale(rng, shape, shards, least, largest):
    gain, own = 1.0, jax.random.fold_in(rng, 6)
    for position, shards_of in shards:
        heights = jnp.exp(jax.random.uniform(jax.random.fold_in(own, position), (shards_of,), jnp.float32, least / len(shards), largest / len(shards)))
        gain = gain * jnp.repeat(heights, shape[position] // shards_of).reshape([-1 if axis == position else 1 for axis in range(len(shape))])
    return gain


def scatter_about(key, dims, deviation, most, shards=(), kind=jnp.bfloat16):
    values = jax.random.normal(key, dims, jnp.float32) * deviation
    if len(shards) > 0:
        values = block_scale(key, dims, shards, -0.22, 0.18) * values
    return jnp.clip(values, min=-most, max=most).astype(kind)


def setup_inputs(seed: int = 0) -> dict:
    streams_of = jax.random.split(jax.random.key(seed), 10)
    conv_input = scatter_about(streams_of[0], (MB, MB_IMAGES, 2, MAP, MAP, CIN), 1.0, 6.0, ((1, 4), (5, 4)))
    group_ids = draw_group_ids(jax.random.fold_in(streams_of[9], 71), 0)
    conv_weight = scatter_about(streams_of[2], (2, 9 * CIN, COUT), (9 * CIN // 4) ** -0.5, 0.21875, ((1, 4), (2, 4)))
    conv_bias = scatter_about(streams_of[3], (2, COUT), 0.5, 3.0, ((1, 4),), jnp.float32)
    conv_stitch = jnp.clip(0.1 + 0.9 * jax.random.uniform(streams_of[4], (2, 2, COUT), jnp.float32) ** block_scale(streams_of[4], (2, 2, COUT), ((2, 4),), -0.2, 0.2), 0.1, 1.0)
    fc_weight = scatter_about(streams_of[5], (2, FEATS, HIDDEN_SIZE), (FEATS // 4) ** -0.5, 0.125, ((1, 4), (2, 4)))
    fc_bias = scatter_about(streams_of[6], (2, HIDDEN_SIZE), 0.5, 3.0, ((1, 4),), jnp.float32)
    fc_stitch = jnp.clip(0.1 + 0.9 * jax.random.uniform(streams_of[7], (2, 2, HIDDEN_SIZE), jnp.float32) ** block_scale(streams_of[7], (2, 2, HIDDEN_SIZE), ((2, 4),), -0.2, 0.2), 0.1, 1.0)
    cotangent = scatter_about(streams_of[8], (MB, MB_IMAGES, 2, HIDDEN_SIZE), 1.0, 6.0, ((3, 4),))
    return dict(conv_input=conv_input, group_ids=group_ids, conv_weight=conv_weight, conv_bias=conv_bias, conv_stitch=conv_stitch, fc_weight=fc_weight, fc_bias=fc_bias, fc_stitch=fc_stitch, cotangent=cotangent)


@jax.custom_vjp
def low(v):
    return lax.optimization_barrier(v.astype(jnp.bfloat16)).astype(jnp.float32)

@jax.custom_vjp
def low_back(v):
    return v

def low_keep(v):
    return (low(v), None)

def low_pass(kept, grad):
    return (grad,)

def back_keep(v):
    return (v, None)

def back_low(kept, grad):
    return (low(grad),)
low.defvjp(low_keep, low_pass)
low_back.defvjp(back_keep, back_low)
highest = lax.Precision.HIGHEST

def valid_maps(group_ids, map_side, pooled_side):
    low_group = group_ids == 1
    extent = jnp.where(low_group, MAP_LOW, map_side)
    pooled_extent = jnp.where(low_group, POOL_LOW, pooled_side)
    valid_rows = (jnp.arange(map_side)[None, :] < extent[:, None]).astype(jnp.float32)
    pooled_rows = (jnp.arange(pooled_side)[None, :] < pooled_extent[:, None]).astype(jnp.float32)
    return (valid_rows[:, :, None] * valid_rows[:, None, :], pooled_rows[:, :, None] * pooled_rows[:, None, :])

def pool_mean(source, pooled_side):
    running = None
    for tap_index in range(9):
        tap_row, tap_col = (tap_index // 3, tap_index % 3)
        window = source[:, :, tap_row:tap_row + 2 * pooled_side - 1:2, tap_col:tap_col + 2 * pooled_side - 1:2, :]
        running = window if running is None else running + window
    return running / 9.0

def stitch_mix(weights, tower_maps):
    extra_dims = tower_maps.ndim - 3
    shaped = weights.reshape((1,) + weights.shape[:2] + (1,) * extra_dims + weights.shape[2:])
    return lax.optimization_barrier(jnp.sum(shaped * tower_maps[:, None], axis=2))

def forward_batch(batch_acts, conv_mask, pool_mask, conv_weight, conv_bias, conv_stitch, fc_weight, fc_bias, fc_stitch):
    inputs = batch_acts * conv_mask[None, None, :, :, None]
    kernels = conv_weight.reshape(2, 3, 3, conv_weight.shape[1] // 9, conv_weight.shape[2])
    tower_outs = []
    for tower in range(2):
        tower_outs.append(lax.conv_general_dilated(inputs[:, tower], kernels[tower], (1, 1), ((1, 1), (1, 1)), dimension_numbers=('NHWC', 'HWIO', 'NHWC'), precision=highest))
    conv_out = low_back(jnp.stack(tower_outs, axis=1) + conv_bias[None, :, None, None, :])
    pooled = pool_mean(jax.nn.gelu(conv_out), POOL) * pool_mask[None, None, :, :, None]
    shared = low(low_back(stitch_mix(conv_stitch, pooled)))
    flat_rows = shared.reshape(shared.shape[0], 2, -1)
    pre_fc = jnp.einsum('ntf,tfk->ntk', flat_rows, fc_weight, precision=highest) + fc_bias[None]
    pre_fc = low_back(pre_fc)
    return stitch_mix(fc_stitch, jax.nn.gelu(pre_fc))

def reference(conv_input, group_ids, conv_weight, conv_bias, conv_stitch, fc_weight, fc_bias, fc_stitch, cotangent):
    conv_masks, pool_masks = valid_maps(group_ids, MAP, POOL)
    params = (conv_weight.astype(jnp.float32), conv_bias.astype(jnp.float32), conv_stitch.astype(jnp.float32), fc_weight.astype(jnp.float32), fc_bias.astype(jnp.float32), fc_stitch.astype(jnp.float32))

    def batch_step(totals, scan_item):
        batch_acts, conv_mask, pool_mask, cot_rows = scan_item

        def forward_fn(inputs, cw_full, cb_full, cs_full, fw_full, fb_full, fs_full):
            return forward_batch(inputs, conv_mask, pool_mask, cw_full, cb_full, cs_full, fw_full, fb_full, fs_full)
        result, pull_back = jax.vjp(forward_fn, batch_acts.astype(jnp.float32), params[0], params[1], params[2], params[3], params[4], params[5])
        all_grads = pull_back(cot_rows.astype(jnp.float32))
        totals = tuple((running + grad_part for running, grad_part in zip(totals, all_grads[1:])))
        return (totals, (result.astype(jnp.bfloat16), all_grads[0].astype(jnp.bfloat16)))
    start = tuple((jnp.zeros_like(param) for param in params))
    totals, (outputs, input_grad) = lax.scan(batch_step, start, (conv_input, conv_masks, pool_masks, cotangent))
    return (outputs, input_grad, totals[0], totals[1], totals[2], totals[3], totals[4], totals[5])
```

```python
from functools import partial

import jax
import jax.numpy as jnp
from jax import lax
from jax.experimental import pallas as pl
from jax.experimental.pallas import tpu as pltpu
from jax.sharding import PartitionSpec as P


MAP_LOW = 11
POOL_LOW = 5
SIDE = 13
POOLED = 6
CELLS = SIDE * SIDE
PLACES = POOLED * POOLED
IMG = 16
BLK = 96
GROUP = 43
WIRE = (GROUP * IMG, 4 * BLK)
BIG = 32 << 20
MID = 20 << 20
SMALL = 8 << 20
F32 = jnp.float32
BF16 = jnp.bfloat16


def swap(value, axis, bit):
    count = lax.axis_size(axis)
    return lax.ppermute(value, axis, [(i, i ^ bit) for i in range(count)])


def sum_over(value, axis):
    bit = 1
    while bit < lax.axis_size(axis):
        value = value + swap(value, axis, bit)
        bit *= 2
    return value


def relative(value, index, axis=0):
    return jnp.concatenate(
        [lax.dynamic_slice_in_dim(value, index ^ k, 1, axis) for k in range(4)], axis
    )


def lane_index(rows=IMG):
    return lax.broadcasted_iota(jnp.int32, (rows, 128), 1)


def join4(parts, lane):
    last = parts[3]
    return [jnp.where(lane < BLK, parts[j], pltpu.roll(last, 96 - 32 * j, 1)) for j in range(3)]


def last_part(tiles, lane):
    a, b, c = [pltpu.roll(tiles[j], 32 + 32 * j, 1) for j in range(3)]
    return jnp.where(lane < 32, a, jnp.where(lane < 64, b, c))


def tiles_of(row):
    return [row[:, 0:128], row[:, 128:256], row[:, 256:384]]


def exchange(rows, lane):
    rows = [tiles_of(row) for row in rows]
    out = []
    for k in range(3):
        last = rows[3][k]
        out.append(
            [
                jnp.where(lane < BLK, rows[j][k], pltpu.roll(last, 96 - 32 * j, 1))
                for j in range(3)
            ]
        )
    thirds = [last_part(rows[q], lane) for q in range(3)]
    out.append([jnp.where(lane < BLK, thirds[j], rows[3][j]) for j in range(3)])
    return [jnp.concatenate(tiles, 1) for tiles in out]


def cell_keep(cell, extent):
    row = lax.div(cell, SIDE)
    col = cell - row * SIDE
    return jnp.logical_and(row < extent, col < extent).astype(F32).astype(BF16)


def at(cell):
    return pl.ds(pl.multiple_of(cell * IMG, IMG), IMG)


def pack_kernel(sel, maps, first, second, rows):
    tower = sel[0]

    def widen(step, _):
        rows[pl.ds(step * 208, 208), :BLK] = maps[0, pl.ds(step * 208, 208), :].astype(F32)
        return 0

    lax.fori_loop(0, 26, widen, 0, unroll=2)
    lane = lane_index()

    def cell(index):
        start = 2 * index + tower
        return jnp.concatenate(
            [
                rows[pl.ds(start, 8, stride=2 * CELLS), :],
                rows[pl.ds(start + 16 * CELLS, 8, stride=2 * CELLS), :],
            ],
            0,
        ).astype(BF16)

    def fill(wire):
        def one(step, _):
            parts = [cell(jnp.minimum(step + GROUP * q, CELLS - 1)) for q in range(4)]
            wire[at(step), :] = jnp.concatenate(join4(parts, lane), 1)
            return 0

        lax.fori_loop(0, GROUP, one, 0, unroll=4)

    pl.when(pl.program_id(0) == 0)(partial(fill, first))
    pl.when(pl.program_id(0) == 1)(partial(fill, second))


def pack_maps(maps, tower, batches):
    return pl.pallas_call(
        pack_kernel,
        grid_spec=pltpu.PrefetchScalarGridSpec(
            num_scalar_prefetch=1,
            grid=(2,),
            in_specs=[pl.BlockSpec((1, IMG * CELLS * 2, BLK), lambda i, sel: (sel[1 + i], 0, 0))],
            out_specs=[pl.BlockSpec(WIRE, lambda i, sel: (0, 0))] * 2,
            scratch_shapes=[pltpu.VMEM((IMG * CELLS * 2, 128), F32)],
        ),
        out_shape=[jax.ShapeDtypeStruct(WIRE, BF16)] * 2,
        compiler_params=pltpu.CompilerParams(vmem_limit_bytes=MID),
        name="pack_maps",
    )(jnp.stack([tower, *batches]).astype(jnp.int32), maps)


def unpack_kernel(sel, w0, w1, w2, w3, maps):
    lane = lane_index()
    extent = sel[0]

    def one(step, _):
        rows = exchange([w[at(step), :] for w in (w0, w1, w2, w3)], lane)
        for q in range(4):
            cell = step + GROUP * q
            row = rows[q] * cell_keep(cell, extent)

            def store():
                maps[at(cell), :] = row

            if q < 3:
                store()
            else:
                pl.when(cell < CELLS)(store)
        return 0

    lax.fori_loop(0, GROUP, one, 0, unroll=4)


def unpack_maps(wires, extent):
    return pl.pallas_call(
        unpack_kernel,
        in_specs=[pl.BlockSpec(memory_space=pltpu.SMEM)]
        + [pl.BlockSpec(memory_space=pltpu.VMEM)] * 4,
        out_specs=pl.BlockSpec(memory_space=pltpu.VMEM),
        out_shape=jax.ShapeDtypeStruct((CELLS * IMG, 4 * BLK), BF16),
        compiler_params=pltpu.CompilerParams(vmem_limit_bytes=MID),
        name="unpack_maps",
    )(extent.reshape(1), *wires)


def pack_grad_kernel(sel, grad, *wires):
    lane = lane_index()
    extent = sel[0]

    def one(step, _):
        rows = []
        for q in range(4):
            cell = jnp.minimum(step + GROUP * q, CELLS - 1)
            rows.append(grad[at(cell), :] * cell_keep(cell, extent))
        for wire, row in zip(wires, exchange(rows, lane)):
            wire[at(step), :] = row
        return 0

    lax.fori_loop(0, GROUP, one, 0, unroll=4)


def pack_grad(grad, extent):
    return pl.pallas_call(
        pack_grad_kernel,
        in_specs=[
            pl.BlockSpec(memory_space=pltpu.SMEM),
            pl.BlockSpec(memory_space=pltpu.VMEM),
        ],
        out_specs=[pl.BlockSpec(memory_space=pltpu.VMEM)] * 4,
        out_shape=[jax.ShapeDtypeStruct(WIRE, BF16)] * 4,
        compiler_params=pltpu.CompilerParams(vmem_limit_bytes=MID),
        name="pack_grad",
    )(extent.reshape(1), grad)


def place_grad_kernel(sel, wire, *refs):
    out = refs[-1]
    lane = lane_index()

    def one(step, _):
        tiles = tiles_of(wire[at(step), :])
        for q in range(3):
            out[0, at(step + GROUP * q), :] = tiles[q][:, :BLK]
        part = last_part(tiles, lane)[:, :BLK]
        cell = step + GROUP * 3

        @pl.when(cell < CELLS)
        def _():
            out[0, at(cell), :] = part

        return 0

    lax.fori_loop(0, GROUP, one, 0, unroll=4)


def place_grad(wire, batch, total):
    args = [batch.reshape(1).astype(jnp.int32), wire]
    in_specs = [pl.BlockSpec(WIRE, lambda i, sel: (0, 0))]
    alias = {}
    if total is not None:
        args.append(total)
        in_specs.append(pl.BlockSpec(memory_space=pl.ANY))
        alias = {2: 0}
    return pl.pallas_call(
        place_grad_kernel,
        grid_spec=pltpu.PrefetchScalarGridSpec(
            num_scalar_prefetch=1,
            grid=(1,),
            in_specs=in_specs,
            out_specs=pl.BlockSpec((1, CELLS * IMG, BLK), lambda i, sel: (sel[0], 0, 0)),
        ),
        out_shape=jax.ShapeDtypeStruct((4, CELLS * IMG, BLK), BF16),
        input_output_aliases=alias,
        compiler_params=pltpu.CompilerParams(vmem_limit_bytes=SMALL),
        name="place_grad",
    )(*args)


def kernels_kernel(sel, *refs):
    blocks, (rows_out, extra_out) = refs[:8], refs[8:]
    d, m = sel[0], sel[1]
    odd = lax.rem(m, 2) == 1
    for k in range(4):
        for x in range(2):
            own = blocks[k][x].astype(F32)
            other = blocks[4 + k][x].astype(F32)
            even_rows = jnp.where(odd, other, own)
            odd_rows = jnp.where(odd, own, other)
            turned = jnp.concatenate([even_rows, odd_rows], 0).T.astype(BF16)
            tile = pl.multiple_of((lax.div(m, 2) ^ x) * 128, 128)
            for part in range(9):
                index = 9 * (d ^ k) + part
                first = lax.div(index, 4) * (4 * BLK)
                block = lax.rem(index, 4) ^ m
                for piece in range(3):
                    place = first + jnp.where(
                        block == 3, 128 * piece + BLK, 128 * block + 32 * piece
                    )
                    start = part * BLK + 32 * piece
                    rows_out[pl.ds(pl.multiple_of(place, 32), 32), pl.ds(tile, 128)] = turned[
                        start : start + 32
                    ]
            if k == 0:
                extra_out[:, pl.ds(tile, 128)] = turned[9 * BLK : 9 * BLK + 32]


def gather_kernels(conv_weight, extras, s, d, m):
    own = lax.dynamic_index_in_dim(conv_weight.transpose(0, 2, 1), s, 0, keepdims=False)
    rows = own.shape[1]
    count = lax.axis_size("dp")
    if count == 4:
        own = jnp.concatenate([own, extras, jnp.zeros((64, 32 - extras.shape[1]), BF16)], 1)
        near = jnp.stack([own, swap(own, "mp", 2)])
        column = [near] + [swap(near, "dp", k) for k in (1, 2, 3)]
        across = [swap(part, "mp", 1) for part in column]
        kernel, extra = pl.pallas_call(
            kernels_kernel,
            in_specs=[pl.BlockSpec(memory_space=pltpu.SMEM)]
            + [pl.BlockSpec(memory_space=pltpu.VMEM)] * 8,
            out_specs=[pl.BlockSpec(memory_space=pltpu.VMEM)] * 2,
            out_shape=[
                jax.ShapeDtypeStruct((4 * rows, 256), BF16),
                jax.ShapeDtypeStruct((32, 256), BF16),
            ],
            compiler_params=pltpu.CompilerParams(vmem_limit_bytes=BIG),
            name="kernels",
        )(jnp.stack([d, m]).astype(jnp.int32), *column, *across)
        return kernel, extra[: extras.shape[1]]
    own = jnp.concatenate([own.T, extras.T], 0)
    full = lax.all_gather(lax.all_gather(own, "dp", axis=0), "mp", axis=2, tiled=True)
    kernel = relative(full[:, :rows].reshape(9, 4, BLK, 256), m, 1)
    last = kernel[:, 3].reshape(9, 3, 32, 256)
    kernel = jnp.concatenate([kernel[:, :3], last], 2)
    return kernel.reshape(36 * BLK, 256), full[0, rows:]


def split_kernel(sel, grad, keep, send):
    d, m = sel[0], sel[1]
    odd = lax.rem(m, 2) == 1
    lane = lane_index(32)

    def one(tap, _):
        for block in range(4):
            index = tap * 4 + (block ^ m)
            part = lax.div(index, 9)
            place = ((part ^ d) * 9 + index - part * 9) * BLK
            for piece in range(3):
                start = tap * 4 * BLK + (128 * piece + BLK if block == 3 else 128 * block + 32 * piece)
                rows = grad[pl.ds(pl.multiple_of(start, 32), 32), :]
                t0, t1 = rows[:, 0:128], rows[:, 128:256]
                low = jnp.where(lane < 64, t0, pltpu.roll(t1, 64, 1)).astype(BF16)
                high = jnp.where(lane < 64, pltpu.roll(t0, 64, 1), t1).astype(BF16)
                here = pl.ds(pl.multiple_of(place + 32 * piece, 32), 32)
                keep[here, :] = jnp.where(odd, high, low)
                send[here, :] = jnp.where(odd, low, high)
        return 0

    lax.fori_loop(0, 9, one, 0)


def scatter_kernels(grad, d, m):
    count = lax.axis_size("dp")
    if count == 4:
        keep, send = pl.pallas_call(
            split_kernel,
            in_specs=[
                pl.BlockSpec(memory_space=pltpu.SMEM),
                pl.BlockSpec(memory_space=pltpu.VMEM),
            ],
            out_specs=[pl.BlockSpec(memory_space=pltpu.VMEM)] * 2,
            out_shape=[jax.ShapeDtypeStruct((36 * BLK, 128), BF16)] * 2,
            compiler_params=pltpu.CompilerParams(vmem_limit_bytes=MID),
            name="split_kernels",
        )(jnp.stack([d, m]).astype(jnp.int32), grad)
        pair = keep.astype(F32) + swap(send, "mp", 1).astype(F32)
        pair = pair.reshape(4, 9 * BLK, 128)
        total = pair[0]
        for k in (1, 2, 3):
            total = total + swap(pair[k].astype(BF16), "dp", k).astype(F32)
        turned = total.T.reshape(2, 64, 9 * BLK)
        x = lax.div(m, 2)
        mine = lax.dynamic_index_in_dim(turned, x, 0, keepdims=False)
        other = lax.dynamic_index_in_dim(turned, 1 - x, 0, keepdims=False)
        mine = mine + swap(other.astype(BF16), "mp", 2).astype(F32)
        return mine.T
    grad = grad.reshape(9, 3, 128, 256)
    last = grad[:, :, BLK:].reshape(9, 1, BLK, 256)
    grad = jnp.concatenate([grad[:, :, :BLK], last], 1)
    grad = relative(grad, m, 1).reshape(36 * BLK, 256).astype(BF16)
    grad = lax.psum_scatter(grad, "mp", scatter_dimension=1, tiled=True)
    return lax.psum_scatter(grad, "dp", scatter_dimension=0, tiled=True).astype(F32)


def all_acts(acts, place):
    return jnp.concatenate([a[:, place].reshape(4 * IMG, 256) for a in acts], 0)


def all_grads(grads):
    return jnp.concatenate([g[r] for r in range(4) for g in grads], 0)


def fc_forward_kernel(a0, a1, a2, a3, weight, own, send):
    rows = jnp.concatenate([all_acts((a0, a1, a2, a3), p) for p in range(9)], 1)
    for n in range(weight.shape[1] // 256):
        here = slice(n * 256, (n + 1) * 256)
        term = jnp.dot(rows, weight[:, here], preferred_element_type=F32)
        for r in range(4):
            for k in range(4):
                part = term[(4 * r + k) * IMG : (4 * r + k + 1) * IMG]
                if k == 0:
                    own[r, :, here] = part
                else:
                    send[k - 1, r, :, here] = part.astype(BF16)


def fc_forward(acts, weight):
    hid = weight.shape[1]
    return pl.pallas_call(
        fc_forward_kernel,
        in_specs=[pl.BlockSpec(memory_space=pltpu.VMEM)] * 5,
        out_specs=[pl.BlockSpec(memory_space=pltpu.VMEM)] * 2,
        out_shape=[
            jax.ShapeDtypeStruct((4, IMG, hid), F32),
            jax.ShapeDtypeStruct((3, 4, IMG, hid), BF16),
        ],
        compiler_params=pltpu.CompilerParams(vmem_limit_bytes=MID),
        name="fc_forward",
    )(*acts, weight)


def fc_rows_kernel(g0, g1, g2, g3, weight, keep, send):
    rows = all_grads((g0, g1, g2, g3))
    for p in range(9):
        term = lax.dot_general(
            rows,
            weight[p * 256 : (p + 1) * 256, :],
            (((1,), (1,)), ((), ())),
            preferred_element_type=F32,
        )
        term = term.reshape(4, 4, IMG, 256)
        for r in range(4):
            if r % 2 == 0:
                keep[r // 2, :, p] = term[r]
            else:
                send[r // 2, :, p] = term[r].astype(BF16)


def fc_rows(grads, weight):
    hid = weight.shape[1]
    return pl.pallas_call(
        fc_rows_kernel,
        in_specs=[pl.BlockSpec(memory_space=pltpu.VMEM)] * 5,
        out_specs=[pl.BlockSpec(memory_space=pltpu.VMEM)] * 2,
        out_shape=[
            jax.ShapeDtypeStruct((2, 4, 9, IMG, 256), F32),
            jax.ShapeDtypeStruct((2, 4, 9, IMG, 256), BF16),
        ],
        compiler_params=pltpu.CompilerParams(vmem_limit_bytes=MID),
        name="fc_rows",
    )(*grads, weight)


def fc_matrix_kernel(a0, a1, a2, a3, g0, g1, g2, g3, out, part, sent):
    grads = all_grads((g0, g1, g2, g3))

    def copy(p):
        return pltpu.make_async_copy(
            part.at[p % 3], out.at[pl.ds(p * 256, 256)], sent.at[p % 3]
        )

    for p in range(9):
        rows = all_acts((a0, a1, a2, a3), p).T
        if p >= 3:
            copy(p - 3).wait()
        part[p % 3] = jnp.dot(rows, grads, preferred_element_type=F32)
        copy(p).start()
    for p in range(6, 9):
        copy(p).wait()


def fc_matrix(acts, grads):
    hid = grads[0].shape[2]
    return pl.pallas_call(
        fc_matrix_kernel,
        in_specs=[pl.BlockSpec(memory_space=pltpu.VMEM)] * 8,
        out_specs=pl.BlockSpec(memory_space=pl.ANY),
        out_shape=jax.ShapeDtypeStruct((9 * 256, hid), F32),
        scratch_shapes=[pltpu.VMEM((3, 256, hid), F32), pltpu.SemaphoreType.DMA((3,))],
        compiler_params=pltpu.CompilerParams(vmem_limit_bytes=MID),
        name="fc_matrix",
    )(*acts, *grads)


def fc_section(shared, weight, bias, stitch, cotangent, s, d, m):
    count = lax.axis_size("dp")
    hid = weight.shape[2]
    cot = lax.dynamic_slice_in_dim(cotangent, d * IMG, IMG, 1).transpose(2, 0, 1, 3)
    cot = relative(cot, m, 1).astype(F32)
    bias_own = lax.dynamic_index_in_dim(bias, s, 0, keepdims=False)
    own_weight = lax.dynamic_index_in_dim(weight, s, 0, keepdims=False)
    if count == 4:
        parts = shared.reshape(4, 9, IMG, 256)
        chunk = [lax.dynamic_index_in_dim(parts, d ^ k, 0, keepdims=False) for k in range(4)]
        near = jnp.stack([chunk[0]] + [swap(chunk[k], "dp", k) for k in (1, 2, 3)])
        far = swap(near, "mp", 2)
        acts = [near, swap(near, "mp", 1), far, swap(far, "mp", 1)]
        pre, send = fc_forward(acts, own_weight)
        for k in (1, 2, 3):
            pre = pre + swap(send[k - 1], "dp", k).astype(F32)
    else:
        flat = shared.transpose(1, 0, 2).reshape(IMG, count, -1).transpose(1, 0, 2)
        flat = lax.all_to_all(flat, "dp", 0, 0, tiled=True)
        flat = lax.all_gather(flat, "mp", axis=0)
        flat = relative(flat, m)
        pre = jnp.einsum("rdnf,fk->drnk", flat, own_weight, preferred_element_type=F32)
        pre = lax.psum_scatter(pre.astype(BF16), "dp", scatter_dimension=0, tiled=True)
        pre = pre.reshape(4, IMG, hid).astype(F32)
    pre = pre + bias_own
    active, pull = jax.vjp(jax.nn.gelu, pre)
    to_own = lax.dynamic_index_in_dim(stitch, s, 1, keepdims=False)
    mixed = to_own[0] * cot[0] + to_own[1] * cot[1]
    pre_grad = pull(mixed)[0].astype(BF16)
    sent = active.astype(BF16)
    other = swap(sent, "section", 1).astype(F32)
    row = lax.dynamic_index_in_dim(stitch, s, 0, keepdims=False)
    by_own = lax.dynamic_index_in_dim(row, s, 0, keepdims=False)
    by_other = lax.dynamic_index_in_dim(row, 1 - s, 0, keepdims=False)
    outputs = relative((by_own * active + by_other * other).astype(BF16), m)
    cot_own = lax.dynamic_index_in_dim(cot, s, 0, keepdims=False)
    own_sum = jnp.sum(cot_own * active, (0, 1))
    other_sum = jnp.sum(cot_own * other, (0, 1))
    first = jnp.where(s == 0, own_sum, other_sum)
    second = jnp.where(s == 0, other_sum, own_sum)
    bias_sum = jnp.sum(pre_grad.astype(F32), (0, 1))
    small = sum_over(jnp.stack([first, second, bias_sum]), "dp")
    if count == 4:
        grads = [pre_grad] + [swap(pre_grad, "dp", k) for k in (1, 2, 3)]
        rows, send = fc_rows(grads, own_weight)
        rows = rows + swap(send, "mp", 1).astype(F32)
        rows = rows[0] + swap(rows[1].astype(BF16), "mp", 2).astype(F32)
        rows = rows.astype(BF16)
        back = jnp.stack([rows[0]] + [swap(rows[k], "dp", k) for k in (1, 2, 3)])
        shared_grad = relative(back, d).reshape(PLACES, IMG, 256)
        matrix = fc_matrix(acts, grads)
    else:
        grads = lax.all_gather(pre_grad, "dp", axis=0)
        rows = jnp.einsum("drnk,fk->rdnf", grads, own_weight, preferred_element_type=F32)
        rows = relative(rows, m).astype(BF16)
        rows = lax.psum_scatter(rows, "mp", scatter_dimension=0, tiled=True)[0]
        rows = lax.all_to_all(rows, "dp", 0, 0, tiled=True)
        shared_grad = rows.transpose(1, 0, 2).reshape(IMG, PLACES, 256).transpose(1, 0, 2)
        matrix = jnp.einsum("rdnf,drnk->fk", flat, grads, preferred_element_type=F32)
    return shared_grad, outputs, matrix, small


def pool_mean(cells):
    total = None
    for a in range(3):
        for b in range(3):
            part = cells[a : a + 11 : 2, b : b + 11 : 2]
            total = part if total is None else total + part
    return total / 9.0


def conv_grad_kernel(sel, own, other, slope, pooled, pooled_other, columns, out, sums):
    extent = sel[0]
    by_own, by_other = columns[0:1, :], columns[1:2, :]
    spread = []
    own_sum = other_sum = None
    for p in range(POOLED):
        line = []
        for q in range(POOLED):
            place = POOLED * p + q
            mine = own[place].astype(F32)
            crossed = other[place].astype(F32)
            keep = jnp.logical_and(p < extent, q < extent).astype(F32) / 9.0
            line.append((by_own * mine + by_other * crossed) * keep)
            first = mine * pooled[place]
            second = mine * pooled_other[place].astype(F32)
            own_sum = first if own_sum is None else own_sum + first
            other_sum = second if other_sum is None else other_sum + second
        spread.append(line)
    bias_sum = jnp.zeros((IMG, 256), F32)

    def over(values, index):
        near, far = index // 2, index // 2 - 1
        if index % 2 == 1:
            return values[near]
        if index == 0:
            return values[0]
        if near >= POOLED:
            return values[far]
        return values[near] + values[far]

    for i in range(SIDE):
        line = [over([spread[p][q] for p in range(POOLED)], i) for q in range(POOLED)]
        for j in range(SIDE):
            cell = SIDE * i + j
            value = (slope[cell] * over(line, j)).astype(BF16)
            out[cell] = value
            bias_sum = bias_sum + value.astype(F32)
    for row, total in enumerate((own_sum, other_sum, bias_sum)):
        sums[row : row + 1, :] = jnp.sum(total, 0, keepdims=True)


def conv_gradient(own, other, slope, pooled, pooled_other, columns, extent):
    return pl.pallas_call(
        conv_grad_kernel,
        in_specs=[pl.BlockSpec(memory_space=pltpu.SMEM)]
        + [pl.BlockSpec(memory_space=pltpu.VMEM)] * 6,
        out_specs=[pl.BlockSpec(memory_space=pltpu.VMEM)] * 2,
        out_shape=[
            jax.ShapeDtypeStruct((CELLS, IMG, 256), BF16),
            jax.ShapeDtypeStruct((3, 256), F32),
        ],
        compiler_params=pltpu.CompilerParams(vmem_limit_bytes=MID),
        name="conv_gradient",
    )(extent.reshape(1), own, other, slope, pooled, pooled_other, columns)


def on_device(
    conv_input,
    group_ids,
    conv_weight,
    conv_bias,
    conv_stitch,
    fc_weight,
    fc_bias,
    fc_stitch,
    cotangent,
):
    s = lax.axis_index("section")
    d = lax.axis_index("dp")
    m = lax.axis_index("mp")
    assert conv_input.shape == (4, IMG, 2, SIDE, SIDE, BLK) and lax.axis_size("mp") == 4
    low_group = lax.dynamic_index_in_dim(group_ids, m, 0, keepdims=False) == 1
    extent = jnp.where(low_group, MAP_LOW, SIDE)
    pooled_extent = jnp.where(low_group, POOL_LOW, POOLED)
    inside = jnp.arange(POOLED) < pooled_extent
    pool_map = (inside[:, None] & inside[None, :]).astype(F32)[:, :, None, None]

    by_row = conv_input.transpose(0, 1, 3, 4, 2, 5).reshape(4, IMG * CELLS * 2, BLK)
    wires = [None] * 4
    wires[3], wires[2] = pack_maps(by_row, s, (m ^ 3, m ^ 2))
    wires[1], wires[0] = pack_maps(by_row, s, (m ^ 1, m))
    arrived = [wires[0]] + [swap(wires[k], "mp", k) for k in (1, 2, 3)]

    small_params = jnp.concatenate([conv_bias, conv_stitch.reshape(4, 64)], 0)
    thirds = []
    rest = small_params
    for _ in range(3):
        piece = lax.reduce_precision(rest, 8, 7)
        thirds.append(piece.astype(BF16))
        rest = rest - piece
    extras = jnp.stack(thirds, 1).reshape(18, 64).T
    kernel, extra = gather_kernels(conv_weight, extras, s, d, m)
    params = jnp.sum(extra.astype(F32).reshape(6, 3, 256), 1)
    bias_own = lax.dynamic_index_in_dim(params, s, 0, keepdims=False)
    stitch = params[2:].reshape(2, 2, 256)

    maps = unpack_maps(arrived, extent).reshape(SIDE, SIDE, IMG, 4 * BLK)
    taps = kernel.reshape(3, 3, 4 * BLK, 256)
    conv_out = lax.conv_general_dilated(
        maps,
        taps,
        (1, 1),
        ((1, 1), (1, 1)),
        dimension_numbers=("HWNC", "HWIO", "HWNC"),
        preferred_element_type=F32,
    )
    conv_out = conv_out + bias_own
    active, pull = jax.vjp(jax.nn.gelu, conv_out)
    slope = pull(jnp.ones_like(conv_out))[0]
    pooled = pool_mean(active) * pool_map
    other = swap(pooled.astype(BF16), "section", 1)
    stitch_row = lax.dynamic_index_in_dim(stitch, s, 0, keepdims=False)
    by_own = lax.dynamic_index_in_dim(stitch_row, s, 0, keepdims=False)
    by_other = lax.dynamic_index_in_dim(stitch_row, 1 - s, 0, keepdims=False)
    shared = (by_own * pooled + by_other * other.astype(F32)).astype(BF16).reshape(PLACES, IMG, 256)

    shared_grad, outputs, matrix, fc_small = fc_section(
        shared, fc_weight, fc_bias, fc_stitch, cotangent, s, d, m
    )
    other_grad = swap(shared_grad, "section", 1)
    stitch_col = lax.dynamic_index_in_dim(stitch, s, 1, keepdims=False)
    own_col = lax.dynamic_index_in_dim(stitch_col, s, 0, keepdims=False)
    other_col = lax.dynamic_index_in_dim(stitch_col, 1 - s, 0, keepdims=False)
    conv_grad, sums = conv_gradient(
        shared_grad,
        other_grad,
        slope.reshape(CELLS, IMG, 256),
        pooled.reshape(PLACES, IMG, 256),
        other.reshape(PLACES, IMG, 256),
        jnp.stack([own_col, other_col]),
        pooled_extent,
    )
    conv_grad = conv_grad.reshape(SIDE, SIDE, IMG, 256)
    own_sum, other_sum, bias_sum = sums
    first = jnp.where(s == 0, own_sum, other_sum)
    second = jnp.where(s == 0, other_sum, own_sum)
    conv_small = sum_over(sum_over(jnp.stack([first, second, bias_sum]), "dp"), "mp")
    conv_small = lax.dynamic_slice_in_dim(conv_small, m * 64, 64, 1)

    input_part = lax.conv_general_dilated(
        conv_grad,
        taps[::-1, ::-1],
        (1, 1),
        ((1, 1), (1, 1)),
        dimension_numbers=("HWNC", "HWOI", "HWNC"),
        preferred_element_type=F32,
    )
    grad_wires = pack_grad(input_part.astype(BF16).reshape(CELLS * IMG, 4 * BLK), extent)
    returned = [grad_wires[0]] + [swap(grad_wires[k], "mp", k) for k in (1, 2, 3)]
    input_grad = None
    for k in range(4):
        input_grad = place_grad(returned[k], m ^ k, input_grad)
    input_grad = input_grad.reshape(4, 1, SIDE, SIDE, IMG, BLK).transpose(0, 4, 1, 2, 3, 5)

    kernel_grad = lax.conv_general_dilated(
        maps,
        conv_grad,
        (1, 1),
        ((1, 1), (1, 1)),
        dimension_numbers=("HWCN", "HWIO", "HWNC"),
        preferred_element_type=F32,
    )
    kernel_rows = scatter_kernels(kernel_grad.reshape(36 * BLK, 256), d, m)
    return (
        outputs[:, :, None],
        input_grad,
        kernel_rows[None],
        conv_small[2][None],
        conv_small[:2][None],
        matrix[None],
        fc_small[2][None],
        fc_small[:2][None],
    )


def solution(mesh):
    placed = (
        P(None, "dp", None, None, None, "mp"),
        P(),
        P(None, "dp", "mp"),
        P(None, "mp"),
        P(None, None, "mp"),
        P(None, "dp", "mp"),
        P(None, "mp"),
        P(None, None, "mp"),
        P(None, None, None, "mp"),
    )
    return jax.shard_map(
        on_device,
        mesh=mesh,
        in_specs=placed,
        out_specs=(
            P(None, "dp", "section", "mp"),
            P(None, "dp", "section", None, None, "mp"),
            P("section", "dp", "mp"),
            P("section", "mp"),
            P("section", None, "mp"),
            P("section", "dp", "mp"),
            P("section", "mp"),
            P("section", None, "mp"),
        ),
        check_vma=False,
    )
```

```python
from functools import partial

import jax
import jax.numpy as jnp
from jax import lax
from jax.experimental import pallas as pl
from jax.experimental.pallas import tpu as pltpu
from jax.sharding import PartitionSpec as P


MAP_LOW = 11
POOL_LOW = 5
SIDE = 13
POOLED = 6
CELLS = SIDE * SIDE
PLACES = POOLED * POOLED
IMG = 16
BLK = 96
OUT = 256
ROWS = 9 * BLK
WHOLE = (0, 13)
HALVES = ((0, 7), (7, 13))
SCOPE = 4 << 20
F32 = jnp.float32
BF16 = jnp.bfloat16
VMEM = pl.BlockSpec(memory_space=pltpu.VMEM)
SMEM = pl.BlockSpec(memory_space=pltpu.SMEM)
ANY = pl.BlockSpec(memory_space=pl.ANY)
HBM = pl.BlockSpec(memory_space=pltpu.HBM)


def swap(value, axis, bit):
    count = lax.axis_size(axis)
    return lax.ppermute(value, axis, [(i, i ^ bit) for i in range(count)])


def sum_over(value, axis):
    bit = 1
    while bit < lax.axis_size(axis):
        value = value + swap(value, axis, bit)
        bit *= 2
    return value


def relative(value, index, axis=0):
    return jnp.concatenate(
        [lax.dynamic_slice_in_dim(value, index ^ k, 1, axis) for k in range(4)], axis
    )


def scalars(*values):
    return jnp.stack(values).astype(jnp.int32)


S, D, M, GROUPS = range(4)
COST = pl.CostEstimate(flops=1, bytes_accessed=1, transcendentals=0)


def is_low(sel):
    return sel[GROUPS + sel[M]] == 1


def struct(shape, dtype):
    return jax.ShapeDtypeStruct(shape, dtype)


def call(body, name, inputs, outs, after=(), scratch=(), limit=SCOPE, specs=None, out_specs=None):
    if specs is None:
        specs = [SMEM if v.dtype == jnp.int32 else VMEM for v in inputs]
    count = len(inputs)

    def kernel(*refs):
        body(*refs[:count], *refs[count + len(after) :])

    single = not isinstance(outs, (list, tuple))
    if out_specs is None:
        out_specs = VMEM if single else [VMEM] * len(outs)
    return pl.pallas_call(
        kernel,
        in_specs=specs + [VMEM] * len(after),
        out_specs=out_specs,
        out_shape=outs if single else list(outs),
        scratch_shapes=list(scratch),
        compiler_params=pltpu.CompilerParams(vmem_limit_bytes=limit),
        cost_estimate=COST,
        name=name,
    )(*inputs, *after)


def lane_index(rows=IMG):
    return lax.broadcasted_iota(jnp.int32, (rows, 128), 1)


def join4(parts, lane):
    last = parts[3]
    return [jnp.where(lane < BLK, parts[j], pltpu.roll(last, 96 - 32 * j, 1)) for j in range(3)]


def last_part(tiles, lane):
    a, b, c = [pltpu.roll(tiles[j], 32 + 32 * j, 1) for j in range(3)]
    return jnp.where(lane < 32, a, jnp.where(lane < 64, b, c))


def tiles_of(row):
    return [row[:, 0:128], row[:, 128:256], row[:, 256:384]]


def exchange(rows, lane):
    rows = [tiles_of(row) for row in rows]
    out = []
    for k in range(3):
        last = rows[3][k]
        out.append(
            [
                jnp.where(lane < BLK, rows[j][k], pltpu.roll(last, 96 - 32 * j, 1))
                for j in range(3)
            ]
        )
    thirds = [last_part(rows[q], lane) for q in range(3)]
    out.append([jnp.where(lane < BLK, thirds[j], rows[3][j]) for j in range(3)])
    return [jnp.concatenate(tiles, 1) for tiles in out]


def chunk_cells(chunk):
    return SIDE * chunk[0], SIDE * (chunk[1] - chunk[0])


def chunk_group(chunk):
    return -(-chunk_cells(chunk)[1] // 4)


def wire_shape(chunk):
    return (chunk_group(chunk) * IMG, 4 * BLK)


def masked(row, cell, whole):
    if cell // SIDE >= MAP_LOW or cell % SIDE >= MAP_LOW:
        return row * whole
    return row


def whole_map(sel):
    return jnp.where(is_low(sel), 0.0, 1.0).astype(BF16)


def at(cell):
    return pl.ds(cell * IMG, IMG)


def pack_kernel(count, sel, maps, *refs):
    wires, token, rows = refs[count:-2], refs[-2], refs[-1]
    token[...] = jnp.zeros(token.shape, F32)
    tower = sel[S]

    def widen(step, _):
        rows[pl.ds(step * 208, 208), :BLK] = maps[0, pl.ds(step * 208, 208), :].astype(F32)
        return 0

    lax.fori_loop(0, 26, widen, 0, unroll=2)
    lane = lane_index()

    def cell(index):
        start = 2 * index + tower
        return jnp.concatenate(
            [
                rows[pl.ds(start, 8, stride=2 * CELLS), :],
                rows[pl.ds(start + 16 * CELLS, 8, stride=2 * CELLS), :],
            ],
            0,
        ).astype(BF16)

    def fill(wire):
        group = chunk_group(WHOLE)
        for step in range(group):
            parts = [cell(min(step + group * q, CELLS - 1)) for q in range(4)]
            wire[at(step), :] = jnp.concatenate(join4(parts, lane), 1)

    pl.when(pl.program_id(0) == 0)(partial(fill, wires[0]))
    pl.when(pl.program_id(0) == 1)(partial(fill, wires[1]))


def pack_maps(maps, sel, first, after=()):
    shape = wire_shape(WHOLE)
    return pl.pallas_call(
        partial(pack_kernel, len(after)),
        grid_spec=pltpu.PrefetchScalarGridSpec(
            num_scalar_prefetch=1,
            grid=(2,),
            in_specs=[pl.BlockSpec((1, IMG * CELLS * 2, BLK), lambda i, sel: (sel[M] ^ (first - i), 0, 0))]
            + [VMEM] * len(after),
            out_specs=[pl.BlockSpec(shape, lambda i, sel: (0, 0))] * 2
            + [pl.BlockSpec((8, 128), lambda i, sel: (0, 0))],
            scratch_shapes=[pltpu.VMEM((IMG * CELLS * 2, 128), F32)],
        ),
        out_shape=[struct(shape, BF16)] * 2 + [struct((8, 128), F32)],
        compiler_params=pltpu.CompilerParams(vmem_limit_bytes=12 << 20),
        cost_estimate=COST,
        name="pack_maps",
    )(sel, maps, *after)


def unpack_kernel(sel, w0, w1, w2, w3, maps):
    lane = lane_index()
    whole = whole_map(sel)
    group = chunk_group(WHOLE)
    for step in range(group):
        rows = exchange([w[at(step), :] for w in (w0, w1, w2, w3)], lane)
        for q in range(4):
            cell = step + group * q
            if cell < CELLS:
                maps[at(cell), :] = masked(rows[q], cell, whole)


def pack_grad_kernel(chunk, sel, grad, *wires):
    lane = lane_index()
    whole = whole_map(sel)
    first, cells = chunk_cells(chunk)
    group = chunk_group(chunk)
    for step in range(group):
        rows = []
        for q in range(4):
            cell = min(step + group * q, cells - 1)
            rows.append(masked(grad[at(cell), :], first + cell, whole))
        for wire, row in zip(wires, exchange(rows, lane)):
            wire[at(step), :] = row


def pack_grad(grad, sel, chunk, after=()):
    shape = struct(wire_shape(chunk), BF16)
    return call(partial(pack_grad_kernel, chunk), "pack_grad", [sel, grad], [shape] * 4, after)


def place_grad_kernel(chunk, ks, sel, *refs):
    wires = refs[: len(ks)]
    out, parts, sent = refs[-3:]
    lane = lane_index()
    first, cells = chunk_cells(chunk)
    group = chunk_group(chunk)
    copies = []
    for index, (k, wire) in enumerate(zip(ks, wires)):
        for step in range(group):
            tiles = tiles_of(wire[at(step), :])
            tiles.append(last_part(tiles, lane))
            for q in range(4):
                if step + group * q < cells:
                    parts[index, at(step + group * q), :] = tiles[q][:, :BLK]
        place = out.at[sel[M] ^ k, pl.ds(first * IMG, cells * IMG)]
        copies.append(pltpu.make_async_copy(parts.at[index], place, sent.at[index]))
        copies[-1].start()
    for copy in copies:
        copy.wait()


def place_grad(wires, sel, chunk, ks, total):
    args = [sel, *wires]
    in_specs = [SMEM] + [VMEM] * len(wires)
    alias = {}
    if total is not None:
        alias = {len(args): 0}
        args.append(total)
        in_specs.append(ANY)
    cells = chunk_cells(chunk)[1]
    return pl.pallas_call(
        partial(place_grad_kernel, chunk, ks),
        in_specs=in_specs,
        out_specs=ANY,
        out_shape=struct((4, CELLS * IMG, BLK), BF16),
        scratch_shapes=[
            pltpu.VMEM((len(ks), cells * IMG, BLK), BF16),
            pltpu.SemaphoreType.DMA((len(ks),)),
        ],
        input_output_aliases=alias,
        compiler_params=pltpu.CompilerParams(vmem_limit_bytes=8 << 20),
        cost_estimate=COST,
        name="place_grad",
    )(*args)


def join_kernel(*refs):
    for k, part in enumerate(refs[:-1]):
        refs[-1][k] = part[...]


def own_kernel(sel, weight_in, bias_in, stitch_in, out, weight, bias, stitch, done):
    copies = [
        pltpu.make_async_copy(weight_in.at[sel[S]], weight, done.at[0]),
        pltpu.make_async_copy(bias_in, bias, done.at[1]),
        pltpu.make_async_copy(stitch_in, stitch, done.at[2]),
    ]
    for copy in copies:
        copy.start()
    for copy in copies:
        copy.wait()
    out[:, :ROWS] = weight[...]
    values = jnp.concatenate([bias[...], stitch[0], stitch[1], jnp.zeros((2, 64), F32)], 0)
    pieces = []
    for _ in range(3):
        pieces.append(values.astype(BF16).astype(F32))
        values = values - pieces[-1]
    zeros = jnp.zeros((BLK, 64), F32)
    rows = jnp.concatenate([zeros, *pieces, jnp.zeros((8, 64), F32)], 0)
    last = slice(ROWS - BLK, ROWS + 32)
    tile = jnp.where(lane_index(64) < BLK, out[:, last].astype(F32), rows.T)
    out[:, last] = tile.astype(BF16)


def kernels_kernel(sel, *refs):
    rows_out, params = refs[6:]
    blocks = []
    for first, second, third in (refs[:3], refs[3:6]):
        blocks += [first.at[0], first.at[1], second, third]
    d, m = sel[D], sel[M]
    odd = lax.rem(m, 2) == 1
    for k in range(4):
        for x in range(2):
            own = blocks[k][x].astype(F32)
            other = blocks[4 + k][x].astype(F32)
            even_rows = jnp.where(odd, other, own)
            odd_rows = jnp.where(odd, own, other)
            turned = jnp.concatenate([even_rows, odd_rows], 0).T
            tile = pl.multiple_of((lax.div(m, 2) ^ x) * 128, 128)
            if k == 0:
                values = turned[ROWS : ROWS + 8] + turned[ROWS + 8 : ROWS + 16]
                params[:, pl.ds(tile, 128)] = values + turned[ROWS + 16 : ROWS + 24]
            turned = turned.astype(BF16)
            for part in range(9):
                index = 9 * (d ^ k) + part
                first = lax.div(index, 4) * (4 * BLK)
                block = lax.rem(index, 4) ^ m
                for piece in range(3):
                    place = first + jnp.where(
                        block == 3, 128 * piece + BLK, 128 * block + 32 * piece
                    )
                    start = part * BLK + 32 * piece
                    rows_out[pl.ds(pl.multiple_of(place, 32), 32), pl.ds(tile, 128)] = turned[
                        start : start + 32
                    ]


def gather_kernels(conv_weight, conv_bias, conv_stitch, sel, s, m, token):
    turned = conv_weight.transpose(0, 2, 1)
    rows = turned.shape[2]
    if lax.axis_size("dp") == 4:
        shape = struct((64, rows + 32), BF16)
        inputs = [turned, conv_bias, conv_stitch]
        own = call(
            own_kernel,
            "own_kernels",
            [sel] + [pltpu.with_memory_space_constraint(v, pltpu.HBM) for v in inputs],
            shape,
            scratch=[pltpu.VMEM((64, rows), BF16)]
            + [pltpu.VMEM(v.shape, F32) for v in inputs[1:]]
            + [pltpu.SemaphoreType.DMA((3,))],
            specs=[SMEM] + [HBM] * 3,
        )
        near = call(
            join_kernel,
            "join_kernels",
            [own, swap(own, "mp", 2)],
            struct((2, *own.shape), BF16),
            (token,),
        )
        column = [swap(near, "dp", k) for k in (1, 2, 3)]
        first = call(
            join_kernel, "join_columns", [near, column[0]], struct((2, *near.shape), BF16)
        )
        column = [first, *column[1:]]
        across = [swap(part, "mp", 1) for part in column]
        kernel, params = call(
            kernels_kernel,
            "kernels",
            [sel, *column, *across],
            [struct((4 * rows, OUT), BF16), struct((8, OUT), F32)],
        )
        return kernel, params, near
    own = lax.dynamic_index_in_dim(conv_weight, s, 0, keepdims=False)
    full = lax.all_gather(lax.all_gather(own, "dp", axis=0), "mp", axis=2, tiled=True)
    kernel = relative(full.reshape(9, 4, BLK, OUT), m, 1)
    last = kernel[:, 3].reshape(9, 3, 32, OUT)
    kernel = jnp.concatenate([kernel[:, :3], last], 2).reshape(36 * BLK, OUT)
    params = jnp.concatenate([conv_bias, conv_stitch.reshape(4, 64), jnp.zeros((2, 64), F32)], 0)
    params = lax.all_gather(params, "mp", axis=1, tiled=True)
    return kernel, params, jnp.zeros((8, 128), F32)


def split_kernel(sel, grad, small, keep, send):
    d, m = sel[D], sel[M]
    odd = lax.rem(m, 2) == 1
    lane = lane_index(32)

    def write(rows, place):
        count = rows.shape[0]
        t0, t1 = rows[:, 0:128], rows[:, 128:256]
        low = jnp.where(lane[:count] < 64, t0, pltpu.roll(t1, 64, 1)).astype(BF16)
        high = jnp.where(lane[:count] < 64, pltpu.roll(t0, 64, 1), t1).astype(BF16)
        here = pl.ds(pl.multiple_of(place, 16), count)
        keep[here, :] = jnp.where(odd, high, low)
        send[here, :] = jnp.where(odd, low, high)

    for tap in range(9):
        for block in range(4):
            index = tap * 4 + (block ^ m)
            part = lax.div(index, 9)
            place = (part ^ d) * (ROWS + 16) + (index - part * 9) * BLK
            for piece in range(3):
                start = tap * 4 * BLK + (128 * piece + BLK if block == 3 else 128 * block + 32 * piece)
                write(grad[start : start + 32, :], place + 32 * piece)
    sums = jnp.concatenate([small[...], jnp.zeros((16 - small.shape[0], OUT), F32)], 0)
    for part in range(4):
        write(sums, part * (ROWS + 16) + ROWS)


def pair_kernel(keep, arrived, own, *sends):
    size = ROWS + 16
    for k in range(4):
        here = slice(k * size, (k + 1) * size)
        total = keep[here, :].astype(F32) + arrived[here, :].astype(F32)
        if k == 0:
            own[...] = total
        else:
            sends[k - 1][...] = total.astype(BF16)


def turn_kernel(sel, own, a, b, c, mine, send):
    total = own[...] + a[...].astype(F32) + b[...].astype(F32) + c[...].astype(F32)
    total = jnp.concatenate([total, jnp.zeros((16, 128), F32)], 0).T
    low = sel[M] < 2
    mine[...] = jnp.where(low, total[:64], total[64:])
    send[...] = jnp.where(low, total[64:], total[:64]).astype(BF16)


def finish_kernel(sel, mine, arrived, rows, bias, stitch):
    rows[...] = mine[:, :ROWS] + arrived[:, :ROWS].astype(F32)
    last = slice(ROWS - BLK, ROWS + 32)
    small = (mine[:, last] + arrived[:, last].astype(F32)).T
    stitch[pl.ds(sel[S], 1), :] = small[BLK : BLK + 1]
    stitch[pl.ds(1 - sel[S], 1), :] = small[BLK + 1 : BLK + 2]
    bias[...] = small[BLK + 2 : BLK + 3]


def scatter_kernels(grad, small, sel, s, m, meanwhile):
    rows = grad.shape[0] // lax.axis_size("dp")
    small_shapes = [struct((1, 64), F32), struct((2, 64), F32)]
    if lax.axis_size("dp") == 4:
        size = ROWS + 16
        keep, send = call(
            split_kernel, "split_kernels", [sel, grad, small], [struct((4 * size, 128), BF16)] * 2
        )
        own, *sends = call(
            pair_kernel,
            "pair_kernels",
            [keep, swap(send, "mp", 1)],
            [struct((size, 128), F32)] + [struct((size, 128), BF16)] * 3,
            meanwhile(keep),
        )
        arrived = [swap(part, "dp", k) for k, part in zip((1, 2, 3), sends)]
        mine, other = call(
            turn_kernel,
            "turn_kernels",
            [sel, own, *arrived],
            [struct((64, ROWS + 32), F32), struct((64, ROWS + 32), BF16)],
        )
        result, bias, stitch = call(
            finish_kernel,
            "finish_kernels",
            [sel, mine, swap(other, "mp", 2)],
            [struct((64, ROWS), F32), *small_shapes],
        )
        return result.T, bias, stitch
    grad = grad.reshape(9, 3, 128, OUT)
    last = grad[:, :, BLK:].reshape(9, 1, BLK, OUT)
    grad = jnp.concatenate([grad[:, :, :BLK], last], 1)
    grad = relative(grad, m, 1).reshape(36 * BLK, OUT).astype(BF16)
    grad = lax.psum_scatter(grad, "mp", scatter_dimension=1, tiled=True)
    grad = lax.psum_scatter(grad, "dp", scatter_dimension=0, tiled=True).astype(F32)
    small = sum_over(sum_over(small, "dp"), "mp")
    small = lax.dynamic_slice_in_dim(small, m * 64, 64, 1)
    stitch = jnp.stack([jnp.where(s == 0, small[0], small[1]), jnp.where(s == 0, small[1], small[0])])
    meanwhile(small)
    return grad, small[2:3], stitch


def gelu_parts(value):
    scale = 0.7978845608028654
    square = value * value
    curve = jnp.tanh(scale * value * (1.0 + 0.044715 * square))
    return curve, square, scale


def gelu(value):
    curve, _, _ = gelu_parts(value)
    return 0.5 * value * (1.0 + curve)


def gelu_slope(value):
    curve, square, scale = gelu_parts(value)
    bend = (0.5 * scale) * value * (1.0 - curve * curve) * (1.0 + 0.134145 * square)
    return 0.5 * (1.0 + curve) + bend


def place_of(sel, k, p):
    return 9 * (lax.rem(sel[D], 4) ^ k) + p


def half_kernel(first, sel, pooled, out):
    for k in range(2):
        for p in range(9):
            out[k, p] = pooled[place_of(sel, first + k, p)].astype(BF16)


def pool_kernel(sel, conv_out, params, pooled, far):
    extent = jnp.where(is_low(sel), POOL_LOW, POOLED)
    shift = params[pl.ds(sel[S], 1), :]
    lines = []
    for i in range(SIDE):
        cells = [gelu(conv_out[i, j] + shift) for j in range(SIDE)]
        lines.append([cells[2 * q] + cells[2 * q + 1] + cells[2 * q + 2] for q in range(POOLED)])
        if i >= 2 and i % 2 == 0:
            p = i // 2 - 1
            for q in range(POOLED):
                total = lines[i - 2][q] + lines[i - 1][q] + lines[i][q]
                keep = jnp.logical_and(p < extent, q < extent).astype(F32) / 9.0
                total = total * keep
                pooled[POOLED * p + q] = total
    half_kernel(2, sel, pooled, far)


def slope_kernel(sel, conv_out, params, slope, token):
    token[...] = jnp.zeros(token.shape, F32)
    shift = params[pl.ds(sel[S], 1), :]
    for i in range(SIDE):
        for j in range(SIDE):
            slope[SIDE * i + j] = gelu_slope(conv_out[i, j] + shift)


def entry(params, t, u):
    return params[pl.ds(2 + 2 * t + u, 1), :]


def stitch_kernel(first, sel, pooled, other, params, *chunks):
    s = sel[S]
    by_own, by_other = entry(params, s, s), entry(params, s, 1 - s)
    for k, chunk in enumerate(chunks):
        for p in range(9):
            mixed = by_own * pooled[place_of(sel, first + k, p)] + by_other * other[k, p].astype(F32)
            chunk[p] = mixed.astype(BF16)


def conv_grad_kernel(
    sel, near, far, near_other, far_other, slope, pooled, near_pooled, far_pooled, params, out, sums, mixed
):
    extent, s = jnp.where(is_low(sel), POOL_LOW, POOLED), sel[S]
    by_own, by_other = entry(params, s, s), entry(params, 1 - s, s)
    own_sum = other_sum = jnp.zeros((IMG, OUT), F32)
    for k in range(4):
        grad = (near, far)[k // 2]
        grad_other = (near_other, far_other)[k // 2]
        pooled_other = (near_pooled, far_pooled)[k // 2]
        for p in range(9):
            place = place_of(sel, k, p)
            mine = grad[k % 2, p].astype(F32)
            mixed[place] = by_own * mine + by_other * grad_other[k % 2, p].astype(F32)
            own_sum = own_sum + mine * pooled[place]
            other_sum = other_sum + mine * pooled_other[k % 2, p].astype(F32)
    spread = []
    for p in range(POOLED):
        line = []
        for q in range(POOLED):
            keep = jnp.logical_and(p < extent, q < extent).astype(F32) / 9.0
            line.append(mixed[POOLED * p + q] * keep)
        spread.append(line)
    bias_sum = jnp.zeros((IMG, OUT), F32)

    def over(values, index):
        near, far = index // 2, index // 2 - 1
        if index % 2 == 1 or index == 0:
            return values[near]
        if near >= POOLED:
            return values[far]
        return values[near] + values[far]

    for i in range(SIDE):
        line = [over([spread[p][q] for p in range(POOLED)], i) for q in range(POOLED)]
        for j in range(SIDE):
            cell = SIDE * i + j
            value = (slope[cell] * over(line, j)).astype(BF16)
            out[cell] = value
            bias_sum = bias_sum + value.astype(F32)
    for row, total in enumerate((own_sum, other_sum, bias_sum)):
        sums[row : row + 1, :] = jnp.sum(total, 0, keepdims=True)


def all_acts(acts, place):
    return jnp.concatenate([a[:, place].reshape(4 * IMG, OUT) for a in acts], 0)


def all_grads(grads):
    return jnp.concatenate([g[r] for r in range(4) for g in grads], 0)


def load_kernel(sel, weight, out, token, done):
    token[...] = jnp.zeros(token.shape, F32)
    count = done.shape[0]
    size = weight.shape[1] // count
    copies = []
    for part in range(count):
        here = pl.ds(part * size, size)
        copies.append(pltpu.make_async_copy(weight.at[sel[S], here], out.at[here], done.at[part]))
        copies[-1].start()
    for copy in copies:
        copy.wait()


def load_matrix(weight, sel, s, after):
    if lax.axis_size("dp") != 4:
        return lax.dynamic_index_in_dim(weight, s, 0, keepdims=False), ()
    matrix, token = call(
        load_kernel,
        "load_matrix",
        [sel, pltpu.with_memory_space_constraint(weight, pltpu.HBM)],
        [struct(weight.shape[1:], BF16), struct((8, 128), F32)],
        after,
        scratch=[pltpu.SemaphoreType.DMA((9,))],
        specs=[SMEM, HBM],
    )
    return matrix, (token,)


def fc_forward_kernel(a0, a1, a2, a3, weight, own, *sends):
    rows = jnp.concatenate([all_acts((a0, a1, a2, a3), p) for p in range(9)], 1)
    for n in range(weight.shape[1] // 256):
        here = slice(n * 256, (n + 1) * 256)
        term = jnp.dot(rows, weight[:, here], preferred_element_type=F32)
        for r in range(4):
            for k in range(4):
                part = term[(4 * r + k) * IMG : (4 * r + k + 1) * IMG]
                if k == 0:
                    own[r, :, here] = part
                else:
                    sends[k - 1][r, :, here] = part.astype(BF16)


def fc_active_kernel(sel, own, a, b, c, bias, stitch, cot, grad, active, sent, sums):
    s, m = sel[S], sel[M]
    for n in range(own.shape[2] // 256):
        here = slice(n * 256, (n + 1) * 256)
        shift = bias[pl.ds(s, 1), here]
        w0, w1 = stitch[0, pl.ds(s, 1), here], stitch[1, pl.ds(s, 1), here]
        sum0 = sum1 = jnp.zeros((IMG, 256), F32)
        for r in range(4):
            value = own[r, :, here] + a[r, :, here].astype(F32)
            value = value + (b[r, :, here].astype(F32) + c[r, :, here].astype(F32)) + shift
            curve, square, scale = gelu_parts(value)
            half = 0.5 * (1.0 + curve)
            bend = (0.5 * scale) * value * (1.0 - curve * curve) * (1.0 + 0.134145 * square)
            result = value * half
            c0, c1 = cot[0, m ^ r, :, here].astype(F32), cot[1, m ^ r, :, here].astype(F32)
            grad[r, :, here] = ((half + bend) * (w0 * c0 + w1 * c1)).astype(BF16)
            active[r, :, here] = result
            sent[r, :, here] = result.astype(BF16)
            sum0 = sum0 + c0 * result
            sum1 = sum1 + c1 * result
        for t, total in enumerate((sum0, sum1)):
            sums[4 * t + n : 4 * t + n + 1, :] = jnp.sum(total, 0, keepdims=True)


def fc_rows_kernel(g0, g1, weight, keep, send):
    rows = all_grads((g0, g1))
    for p in range(9):
        term = lax.dot_general(
            rows,
            weight[p * 256 : (p + 1) * 256, :],
            (((1,), (1,)), ((), ())),
            preferred_element_type=F32,
        )
        term = term.reshape(4, 2, IMG, 256)
        for r in range(4):
            if r % 2 == 0:
                keep[r // 2, :, p] = term[r]
            else:
                send[r // 2, :, p] = term[r].astype(BF16)


def cross_kernel(keep, arrived, out):
    out[...] = (keep[1] + arrived[1].astype(F32)).astype(BF16)


def home_kernel(keep, arrived, crossed, sums, *chunks):
    high = sums[...].astype(BF16).astype(F32)
    small = jnp.concatenate([high, sums[...] - high], 0).astype(BF16)
    for k in range(2):
        total = keep[0, k] + arrived[0, k].astype(F32) + crossed[k].astype(F32)
        chunks[k][0:9] = total.astype(BF16)
        chunks[k][9] = small


def fc_matrix_kernel(a0, a1, a2, a3, g0, g1, g2, g3, out, bias, token, part, sent):
    token[...] = jnp.zeros(token.shape, F32)
    grads = all_grads((g0, g1, g2, g3))

    def copy(p):
        return pltpu.make_async_copy(part.at[p % 3], out.at[pl.ds(p * 256, 256)], sent.at[p % 3])

    for p in range(9):
        rows = all_acts((a0, a1, a2, a3), p).T
        if p >= 3:
            copy(p - 3).wait()
        part[p % 3] = jnp.dot(rows, grads, preferred_element_type=F32)
        copy(p).start()
    bias[...] = jnp.sum(grads.astype(F32), 0, keepdims=True)
    for p in range(6, 9):
        copy(p).wait()


def outputs_kernel(sel, active, arrived, stitch, out, token):
    token[...] = jnp.zeros(token.shape, F32)
    s, m = sel[S], sel[M]
    for n in range(active.shape[2] // 256):
        here = slice(n * 256, (n + 1) * 256)
        by_own = jnp.where(s == 0, stitch[0, 0:1, here], stitch[1, 1:2, here])
        by_other = jnp.where(s == 0, stitch[0, 1:2, here], stitch[1, 0:1, here])
        for r in range(4):
            mixed = by_own * active[r, :, here] + by_other * arrived[r, :, here].astype(F32)
            out[m ^ r, :, here] = mixed.astype(BF16)


def plane_sum(near, far):
    total = jnp.zeros((8, OUT), F32)
    for half in (near, far):
        for k in range(2):
            plane = half[k, 9].astype(F32)
            total = total + (plane[0:8] + plane[8:16])
    return total


def stitch_sums_kernel(sel, near, far, near_other, far_other, out, own, other):
    s = sel[S]
    own[...] = plane_sum(near, far)
    other[...] = plane_sum(near_other, far_other)
    for n in range(4):
        here = slice(n * OUT, (n + 1) * OUT)
        out[pl.ds(s, 1), here] = own[pl.ds(4 * s + n, 1), :]
        out[pl.ds(1 - s, 1), here] = other[pl.ds(4 * s + n, 1), :]


def fc_section(pooled, near, far, params, own_weight, bias, stitch, cotangent, sel, s, d, m, slope_of):
    count = lax.axis_size("dp")
    hid = own_weight.shape[1]
    cot = lax.dynamic_slice_in_dim(cotangent, d * IMG, IMG, 1).transpose(2, 0, 1, 3)
    plane = struct((9, IMG, OUT), BF16)
    block = struct((4, IMG, hid), BF16)
    token = struct((8, 128), F32)
    chunks = [None] * 4
    chunks[2:] = call(
        partial(stitch_kernel, 2), "stitch_far", [sel, pooled, far, params], [plane] * 2
    )
    chunks[:2] = call(
        partial(stitch_kernel, 0), "stitch_near", [sel, pooled, near, params], [plane] * 2, chunks[2:3]
    )
    slope, after = slope_of((chunks[0],))
    if count == 4:
        moved = [chunks[0]] + [swap(chunks[k], "dp", k) for k in (1, 2, 3)]
        own_acts = call(join_kernel, "join_acts", moved, struct((4, 9, IMG, OUT), BF16), (after,))
        far_acts = swap(own_acts, "mp", 2)
        acts = [own_acts, swap(own_acts, "mp", 1), far_acts, swap(far_acts, "mp", 1)]
        pre, *sends = call(
            fc_forward_kernel,
            "fc_forward",
            [*acts, own_weight],
            [struct((4, IMG, hid), F32)] + [block] * 3,
        )
        arrived = [swap(part, "dp", k) for k, part in zip((1, 2, 3), sends)]
    else:
        shared = by_position(chunks, d)
        flat = shared.transpose(1, 0, 2).reshape(IMG, count, -1).transpose(1, 0, 2)
        flat = lax.all_to_all(flat, "dp", 0, 0, tiled=True)
        flat = lax.all_gather(flat, "mp", axis=0)
        flat = relative(flat, m)
        pre = jnp.einsum("rdnf,fk->drnk", flat, own_weight, preferred_element_type=F32)
        pre = lax.psum_scatter(pre.astype(BF16), "dp", scatter_dimension=0, tiled=True)
        pre = pre.reshape(4, IMG, hid).astype(F32)
        arrived = [jnp.zeros(block.shape, BF16)] * 3
    pre_grad, active, sent, sums = call(
        fc_active_kernel,
        "fc_active",
        [sel, pre, *arrived, bias, stitch, cot],
        [block, struct(block.shape, F32), block, struct((8, OUT), F32)],
    )
    outputs, output_token = call(
        outputs_kernel, "outputs", [sel, active, swap(sent, "section", 1), stitch], [block, token]
    )
    half = struct((2, 10, IMG, OUT), BF16)
    if count == 4:
        grads = [pre_grad] + [swap(pre_grad, "dp", k) for k in (1, 2, 3)]
        pair = struct((2, 2, 9, IMG, OUT), F32)
        ten = struct(half.shape[1:], BF16)

        def home(ks, name, after=()):
            keep, send = call(
                fc_rows_kernel,
                "fc_rows_" + name,
                [*[grads[k] for k in ks], own_weight],
                [pair, struct(pair.shape, BF16)],
                after,
            )
            arrived = swap(send, "mp", 1)
            crossing = call(
                cross_kernel, "cross_" + name, [keep, arrived], struct(pair.shape[1:], BF16)
            )
            crossed = swap(crossing, "mp", 2)
            return call(home_kernel, "home_" + name, [keep, arrived, crossed, sums], [ten] * 2)

        first, second = home((0, 1), "near")
        near_grad = call(join_kernel, "join_near", [first, swap(second, "dp", 1)], half)
        near_back = (near_grad, swap(near_grad, "section", 1))
        first, second = home((2, 3), "far", (first, output_token))
        matrix_grad, bias_sum, after = call(
            fc_matrix_kernel,
            "fc_matrix",
            [*acts, *grads],
            [struct(own_weight.shape, F32), struct((1, hid), F32), token],
            (first,),
            scratch=[pltpu.VMEM((3, 256, hid), F32), pltpu.SemaphoreType.DMA((3,))],
            limit=10 << 20,
            out_specs=[HBM, VMEM, VMEM],
        )
        moved = [swap(first, "dp", 2), swap(second, "dp", 3)]
        far_grad = call(join_kernel, "join_far", moved, half, (after,))
        far_back = (far_grad, swap(far_grad, "section", 1))
    else:
        grads = lax.all_gather(pre_grad, "dp", axis=0)
        rows = jnp.einsum("drnk,fk->rdnf", grads, own_weight, preferred_element_type=F32)
        rows = relative(rows, m).astype(BF16)
        rows = lax.psum_scatter(rows, "mp", scatter_dimension=0, tiled=True)[0]
        rows = lax.all_to_all(rows, "dp", 0, 0, tiled=True)
        back = rows.transpose(1, 0, 2).reshape(IMG, 4, 9, OUT).transpose(1, 2, 0, 3)
        matrix_grad = jnp.einsum("rdnf,drnk->fk", flat, grads, preferred_element_type=F32)
        bias_sum = jnp.sum(grads.astype(F32), (0, 1, 2))[None]
        total = sum_over(sums, "dp")
        high = lax.reduce_precision(total, 8, 7)
        small = jnp.concatenate([high, total - high], 0).astype(BF16)
        small = jnp.stack([small] + [jnp.zeros_like(small)] * 3)
        back = jnp.concatenate([relative(back, lax.rem(d, 4)), small[:, None]], 1)
        near_back, far_back = [(part, swap(part, "section", 1)) for part in (back[:2], back[2:])]
    stitch_sum = call(
        stitch_sums_kernel,
        "stitch_sums",
        [sel, near_back[0], far_back[0], near_back[1], far_back[1]],
        struct((2, hid), F32),
        scratch=[pltpu.VMEM((8, OUT), F32)] * 2,
    )
    grads = [near_back[0], far_back[0], near_back[1], far_back[1]]
    return grads, slope, outputs, matrix_grad, bias_sum, stitch_sum


def by_position(chunks, d):
    return relative(jnp.stack(chunks), lax.rem(d, 4)).reshape(PLACES, IMG, OUT)


def conv(maps, taps, rows, form, kind=F32):
    return lax.conv_general_dilated(
        maps,
        taps,
        (1, 1),
        (rows, (1, 1)),
        dimension_numbers=form,
        preferred_element_type=F32,
    ).astype(kind)


def on_device(
    conv_input,
    group_ids,
    conv_weight,
    conv_bias,
    conv_stitch,
    fc_weight,
    fc_bias,
    fc_stitch,
    cotangent,
):
    s = lax.axis_index("section")
    d = lax.axis_index("dp")
    m = lax.axis_index("mp")
    assert conv_input.shape == (4, IMG, 2, SIDE, SIDE, BLK) and lax.axis_size("mp") == 4
    sel = jnp.concatenate([scalars(s, d, m), group_ids])

    by_row = conv_input.transpose(0, 1, 3, 4, 2, 5).reshape(4, IMG * CELLS * 2, BLK)
    by_row = pltpu.with_memory_space_constraint(by_row, pltpu.HBM)
    far3, far2, token = pack_maps(by_row, sel, 3)
    kernel, params, early = gather_kernels(conv_weight, conv_bias, conv_stitch, sel, s, m, token)
    near1, near0, token = pack_maps(by_row, sel, 1, (token, early))
    wires = [near0, swap(near1, "mp", 1), swap(far2, "mp", 2), swap(far3, "mp", 3)]

    taps = kernel.reshape(3, 3, 4 * BLK, OUT)
    maps = call(
        unpack_kernel, "unpack_maps", [sel, *wires], struct((CELLS * IMG, 4 * BLK), BF16)
    )
    maps = maps.reshape(SIDE, SIDE, IMG, 4 * BLK)
    conv_out = conv(maps, taps, (1, 1), ("HWNC", "HWIO", "HWNC"))
    half = struct((2, 9, IMG, OUT), BF16)
    pooled, far = call(
        pool_kernel, "pool", [sel, conv_out, params], [struct((PLACES, IMG, OUT), F32), half]
    )
    matrix, after = load_matrix(fc_weight, sel, s, (pooled,))
    near = call(partial(half_kernel, 0), "pool_near", [sel, pooled], half, after)
    far = swap(far, "section", 1)
    near = swap(near, "section", 1)

    def slope_of(after):
        return call(
            slope_kernel,
            "slope",
            [sel, conv_out, params],
            [struct((CELLS, IMG, OUT), F32), struct((8, 128), F32)],
            after,
        )

    back, slope, outputs, matrix_grad, fc_bias_sum, fc_stitch_sum = fc_section(
        pooled, near, far, params, matrix, fc_bias, fc_stitch, cotangent, sel, s, d, m, slope_of
    )
    conv_grad, sums = call(
        conv_grad_kernel,
        "conv_gradient",
        [sel, *back, slope, pooled, near, far, params],
        [struct((CELLS, IMG, OUT), BF16), struct((3, OUT), F32)],
        scratch=[pltpu.VMEM((PLACES, IMG, OUT), F32)],
    )
    conv_grad = conv_grad.reshape(SIDE, SIDE, IMG, OUT)

    kernel_grad = conv(maps, conv_grad, (1, 1), ("HWCN", "HWIO", "HWNC"))
    back_taps = taps[::-1, ::-1]
    wires = []

    def send_input_grad(after):
        chunk = HALVES[len(wires)]
        padding = ((1, -5), (-6, 1))[len(wires)]
        part = conv(conv_grad, back_taps, padding, ("HWNC", "HWOI", "HWNC"), BF16)
        sends = pack_grad(part.reshape(-1, 4 * BLK), sel, chunk, after)
        wires.append([sends[0]] + [swap(sends[k], "mp", k) for k in (1, 2, 3)])
        return (sends[0],)

    kernel_rows, conv_bias_sum, conv_stitch_sum = scatter_kernels(
        kernel_grad.reshape(36 * BLK, OUT), sums, sel, s, m, lambda mark: send_input_grad((mark,))
    )
    send_input_grad(())
    input_grad = place_grad(wires[0], sel, HALVES[0], (0, 1, 2, 3), None)
    input_grad = place_grad(wires[1][:2], sel, HALVES[1], (0, 1), input_grad)
    input_grad = place_grad(wires[1][2:], sel, HALVES[1], (2, 3), input_grad)
    input_grad = input_grad.reshape(4, 1, SIDE, SIDE, IMG, BLK).transpose(0, 4, 1, 2, 3, 5)
    return (
        outputs[:, :, None],
        input_grad,
        kernel_rows[None],
        conv_bias_sum,
        conv_stitch_sum[None],
        matrix_grad[None],
        fc_bias_sum,
        fc_stitch_sum[None],
    )


def solution(mesh):
    placed = (
        P(None, "dp", None, None, None, "mp"),
        P(),
        P(None, "dp", "mp"),
        P(None, "mp"),
        P(None, None, "mp"),
        P(None, "dp", "mp"),
        P(None, "mp"),
        P(None, None, "mp"),
        P(None, None, None, "mp"),
    )
    return jax.shard_map(
        on_device,
        mesh=mesh,
        in_specs=placed,
        out_specs=(
            P(None, "dp", "section", "mp"),
            P(None, "dp", "section", None, None, "mp"),
            P("section", "dp", "mp"),
            P("section", "mp"),
            P("section", None, "mp"),
            P("section", "dp", "mp"),
            P("section", "mp"),
            P("section", None, "mp"),
        ),
        check_vma=False,
    )
```

```python
from functools import partial

import jax
import jax.numpy as jnp
from jax import lax
from jax.experimental import pallas as pl
from jax.experimental.pallas import tpu as pltpu
from jax.sharding import PartitionSpec as P


MAP_LOW = 11
POOL_LOW = 5
SIDE = 13
POOLED = 6
CELLS = SIDE * SIDE
PLACES = POOLED * POOLED
IMG = 16
BLK = 96
OUT = 256
ROWS = 9 * BLK
WHOLE = (0, 13)
HALVES = ((0, 7), (7, 13))
SCOPE = 4 << 20
F32 = jnp.float32
BF16 = jnp.bfloat16
VMEM = pl.BlockSpec(memory_space=pltpu.VMEM)
SMEM = pl.BlockSpec(memory_space=pltpu.SMEM)
ANY = pl.BlockSpec(memory_space=pl.ANY)
HBM = pl.BlockSpec(memory_space=pltpu.HBM)


def swap(value, axis, bit):
    count = lax.axis_size(axis)
    return lax.ppermute(value, axis, [(i, i ^ bit) for i in range(count)])


def gather4(value):
    near = swap(value, "dp", 1)
    far = swap(value, "dp", 2)
    return [value, near, far, swap(far, "dp", 1)]


def sum_over(value, axis):
    bit = 1
    while bit < lax.axis_size(axis):
        value = value + swap(value, axis, bit)
        bit *= 2
    return value


def relative(value, index, axis=0):
    return jnp.concatenate(
        [lax.dynamic_slice_in_dim(value, index ^ k, 1, axis) for k in range(4)], axis
    )


def scalars(*values):
    return jnp.stack(values).astype(jnp.int32)


S, D, M, GROUPS = range(4)
COST = pl.CostEstimate(flops=1, bytes_accessed=1, transcendentals=0)


def is_low(sel):
    return sel[GROUPS + sel[M]] == 1


def struct(shape, dtype):
    return jax.ShapeDtypeStruct(shape, dtype)


def call(body, name, inputs, outs, after=(), scratch=(), limit=SCOPE, specs=None, out_specs=None):
    if specs is None:
        specs = [SMEM if v.dtype == jnp.int32 else VMEM for v in inputs]
    count = len(inputs)

    def kernel(*refs):
        body(*refs[:count], *refs[count + len(after) :])

    single = not isinstance(outs, (list, tuple))
    if out_specs is None:
        out_specs = VMEM if single else [VMEM] * len(outs)
    return pl.pallas_call(
        kernel,
        in_specs=specs + [VMEM] * len(after),
        out_specs=out_specs,
        out_shape=outs if single else list(outs),
        scratch_shapes=list(scratch),
        compiler_params=pltpu.CompilerParams(vmem_limit_bytes=limit),
        cost_estimate=COST,
        name=name,
    )(*inputs, *after)


def lane_index(rows=IMG):
    return lax.broadcasted_iota(jnp.int32, (rows, 128), 1)


def join4(parts, lane):
    last = parts[3]
    return [jnp.where(lane < BLK, parts[j], pltpu.roll(last, 96 - 32 * j, 1)) for j in range(3)]


def last_part(tiles, lane):
    a, b, c = [pltpu.roll(tiles[j], 32 + 32 * j, 1) for j in range(3)]
    return jnp.where(lane < 32, a, jnp.where(lane < 64, b, c))


def tiles_of(row):
    return [row[:, 0:128], row[:, 128:256], row[:, 256:384]]


def exchange(rows, lane):
    rows = [tiles_of(row) for row in rows]
    out = []
    for k in range(3):
        last = rows[3][k]
        out.append(
            [
                jnp.where(lane < BLK, rows[j][k], pltpu.roll(last, 96 - 32 * j, 1))
                for j in range(3)
            ]
        )
    thirds = [last_part(rows[q], lane) for q in range(3)]
    out.append([jnp.where(lane < BLK, thirds[j], rows[3][j]) for j in range(3)])
    return [jnp.concatenate(tiles, 1) for tiles in out]


def chunk_cells(chunk):
    return SIDE * chunk[0], SIDE * (chunk[1] - chunk[0])


def chunk_group(chunk):
    return -(-chunk_cells(chunk)[1] // 4)


def wire_shape(chunk):
    return (chunk_group(chunk) * IMG, 4 * BLK)


def masked(row, cell, whole):
    if cell // SIDE >= MAP_LOW or cell % SIDE >= MAP_LOW:
        return row * whole
    return row


def whole_map(sel):
    return jnp.where(is_low(sel), 0.0, 1.0).astype(BF16)


def at(cell):
    return pl.ds(cell * IMG, IMG)


def pack_kernel(count, sel, maps, *refs):
    wires, token, rows = refs[count:-2], refs[-2], refs[-1]
    token[...] = jnp.zeros(token.shape, F32)
    tower = sel[S]

    def widen(step, _):
        rows[pl.ds(step * 208, 208), :BLK] = maps[0, pl.ds(step * 208, 208), :].astype(F32)
        return 0

    lax.fori_loop(0, 26, widen, 0, unroll=2)
    lane = lane_index()

    def cell(index):
        start = 2 * index + tower
        return jnp.concatenate(
            [
                rows[pl.ds(start, 8, stride=2 * CELLS), :],
                rows[pl.ds(start + 16 * CELLS, 8, stride=2 * CELLS), :],
            ],
            0,
        ).astype(BF16)

    def fill(wire):
        group = chunk_group(WHOLE)
        for step in range(group):
            parts = [cell(min(step + group * q, CELLS - 1)) for q in range(4)]
            wire[at(step), :] = jnp.concatenate(join4(parts, lane), 1)

    pl.when(pl.program_id(0) == 0)(partial(fill, wires[0]))
    pl.when(pl.program_id(0) == 1)(partial(fill, wires[1]))


def pack_maps(maps, sel, first, after=()):
    shape = wire_shape(WHOLE)
    return pl.pallas_call(
        partial(pack_kernel, len(after)),
        grid_spec=pltpu.PrefetchScalarGridSpec(
            num_scalar_prefetch=1,
            grid=(2,),
            in_specs=[pl.BlockSpec((1, IMG * CELLS * 2, BLK), lambda i, sel: (sel[M] ^ (first - i), 0, 0))]
            + [VMEM] * len(after),
            out_specs=[pl.BlockSpec(shape, lambda i, sel: (0, 0))] * 2
            + [pl.BlockSpec((8, 128), lambda i, sel: (0, 0))],
            scratch_shapes=[pltpu.VMEM((IMG * CELLS * 2, 128), F32)],
        ),
        out_shape=[struct(shape, BF16)] * 2 + [struct((8, 128), F32)],
        compiler_params=pltpu.CompilerParams(vmem_limit_bytes=12 << 20),
        cost_estimate=COST,
        name="pack_maps",
    )(sel, maps, *after)


def unpack_kernel(sel, w0, w1, w2, w3, maps):
    lane = lane_index()
    whole = whole_map(sel)
    group = chunk_group(WHOLE)
    for step in range(group):
        rows = exchange([w[at(step), :] for w in (w0, w1, w2, w3)], lane)
        for q in range(4):
            cell = step + group * q
            if cell < CELLS:
                maps[at(cell), :] = masked(rows[q], cell, whole)


def pack_grad_kernel(chunk, sel, grad, *wires):
    lane = lane_index()
    whole = whole_map(sel)
    first, cells = chunk_cells(chunk)
    group = chunk_group(chunk)
    for step in range(group):
        rows = []
        for q in range(4):
            cell = min(step + group * q, cells - 1)
            rows.append(masked(grad[at(cell), :], first + cell, whole))
        for wire, row in zip(wires, exchange(rows, lane)):
            wire[at(step), :] = row


def pack_grad(grad, sel, chunk, after=()):
    shape = struct(wire_shape(chunk), BF16)
    return call(partial(pack_grad_kernel, chunk), "pack_grad", [sel, grad], [shape] * 4, after)


def place_grad_kernel(chunk, ks, sel, *refs):
    wires = refs[: len(ks)]
    out, parts, sent = refs[-3:]
    lane = lane_index()
    first, cells = chunk_cells(chunk)
    group = chunk_group(chunk)
    copies = []
    for index, (k, wire) in enumerate(zip(ks, wires)):
        for step in range(group):
            tiles = tiles_of(wire[at(step), :])
            tiles.append(last_part(tiles, lane))
            for q in range(4):
                if step + group * q < cells:
                    parts[index, at(step + group * q), :] = tiles[q][:, :BLK]
        place = out.at[sel[M] ^ k, pl.ds(first * IMG, cells * IMG)]
        copies.append(pltpu.make_async_copy(parts.at[index], place, sent.at[index]))
        copies[-1].start()
    for copy in copies:
        copy.wait()


def place_grad(wires, sel, chunk, ks, total):
    args = [sel, *wires]
    in_specs = [SMEM] + [VMEM] * len(wires)
    alias = {}
    if total is not None:
        alias = {len(args): 0}
        args.append(total)
        in_specs.append(ANY)
    cells = chunk_cells(chunk)[1]
    return pl.pallas_call(
        partial(place_grad_kernel, chunk, ks),
        in_specs=in_specs,
        out_specs=ANY,
        out_shape=struct((4, CELLS * IMG, BLK), BF16),
        scratch_shapes=[
            pltpu.VMEM((len(ks), cells * IMG, BLK), BF16),
            pltpu.SemaphoreType.DMA((len(ks),)),
        ],
        input_output_aliases=alias,
        compiler_params=pltpu.CompilerParams(vmem_limit_bytes=8 << 20),
        cost_estimate=COST,
        name="place_grad",
    )(*args)


def join_kernel(*refs):
    for k, part in enumerate(refs[:-1]):
        refs[-1][k] = part[...]


def own_kernel(sel, weight_in, bias_in, stitch_in, out, weight, bias, stitch, done):
    copies = [
        pltpu.make_async_copy(weight_in.at[sel[S]], weight, done.at[0]),
        pltpu.make_async_copy(bias_in, bias, done.at[1]),
        pltpu.make_async_copy(stitch_in, stitch, done.at[2]),
    ]
    for copy in copies:
        copy.start()
    for copy in copies:
        copy.wait()
    out[:, :ROWS] = weight[...]
    values = jnp.concatenate([bias[...], stitch[0], stitch[1], jnp.zeros((2, 64), F32)], 0)
    pieces = []
    for _ in range(3):
        pieces.append(values.astype(BF16).astype(F32))
        values = values - pieces[-1]
    zeros = jnp.zeros((BLK, 64), F32)
    rows = jnp.concatenate([zeros, *pieces, jnp.zeros((8, 64), F32)], 0)
    last = slice(ROWS - BLK, ROWS + 32)
    tile = jnp.where(lane_index(64) < BLK, out[:, last].astype(F32), rows.T)
    out[:, last] = tile.astype(BF16)


def kernels_kernel(sel, *refs):
    rows_out, params = refs[6:]
    blocks = []
    for first, second, third in (refs[:3], refs[3:6]):
        blocks += [first.at[0], first.at[1], second, third]
    d, m = sel[D], sel[M]
    odd = lax.rem(m, 2) == 1
    for k in range(4):
        for x in range(2):
            own = blocks[k][x].astype(F32)
            other = blocks[4 + k][x].astype(F32)
            even_rows = jnp.where(odd, other, own)
            odd_rows = jnp.where(odd, own, other)
            turned = jnp.concatenate([even_rows, odd_rows], 0).T
            tile = pl.multiple_of((lax.div(m, 2) ^ x) * 128, 128)
            if k == 0:
                values = turned[ROWS : ROWS + 8] + turned[ROWS + 8 : ROWS + 16]
                params[:, pl.ds(tile, 128)] = values + turned[ROWS + 16 : ROWS + 24]
            turned = turned.astype(BF16)
            for part in range(9):
                index = 9 * (d ^ k) + part
                first = lax.div(index, 4) * (4 * BLK)
                block = lax.rem(index, 4) ^ m
                for piece in range(3):
                    place = first + jnp.where(
                        block == 3, 128 * piece + BLK, 128 * block + 32 * piece
                    )
                    start = part * BLK + 32 * piece
                    rows_out[pl.ds(pl.multiple_of(place, 32), 32), pl.ds(tile, 128)] = turned[
                        start : start + 32
                    ]


def gather_kernels(conv_weight, conv_bias, conv_stitch, sel, s, m, token):
    turned = conv_weight.transpose(0, 2, 1)
    rows = turned.shape[2]
    if lax.axis_size("dp") == 4:
        shape = struct((64, rows + 32), BF16)
        inputs = [turned, conv_bias, conv_stitch]
        own = call(
            own_kernel,
            "own_kernels",
            [sel] + [pltpu.with_memory_space_constraint(v, pltpu.HBM) for v in inputs],
            shape,
            scratch=[pltpu.VMEM((64, rows), BF16)]
            + [pltpu.VMEM(v.shape, F32) for v in inputs[1:]]
            + [pltpu.SemaphoreType.DMA((3,))],
            specs=[SMEM] + [HBM] * 3,
        )
        near = call(
            join_kernel,
            "join_kernels",
            [own, swap(own, "mp", 2)],
            struct((2, *own.shape), BF16),
            (token,),
        )
        column = [near] + [swap(near, "dp", k) for k in (1, 2, 3)]
        first = call(join_kernel, "join_columns", column[:2], struct((2, *near.shape), BF16))
        column = [first, *column[2:]]
        across = [swap(part, "mp", 1) for part in column]
        kernel, params = call(
            kernels_kernel,
            "kernels",
            [sel, *column, *across],
            [struct((4 * rows, OUT), BF16), struct((8, OUT), F32)],
        )
        return kernel, params, near
    own = lax.dynamic_index_in_dim(conv_weight, s, 0, keepdims=False)
    full = lax.all_gather(lax.all_gather(own, "dp", axis=0), "mp", axis=2, tiled=True)
    kernel = relative(full.reshape(9, 4, BLK, OUT), m, 1)
    last = kernel[:, 3].reshape(9, 3, 32, OUT)
    kernel = jnp.concatenate([kernel[:, :3], last], 2).reshape(36 * BLK, OUT)
    params = jnp.concatenate([conv_bias, conv_stitch.reshape(4, 64), jnp.zeros((2, 64), F32)], 0)
    params = lax.all_gather(params, "mp", axis=1, tiled=True)
    return kernel, params, jnp.zeros((8, 128), F32)


def split_kernel(sel, grad, small, keep, send):
    d, m = sel[D], sel[M]
    odd = lax.rem(m, 2) == 1
    lane = lane_index(32)

    def write(rows, place):
        count = rows.shape[0]
        t0, t1 = rows[:, 0:128], rows[:, 128:256]
        low = jnp.where(lane[:count] < 64, t0, pltpu.roll(t1, 64, 1)).astype(BF16)
        high = jnp.where(lane[:count] < 64, pltpu.roll(t0, 64, 1), t1).astype(BF16)
        here = pl.ds(pl.multiple_of(place, 16), count)
        keep[here, :] = jnp.where(odd, high, low)
        send[here, :] = jnp.where(odd, low, high)

    for tap in range(9):
        for block in range(4):
            index = tap * 4 + (block ^ m)
            part = lax.div(index, 9)
            place = (part ^ d) * (ROWS + 16) + (index - part * 9) * BLK
            for piece in range(3):
                start = tap * 4 * BLK + (128 * piece + BLK if block == 3 else 128 * block + 32 * piece)
                write(grad[start : start + 32, :], place + 32 * piece)
    sums = jnp.concatenate([small[...], jnp.zeros((16 - small.shape[0], OUT), F32)], 0)
    for part in range(4):
        write(sums, part * (ROWS + 16) + ROWS)


def pair_kernel(keep, arrived, own, *sends):
    size = ROWS + 16
    for k in range(4):
        here = slice(k * size, (k + 1) * size)
        total = keep[here, :].astype(F32) + arrived[here, :].astype(F32)
        if k == 0:
            own[...] = total
        else:
            sends[k - 1][...] = total.astype(BF16)


def turn_kernel(sel, own, a, b, c, mine, send):
    total = own[...] + a[...].astype(F32) + b[...].astype(F32) + c[...].astype(F32)
    total = jnp.concatenate([total, jnp.zeros((16, 128), F32)], 0).T
    low = sel[M] < 2
    mine[...] = jnp.where(low, total[:64], total[64:])
    send[...] = jnp.where(low, total[64:], total[:64]).astype(BF16)


def finish_kernel(sel, mine, arrived, rows, bias, stitch):
    rows[...] = mine[:, :ROWS] + arrived[:, :ROWS].astype(F32)
    last = slice(ROWS - BLK, ROWS + 32)
    small = (mine[:, last] + arrived[:, last].astype(F32)).T
    stitch[pl.ds(sel[S], 1), :] = small[BLK : BLK + 1]
    stitch[pl.ds(1 - sel[S], 1), :] = small[BLK + 1 : BLK + 2]
    bias[...] = small[BLK + 2 : BLK + 3]


def scatter_kernels(grad, small, sel, s, m, meanwhile):
    rows = grad.shape[0] // lax.axis_size("dp")
    small_shapes = [struct((1, 64), F32), struct((2, 64), F32)]
    if lax.axis_size("dp") == 4:
        size = ROWS + 16
        keep, send = call(
            split_kernel, "split_kernels", [sel, grad, small], [struct((4 * size, 128), BF16)] * 2
        )
        own, *sends = call(
            pair_kernel,
            "pair_kernels",
            [keep, swap(send, "mp", 1)],
            [struct((size, 128), F32)] + [struct((size, 128), BF16)] * 3,
            meanwhile(),
        )
        arrived = [swap(part, "dp", k) for k, part in zip((1, 2, 3), sends)]
        mine, other = call(
            turn_kernel,
            "turn_kernels",
            [sel, own, *arrived],
            [struct((64, ROWS + 32), F32), struct((64, ROWS + 32), BF16)],
        )
        result, bias, stitch = call(
            finish_kernel,
            "finish_kernels",
            [sel, mine, swap(other, "mp", 2)],
            [struct((64, ROWS), F32), *small_shapes],
        )
        return result.T, bias, stitch
    grad = grad.reshape(9, 3, 128, OUT)
    last = grad[:, :, BLK:].reshape(9, 1, BLK, OUT)
    grad = jnp.concatenate([grad[:, :, :BLK], last], 1)
    grad = relative(grad, m, 1).reshape(36 * BLK, OUT).astype(BF16)
    grad = lax.psum_scatter(grad, "mp", scatter_dimension=1, tiled=True)
    grad = lax.psum_scatter(grad, "dp", scatter_dimension=0, tiled=True).astype(F32)
    small = sum_over(sum_over(small, "dp"), "mp")
    small = lax.dynamic_slice_in_dim(small, m * 64, 64, 1)
    stitch = jnp.stack([jnp.where(s == 0, small[0], small[1]), jnp.where(s == 0, small[1], small[0])])
    meanwhile()
    return grad, small[2:3], stitch


def gelu_parts(value):
    scale = 0.7978845608028654
    square = value * value
    curve = jnp.tanh(scale * value * (1.0 + 0.044715 * square))
    return curve, square, scale


def gelu(value):
    curve, _, _ = gelu_parts(value)
    return 0.5 * value * (1.0 + curve)


def gelu_slope(value):
    curve, square, scale = gelu_parts(value)
    bend = (0.5 * scale) * value * (1.0 - curve * curve) * (1.0 + 0.134145 * square)
    return 0.5 * (1.0 + curve) + bend


def place_of(sel, k, p):
    return 9 * (lax.rem(sel[D], 4) ^ k) + p


def half_kernel(first, sel, pooled, out):
    for k in range(2):
        for p in range(9):
            out[k, p] = pooled[place_of(sel, first + k, p)].astype(BF16)


def pool_kernel(sel, conv_out, params, pooled, far):
    extent = jnp.where(is_low(sel), POOL_LOW, POOLED)
    shift = params[pl.ds(sel[S], 1), :]
    lines = []
    for i in range(SIDE):
        cells = [gelu(conv_out[i, j] + shift) for j in range(SIDE)]
        lines.append([cells[2 * q] + cells[2 * q + 1] + cells[2 * q + 2] for q in range(POOLED)])
        if i >= 2 and i % 2 == 0:
            p = i // 2 - 1
            for q in range(POOLED):
                total = lines[i - 2][q] + lines[i - 1][q] + lines[i][q]
                keep = jnp.logical_and(p < extent, q < extent).astype(F32) / 9.0
                total = total * keep
                pooled[POOLED * p + q] = total
    half_kernel(2, sel, pooled, far)


def slope_kernel(sel, conv_out, params, slope):
    shift = params[pl.ds(sel[S], 1), :]
    for i in range(SIDE):
        for j in range(SIDE):
            slope[SIDE * i + j] = gelu_slope(conv_out[i, j] + shift)


def entry(params, t, u):
    return params[pl.ds(2 + 2 * t + u, 1), :]


def stitch_kernel(first, sel, pooled, other, params, *chunks):
    s = sel[S]
    by_own, by_other = entry(params, s, s), entry(params, s, 1 - s)
    for k, chunk in enumerate(chunks):
        for p in range(9):
            mixed = by_own * pooled[place_of(sel, first + k, p)] + by_other * other[k, p].astype(F32)
            chunk[p] = mixed.astype(BF16)


def conv_grad_kernel(
    sel, near, far, near_other, far_other, slope, pooled, near_pooled, far_pooled, params, out, sums, mixed
):
    extent, s = jnp.where(is_low(sel), POOL_LOW, POOLED), sel[S]
    by_own, by_other = entry(params, s, s), entry(params, 1 - s, s)
    own_sum = other_sum = jnp.zeros((IMG, OUT), F32)
    for k in range(4):
        grad = near.at[k] if k < 3 else far
        grad_other = near_other.at[k] if k < 3 else far_other
        pooled_other = (near_pooled, far_pooled)[k // 2]
        for p in range(9):
            place = place_of(sel, k, p)
            mine = grad[p].astype(F32)
            mixed[place] = by_own * mine + by_other * grad_other[p].astype(F32)
            own_sum = own_sum + mine * pooled[place]
            other_sum = other_sum + mine * pooled_other[k % 2, p].astype(F32)
    spread = []
    for p in range(POOLED):
        line = []
        for q in range(POOLED):
            keep = jnp.logical_and(p < extent, q < extent).astype(F32) / 9.0
            line.append(mixed[POOLED * p + q] * keep)
        spread.append(line)
    bias_sum = jnp.zeros((IMG, OUT), F32)

    def over(values, index):
        near, far = index // 2, index // 2 - 1
        if index % 2 == 1 or index == 0:
            return values[near]
        if near >= POOLED:
            return values[far]
        return values[near] + values[far]

    for i in range(SIDE):
        line = [over([spread[p][q] for p in range(POOLED)], i) for q in range(POOLED)]
        for j in range(SIDE):
            cell = SIDE * i + j
            value = (slope[cell] * over(line, j)).astype(BF16)
            out[cell] = value
            bias_sum = bias_sum + value.astype(F32)
    for row, total in enumerate((own_sum, other_sum, bias_sum)):
        sums[row : row + 1, :] = jnp.sum(total, 0, keepdims=True)


def all_acts(acts, place):
    return jnp.concatenate([a[:, place].reshape(4 * IMG, OUT) for a in acts], 0)


def all_grads(grads):
    return jnp.concatenate([g[r] for r in range(4) for g in grads], 0)


def load_kernel(sel, weight, out, token, done):
    token[...] = jnp.zeros(token.shape, F32)
    count = done.shape[0]
    size = weight.shape[1] // count
    copies = []
    for part in range(count):
        here = pl.ds(part * size, size)
        copies.append(pltpu.make_async_copy(weight.at[sel[S], here], out.at[here], done.at[part]))
        copies[-1].start()
    for copy in copies:
        copy.wait()


def load_matrix(weight, sel, s, after):
    if lax.axis_size("dp") != 4:
        return lax.dynamic_index_in_dim(weight, s, 0, keepdims=False), ()
    matrix, token = call(
        load_kernel,
        "load_matrix",
        [sel, pltpu.with_memory_space_constraint(weight, pltpu.HBM)],
        [struct(weight.shape[1:], BF16), struct((8, 128), F32)],
        after,
        scratch=[pltpu.SemaphoreType.DMA((9,))],
        specs=[SMEM, HBM],
    )
    return matrix, (token,)


def fc_forward_kernel(a0, a1, a2, a3, weight, own, *sends):
    rows = jnp.concatenate([all_acts((a0, a1, a2, a3), p) for p in range(9)], 1)
    for n in range(weight.shape[1] // 256):
        here = slice(n * 256, (n + 1) * 256)
        term = jnp.dot(rows, weight[:, here], preferred_element_type=F32)
        for r in range(4):
            for k in range(4):
                part = term[(4 * r + k) * IMG : (4 * r + k + 1) * IMG]
                if k == 0:
                    own[r, :, here] = part
                else:
                    sends[k - 1][r, :, here] = part.astype(BF16)


def fc_active_kernel(sel, own, a, b, c, bias, stitch, cot, grad, active, sent, sums):
    s, m = sel[S], sel[M]
    for n in range(own.shape[2] // 256):
        here = slice(n * 256, (n + 1) * 256)
        shift = bias[pl.ds(s, 1), here]
        w0, w1 = stitch[0, pl.ds(s, 1), here], stitch[1, pl.ds(s, 1), here]
        sum0 = sum1 = jnp.zeros((IMG, 256), F32)
        for r in range(4):
            value = own[r, :, here] + a[r, :, here].astype(F32)
            value = value + (b[r, :, here].astype(F32) + c[r, :, here].astype(F32)) + shift
            curve, square, scale = gelu_parts(value)
            half = 0.5 * (1.0 + curve)
            bend = (0.5 * scale) * value * (1.0 - curve * curve) * (1.0 + 0.134145 * square)
            result = value * half
            c0, c1 = cot[0, m ^ r, :, here].astype(F32), cot[1, m ^ r, :, here].astype(F32)
            grad[r, :, here] = ((half + bend) * (w0 * c0 + w1 * c1)).astype(BF16)
            active[r, :, here] = result
            sent[r, :, here] = result.astype(BF16)
            sum0 = sum0 + c0 * result
            sum1 = sum1 + c1 * result
        for t, total in enumerate((sum0, sum1)):
            sums[4 * t + n : 4 * t + n + 1, :] = jnp.sum(total, 0, keepdims=True)


def fc_rows_kernel(*refs):
    grads, (weight, keep, send) = refs[:-3], refs[-3:]
    rows = all_grads(grads)
    for p in range(9):
        term = lax.dot_general(
            rows,
            weight[p * 256 : (p + 1) * 256, :],
            (((1,), (1,)), ((), ())),
            preferred_element_type=F32,
        )
        term = term.reshape(4, len(grads), IMG, 256)
        for r in range(4):
            if r % 2 == 0:
                keep[r // 2, :, p] = term[r]
            else:
                send[r // 2, :, p] = term[r].astype(BF16)


def cross_kernel(keep, arrived, out):
    out[...] = (keep[1] + arrived[1].astype(F32)).astype(BF16)


def home_kernel(keep, arrived, crossed, sums, *chunks):
    high = sums[...].astype(BF16).astype(F32)
    small = jnp.concatenate([high, sums[...] - high], 0).astype(BF16)
    for k in range(len(chunks)):
        total = keep[0, k] + arrived[0, k].astype(F32) + crossed[k].astype(F32)
        chunks[k][0:9] = total.astype(BF16)
        chunks[k][9] = small


def fc_matrix_kernel(a0, a1, a2, a3, g0, g1, g2, g3, out, bias, token, part, sent):
    token[...] = jnp.zeros(token.shape, F32)
    grads = all_grads((g0, g1, g2, g3))

    def copy(p):
        return pltpu.make_async_copy(part.at[p % 3], out.at[pl.ds(p * 256, 256)], sent.at[p % 3])

    for p in range(9):
        rows = all_acts((a0, a1, a2, a3), p).T
        if p >= 3:
            copy(p - 3).wait()
        part[p % 3] = jnp.dot(rows, grads, preferred_element_type=F32)
        copy(p).start()
    bias[...] = jnp.sum(grads.astype(F32), 0, keepdims=True)
    for p in range(6, 9):
        copy(p).wait()


def copy_kernel(value, out):
    out[...] = value[...]


def outputs_kernel(sel, active, arrived, stitch, out):
    s, m = sel[S], sel[M]
    for n in range(active.shape[2] // 256):
        here = slice(n * 256, (n + 1) * 256)
        by_own = jnp.where(s == 0, stitch[0, 0:1, here], stitch[1, 1:2, here])
        by_other = jnp.where(s == 0, stitch[0, 1:2, here], stitch[1, 0:1, here])
        for r in range(4):
            mixed = by_own * active[r, :, here] + by_other * arrived[r, :, here].astype(F32)
            out[m ^ r, :, here] = mixed.astype(BF16)


def plane_sum(near, far):
    total = jnp.zeros((8, OUT), F32)
    for plane in (near[0, 9], near[1, 9], near[2, 9], far[9]):
        plane = plane.astype(F32)
        total = total + (plane[0:8] + plane[8:16])
    return total


def stitch_sums_kernel(sel, near, far, near_other, far_other, out, own, other):
    s = sel[S]
    own[...] = plane_sum(near, far)
    other[...] = plane_sum(near_other, far_other)
    for n in range(4):
        here = slice(n * OUT, (n + 1) * OUT)
        out[pl.ds(s, 1), here] = own[pl.ds(4 * s + n, 1), :]
        out[pl.ds(1 - s, 1), here] = other[pl.ds(4 * s + n, 1), :]


def fc_section(pooled, near, far, params, own_weight, bias, stitch, cot, sel, s, d, m):
    count = lax.axis_size("dp")
    hid = own_weight.shape[1]
    plane = struct((9, IMG, OUT), BF16)
    block = struct((4, IMG, hid), BF16)
    token = struct((8, 128), F32)
    chunks = [None] * 4
    chunks[2:] = call(
        partial(stitch_kernel, 2), "stitch_far", [sel, pooled, far, params], [plane] * 2
    )
    chunks[:2] = call(
        partial(stitch_kernel, 0), "stitch_near", [sel, pooled, near, params], [plane] * 2, chunks[2:3]
    )
    if count == 4:
        moved = [chunks[0]] + [swap(chunks[k], "dp", k) for k in (1, 2, 3)]
        own_acts = call(join_kernel, "join_acts", moved, struct((4, 9, IMG, OUT), BF16))
        far_acts = swap(own_acts, "mp", 2)
        acts = [own_acts, swap(own_acts, "mp", 1), far_acts, swap(far_acts, "mp", 1)]
        pre, *sends = call(
            fc_forward_kernel,
            "fc_forward",
            [*acts, own_weight],
            [struct((4, IMG, hid), F32)] + [block] * 3,
        )
        arrived = [swap(part, "dp", k) for k, part in zip((1, 2, 3), sends)]
    else:
        shared = by_position(chunks, d)
        flat = shared.transpose(1, 0, 2).reshape(IMG, count, -1).transpose(1, 0, 2)
        flat = lax.all_to_all(flat, "dp", 0, 0, tiled=True)
        flat = lax.all_gather(flat, "mp", axis=0)
        flat = relative(flat, m)
        pre = jnp.einsum("rdnf,fk->drnk", flat, own_weight, preferred_element_type=F32)
        pre = lax.psum_scatter(pre.astype(BF16), "dp", scatter_dimension=0, tiled=True)
        pre = pre.reshape(4, IMG, hid).astype(F32)
        arrived = [jnp.zeros(block.shape, BF16)] * 3
    pre_grad, active, sent, sums = call(
        fc_active_kernel,
        "fc_active",
        [sel, pre, *arrived, bias, stitch, cot],
        [block, struct(block.shape, F32), block, struct((8, OUT), F32)],
    )
    if count == 4:
        grads = gather4(pre_grad)
        ten = struct((10, IMG, OUT), BF16)

        def home(ks, name, after=()):
            shape = (2, len(ks), 9, IMG, OUT)
            keep, send = call(
                fc_rows_kernel,
                "fc_rows_" + name,
                [*[grads[k] for k in ks], own_weight],
                [struct(shape, F32), struct(shape, BF16)],
                after,
            )
            arrived = swap(send, "mp", 1)
            crossing = call(cross_kernel, "cross_" + name, [keep, arrived], struct(shape[1:], BF16))
            crossed = swap(crossing, "mp", 2)
            inputs = [keep, arrived, crossed, sums]
            return call(home_kernel, "home_" + name, inputs, [ten] * len(ks))

        chunks = home((0, 1, 2), "near")
        moved = [chunks[0], swap(chunks[1], "dp", 1), swap(chunks[2], "dp", 2)]
        (chunk,) = home((3,), "far", chunks[:1])
        matrix_grad, bias_sum, after = call(
            fc_matrix_kernel,
            "fc_matrix",
            [*acts, *grads],
            [struct(own_weight.shape, F32), struct((1, hid), F32), token],
            (chunk,),
            scratch=[pltpu.VMEM((3, 256, hid), F32), pltpu.SemaphoreType.DMA((3,))],
            limit=10 << 20,
            out_specs=[HBM, VMEM, VMEM],
        )
        near_grad = call(join_kernel, "join_near", moved, struct((3, *ten.shape), BF16), (after,))
        near_back = (near_grad, swap(near_grad, "section", 1))
        far_grad = swap(chunk, "dp", 3)
        far_back = (far_grad, swap(far_grad, "section", 1))
    else:
        grads = lax.all_gather(pre_grad, "dp", axis=0)
        rows = jnp.einsum("drnk,fk->rdnf", grads, own_weight, preferred_element_type=F32)
        rows = relative(rows, m).astype(BF16)
        rows = lax.psum_scatter(rows, "mp", scatter_dimension=0, tiled=True)[0]
        rows = lax.all_to_all(rows, "dp", 0, 0, tiled=True)
        back = rows.transpose(1, 0, 2).reshape(IMG, 4, 9, OUT).transpose(1, 2, 0, 3)
        matrix_grad = jnp.einsum("rdnf,drnk->fk", flat, grads, preferred_element_type=F32)
        bias_sum = jnp.sum(grads.astype(F32), (0, 1, 2))[None]
        total = sum_over(sums, "dp")
        high = lax.reduce_precision(total, 8, 7)
        small = jnp.concatenate([high, total - high], 0).astype(BF16)
        small = jnp.stack([small] + [jnp.zeros_like(small)] * 3)
        back = jnp.concatenate([relative(back, lax.rem(d, 4)), small[:, None]], 1)
        near_back, far_back = [(part, swap(part, "section", 1)) for part in (back[:3], back[3])]
        after = sums
    stitch_sum = call(
        stitch_sums_kernel,
        "stitch_sums",
        [sel, near_back[0], far_back[0], near_back[1], far_back[1]],
        struct((2, hid), F32),
        scratch=[pltpu.VMEM((8, OUT), F32)] * 2,
    )
    grads = [near_back[0], far_back[0], near_back[1], far_back[1]]
    return grads, after, (active, sent), matrix_grad, bias_sum, stitch_sum


def by_position(chunks, d):
    return relative(jnp.stack(chunks), lax.rem(d, 4)).reshape(PLACES, IMG, OUT)


def conv(maps, taps, rows, form, kind=F32):
    return lax.conv_general_dilated(
        maps,
        taps,
        (1, 1),
        (rows, (1, 1)),
        dimension_numbers=form,
        preferred_element_type=F32,
    ).astype(kind)


def on_device(
    conv_input,
    group_ids,
    conv_weight,
    conv_bias,
    conv_stitch,
    fc_weight,
    fc_bias,
    fc_stitch,
    cotangent,
):
    s = lax.axis_index("section")
    d = lax.axis_index("dp")
    m = lax.axis_index("mp")
    assert conv_input.shape == (4, IMG, 2, SIDE, SIDE, BLK) and lax.axis_size("mp") == 4
    sel = jnp.concatenate([scalars(s, d, m), group_ids])

    by_row = conv_input.transpose(0, 1, 3, 4, 2, 5).reshape(4, IMG * CELLS * 2, BLK)
    by_row = pltpu.with_memory_space_constraint(by_row, pltpu.HBM)
    far3, far2, token = pack_maps(by_row, sel, 3)
    kernel, params, early = gather_kernels(conv_weight, conv_bias, conv_stitch, sel, s, m, token)
    cot = lax.dynamic_slice_in_dim(cotangent, d * IMG, IMG, 1).transpose(2, 0, 1, 3)
    near1, near0, token = pack_maps(by_row, sel, 1, (token, early, cot))
    wires = [near0, swap(near1, "mp", 1), swap(far2, "mp", 2), swap(far3, "mp", 3)]

    taps = kernel.reshape(3, 3, 4 * BLK, OUT)
    maps = call(
        unpack_kernel,
        "unpack_maps",
        [sel, *wires],
        struct((CELLS * IMG, 4 * BLK), BF16),
    )
    maps = maps.reshape(SIDE, SIDE, IMG, 4 * BLK)
    conv_out = conv(maps, taps, (1, 1), ("HWNC", "HWIO", "HWNC"))
    half = struct((2, 9, IMG, OUT), BF16)
    pooled, far = call(
        pool_kernel, "pool", [sel, conv_out, params], [struct((PLACES, IMG, OUT), F32), half]
    )
    matrix, after = load_matrix(fc_weight, sel, s, (pooled,))
    near = call(partial(half_kernel, 0), "pool_near", [sel, pooled], half, after)
    far = swap(far, "section", 1)
    near = swap(near, "section", 1)

    back, after, outputs, matrix_grad, fc_bias_sum, fc_stitch_sum = fc_section(
        pooled, near, far, params, matrix, fc_bias, fc_stitch, cot, sel, s, d, m
    )
    slope = call(
        slope_kernel,
        "slope",
        [sel, conv_out, params],
        struct((CELLS, IMG, OUT), F32),
        (back[0],),
    )
    conv_grad, sums = call(
        conv_grad_kernel,
        "conv_gradient",
        [sel, *back, slope, pooled, near, far, params],
        [struct((CELLS, IMG, OUT), BF16), struct((3, OUT), F32)],
        (after,),
        scratch=[pltpu.VMEM((PLACES, IMG, OUT), F32)],
    )
    conv_grad = conv_grad.reshape(SIDE, SIDE, IMG, OUT)

    kernel_grad = conv(maps, conv_grad, (1, 1), ("HWCN", "HWIO", "HWNC"))
    back_taps = taps[::-1, ::-1]
    wires = []

    def send_input_grad(after=()):
        chunk = len(wires)
        padding = ((1, -5), (-6, 1))[chunk]
        part = conv(conv_grad, back_taps, padding, ("HWNC", "HWOI", "HWNC"), BF16)
        sends = pack_grad(part.reshape(-1, 4 * BLK), sel, HALVES[chunk], after)
        wires.append([sends[0]] + [swap(sends[k], "mp", k) for k in (1, 2, 3)])
        return (sends[0],)

    kernel_rows, conv_bias_sum, conv_stitch_sum = scatter_kernels(
        kernel_grad.reshape(36 * BLK, OUT), sums, sel, s, m, send_input_grad
    )
    mark = send_input_grad(tuple(wires[0][2:]))
    active, sent = outputs
    sent = call(copy_kernel, "outputs_send", [sent], struct(sent.shape, BF16), mark)
    outputs = call(
        outputs_kernel,
        "outputs",
        [sel, active, swap(sent, "section", 1), fc_stitch],
        struct(sent.shape, BF16),
    )
    input_grad = place_grad(wires[0], sel, HALVES[0], (0, 1, 2, 3), None)
    input_grad = place_grad(wires[1][:2], sel, HALVES[1], (0, 1), input_grad)
    input_grad = place_grad(wires[1][2:], sel, HALVES[1], (2, 3), input_grad)
    input_grad = input_grad.reshape(4, 1, SIDE, SIDE, IMG, BLK).transpose(0, 4, 1, 2, 3, 5)
    return (
        outputs[:, :, None],
        input_grad,
        kernel_rows[None],
        conv_bias_sum,
        conv_stitch_sum[None],
        matrix_grad[None],
        fc_bias_sum,
        fc_stitch_sum[None],
    )


def solution(mesh):
    placed = (
        P(None, "dp", None, None, None, "mp"),
        P(),
        P(None, "dp", "mp"),
        P(None, "mp"),
        P(None, None, "mp"),
        P(None, "dp", "mp"),
        P(None, "mp"),
        P(None, None, "mp"),
        P(None, None, None, "mp"),
    )
    return jax.shard_map(
        on_device,
        mesh=mesh,
        in_specs=placed,
        out_specs=(
            P(None, "dp", "section", "mp"),
            P(None, "dp", "section", None, None, "mp"),
            P("section", "dp", "mp"),
            P("section", "mp"),
            P("section", None, "mp"),
            P("section", "dp", "mp"),
            P("section", "mp"),
            P("section", None, "mp"),
        ),
        check_vma=False,
    )
```

```python
from functools import partial

import jax
import jax.numpy as jnp
from jax import lax
from jax.experimental import pallas as pl
from jax.experimental.pallas import tpu as pltpu
from jax.sharding import PartitionSpec as P


MAP_LOW = 11
POOL_LOW = 5
SIDE = 13
POOLED = 6
CELLS = SIDE * SIDE
PLACES = POOLED * POOLED
IMG = 16
BLK = 96
OUT = 256
ROWS = 9 * BLK
WHOLE = (0, 13)
HALVES = ((0, 7), (7, 13))
SCOPE = 4 << 20
F32 = jnp.float32
BF16 = jnp.bfloat16
VMEM = pl.BlockSpec(memory_space=pltpu.VMEM)
SMEM = pl.BlockSpec(memory_space=pltpu.SMEM)
ANY = pl.BlockSpec(memory_space=pl.ANY)
HBM = pl.BlockSpec(memory_space=pltpu.HBM)


def swap(value, axis, bit):
    count = lax.axis_size(axis)
    return lax.ppermute(value, axis, [(i, i ^ bit) for i in range(count)])


def gather4(value):
    near = swap(value, "dp", 1)
    far = swap(value, "dp", 2)
    return [value, near, far, swap(far, "dp", 1)]


def sum_over(value, axis):
    bit = 1
    while bit < lax.axis_size(axis):
        value = value + swap(value, axis, bit)
        bit *= 2
    return value


def relative(value, index, axis=0):
    return jnp.concatenate(
        [lax.dynamic_slice_in_dim(value, index ^ k, 1, axis) for k in range(4)], axis
    )


def scalars(*values):
    return jnp.stack(values).astype(jnp.int32)


S, D, M, GROUPS = range(4)
COST = pl.CostEstimate(flops=1, bytes_accessed=1, transcendentals=0)


def is_low(sel):
    return sel[GROUPS + sel[M]] == 1


def struct(shape, dtype):
    return jax.ShapeDtypeStruct(shape, dtype)


def call(body, name, inputs, outs, after=(), scratch=(), limit=SCOPE, specs=None, out_specs=None):
    if specs is None:
        specs = [SMEM if v.dtype == jnp.int32 else VMEM for v in inputs]
    count = len(inputs)

    def kernel(*refs):
        body(*refs[:count], *refs[count + len(after) :])

    single = not isinstance(outs, (list, tuple))
    if out_specs is None:
        out_specs = VMEM if single else [VMEM] * len(outs)
    return pl.pallas_call(
        kernel,
        in_specs=specs + [VMEM] * len(after),
        out_specs=out_specs,
        out_shape=outs if single else list(outs),
        scratch_shapes=list(scratch),
        compiler_params=pltpu.CompilerParams(vmem_limit_bytes=limit),
        cost_estimate=COST,
        name=name,
    )(*inputs, *after)


def pass_on(value, after):
    def kernel(*refs):
        pass

    return pl.pallas_call(
        kernel,
        in_specs=[ANY] + [VMEM] * len(after),
        out_specs=ANY,
        out_shape=struct(value.shape, value.dtype),
        input_output_aliases={0: 0},
        compiler_params=pltpu.CompilerParams(vmem_limit_bytes=SCOPE),
        cost_estimate=COST,
        name="pass_on",
    )(value, *after)


def lane_index(rows=IMG):
    return lax.broadcasted_iota(jnp.int32, (rows, 128), 1)


def join4(parts, lane):
    last = parts[3]
    return [jnp.where(lane < BLK, parts[j], pltpu.roll(last, 96 - 32 * j, 1)) for j in range(3)]


def last_part(tiles, lane):
    a, b, c = [pltpu.roll(tiles[j], 32 + 32 * j, 1) for j in range(3)]
    return jnp.where(lane < 32, a, jnp.where(lane < 64, b, c))


def tiles_of(row):
    return [row[:, 0:128], row[:, 128:256], row[:, 256:384]]


def exchange(rows, lane):
    rows = [tiles_of(row) for row in rows]
    out = []
    for k in range(3):
        last = rows[3][k]
        out.append(
            [
                jnp.where(lane < BLK, rows[j][k], pltpu.roll(last, 96 - 32 * j, 1))
                for j in range(3)
            ]
        )
    thirds = [last_part(rows[q], lane) for q in range(3)]
    out.append([jnp.where(lane < BLK, thirds[j], rows[3][j]) for j in range(3)])
    return [jnp.concatenate(tiles, 1) for tiles in out]


def chunk_cells(chunk):
    return SIDE * chunk[0], SIDE * (chunk[1] - chunk[0])


def chunk_group(chunk):
    return -(-chunk_cells(chunk)[1] // 4)


def wire_shape(chunk):
    return (chunk_group(chunk) * IMG, 4 * BLK)


def masked(row, cell, whole):
    if cell // SIDE >= MAP_LOW or cell % SIDE >= MAP_LOW:
        return row * whole
    return row


def whole_map(sel):
    return jnp.where(is_low(sel), 0.0, 1.0).astype(BF16)


def at(cell):
    return pl.ds(cell * IMG, IMG)


def pack_kernel(count, sel, maps, *refs):
    wires, token, rows = refs[count:-2], refs[-2], refs[-1]
    token[...] = jnp.zeros(token.shape, F32)
    tower = sel[S]

    def widen(step, _):
        rows[pl.ds(step * 208, 208), :BLK] = maps[0, pl.ds(step * 208, 208), :].astype(F32)
        return 0

    lax.fori_loop(0, 26, widen, 0, unroll=2)
    lane = lane_index()

    def cell(index):
        start = 2 * index + tower
        return jnp.concatenate(
            [
                rows[pl.ds(start, 8, stride=2 * CELLS), :],
                rows[pl.ds(start + 16 * CELLS, 8, stride=2 * CELLS), :],
            ],
            0,
        ).astype(BF16)

    def fill(wire):
        group = chunk_group(WHOLE)
        for step in range(group):
            parts = [cell(min(step + group * q, CELLS - 1)) for q in range(4)]
            wire[at(step), :] = jnp.concatenate(join4(parts, lane), 1)

    pl.when(pl.program_id(0) == 0)(partial(fill, wires[0]))
    pl.when(pl.program_id(0) == 1)(partial(fill, wires[1]))


def pack_maps(maps, sel, first, after=()):
    shape = wire_shape(WHOLE)
    return pl.pallas_call(
        partial(pack_kernel, len(after)),
        grid_spec=pltpu.PrefetchScalarGridSpec(
            num_scalar_prefetch=1,
            grid=(2,),
            in_specs=[pl.BlockSpec((1, IMG * CELLS * 2, BLK), lambda i, sel: (sel[M] ^ (first - i), 0, 0))]
            + [VMEM] * len(after),
            out_specs=[pl.BlockSpec(shape, lambda i, sel: (0, 0))] * 2
            + [pl.BlockSpec((8, 128), lambda i, sel: (0, 0))],
            scratch_shapes=[pltpu.VMEM((IMG * CELLS * 2 + 2 * CELLS + 14, 128), F32)],
        ),
        out_shape=[struct(shape, BF16)] * 2 + [struct((8, 128), F32)],
        compiler_params=pltpu.CompilerParams(vmem_limit_bytes=12 << 20),
        cost_estimate=COST,
        name="pack_maps",
    )(sel, maps, *after)


def unpack_kernel(sel, w0, w1, w2, w3, maps):
    lane = lane_index()
    whole = whole_map(sel)
    group = chunk_group(WHOLE)
    for step in range(group):
        rows = exchange([w[at(step), :] for w in (w0, w1, w2, w3)], lane)
        for q in range(4):
            cell = step + group * q
            if cell < CELLS:
                maps[at(cell), :] = masked(rows[q], cell, whole)


def pack_grad_kernel(chunk, sel, grad, *wires):
    lane = lane_index()
    whole = whole_map(sel)
    first, cells = chunk_cells(chunk)
    group = chunk_group(chunk)
    for step in range(group):
        rows = []
        for q in range(4):
            cell = min(step + group * q, cells - 1)
            rows.append(masked(grad[at(cell), :], first + cell, whole))
        for wire, row in zip(wires, exchange(rows, lane)):
            wire[at(step), :] = row


def pack_grad(grad, sel, chunk, after=()):
    shape = struct(wire_shape(chunk), BF16)
    return call(partial(pack_grad_kernel, chunk), "pack_grad", [sel, grad], [shape] * 4, after)


def place_grad_kernel(chunk, ks, sel, *refs):
    wires = refs[: len(ks)]
    out, parts, sent = refs[-3:]
    lane = lane_index()
    first, cells = chunk_cells(chunk)
    group = chunk_group(chunk)
    copies = []
    for index, (k, wire) in enumerate(zip(ks, wires)):
        for step in range(group):
            tiles = tiles_of(wire[at(step), :])
            tiles.append(last_part(tiles, lane))
            for q in range(4):
                if step + group * q < cells:
                    parts[index, at(step + group * q), :] = tiles[q][:, :BLK]
        place = out.at[sel[M] ^ k, pl.ds(first * IMG, cells * IMG)]
        copies.append(pltpu.make_async_copy(parts.at[index], place, sent.at[index]))
        copies[-1].start()
    for copy in copies:
        copy.wait()


def place_grad(wires, sel, chunk, ks, total):
    args = [sel, *wires]
    in_specs = [SMEM] + [VMEM] * len(wires)
    alias = {}
    if total is not None:
        alias = {len(args): 0}
        args.append(total)
        in_specs.append(ANY)
    cells = chunk_cells(chunk)[1]
    return pl.pallas_call(
        partial(place_grad_kernel, chunk, ks),
        in_specs=in_specs,
        out_specs=ANY,
        out_shape=struct((4, CELLS * IMG, BLK), BF16),
        scratch_shapes=[
            pltpu.VMEM((len(ks), cells * IMG, BLK), BF16),
            pltpu.SemaphoreType.DMA((len(ks),)),
        ],
        input_output_aliases=alias,
        compiler_params=pltpu.CompilerParams(vmem_limit_bytes=8 << 20),
        cost_estimate=COST,
        name="place_grad",
    )(*args)


def join_kernel(*refs):
    for k, part in enumerate(refs[:-1]):
        refs[-1][k] = part[...]


def own_kernel(sel, weight_in, bias_in, stitch_in, out, weight, bias, stitch, done):
    copies = [
        pltpu.make_async_copy(weight_in.at[sel[S]], weight, done.at[0]),
        pltpu.make_async_copy(bias_in, bias, done.at[1]),
        pltpu.make_async_copy(stitch_in, stitch, done.at[2]),
    ]
    for copy in copies:
        copy.start()
    for copy in copies:
        copy.wait()
    out[:, :ROWS] = weight[...]
    values = jnp.concatenate([bias[...], stitch[0], stitch[1], jnp.zeros((2, 64), F32)], 0)
    pieces = []
    for _ in range(3):
        pieces.append(values.astype(BF16).astype(F32))
        values = values - pieces[-1]
    zeros = jnp.zeros((BLK, 64), F32)
    rows = jnp.concatenate([zeros, *pieces, jnp.zeros((8, 64), F32)], 0)
    last = slice(ROWS - BLK, ROWS + 32)
    tile = jnp.where(lane_index(64) < BLK, out[:, last].astype(F32), rows.T)
    out[:, last] = tile.astype(BF16)


def kernels_kernel(sel, *refs):
    rows_out, params = refs[6:]
    blocks = []
    for first, second, third in (refs[:3], refs[3:6]):
        blocks += [first.at[0], first.at[1], second, third]
    d, m = sel[D], sel[M]
    odd = lax.rem(m, 2) == 1
    for k in range(4):
        for x in range(2):
            own = blocks[k][x].astype(F32)
            other = blocks[4 + k][x].astype(F32)
            even_rows = jnp.where(odd, other, own)
            odd_rows = jnp.where(odd, own, other)
            turned = jnp.concatenate([even_rows, odd_rows], 0).T
            tile = pl.multiple_of((lax.div(m, 2) ^ x) * 128, 128)
            if k == 0:
                values = turned[ROWS : ROWS + 8] + turned[ROWS + 8 : ROWS + 16]
                params[:, pl.ds(tile, 128)] = values + turned[ROWS + 16 : ROWS + 24]
            turned = turned.astype(BF16)
            for part in range(9):
                index = 9 * (d ^ k) + part
                first = lax.div(index, 4) * (4 * BLK)
                block = lax.rem(index, 4) ^ m
                for piece in range(3):
                    place = first + jnp.where(
                        block == 3, 128 * piece + BLK, 128 * block + 32 * piece
                    )
                    start = part * BLK + 32 * piece
                    rows_out[pl.ds(pl.multiple_of(place, 32), 32), pl.ds(tile, 128)] = turned[
                        start : start + 32
                    ]


def gather_kernels(conv_weight, conv_bias, conv_stitch, sel, s, m, token):
    turned = conv_weight.transpose(0, 2, 1)
    rows = turned.shape[2]
    if lax.axis_size("dp") == 4:
        shape = struct((64, rows + 32), BF16)
        inputs = [turned, conv_bias, conv_stitch]
        own = call(
            own_kernel,
            "own_kernels",
            [sel] + [pltpu.with_memory_space_constraint(v, pltpu.HBM) for v in inputs],
            shape,
            scratch=[pltpu.VMEM((64, rows), BF16)]
            + [pltpu.VMEM(v.shape, F32) for v in inputs[1:]]
            + [pltpu.SemaphoreType.DMA((3,))],
            specs=[SMEM] + [HBM] * 3,
        )
        near = call(
            join_kernel,
            "join_kernels",
            [own, swap(own, "mp", 2)],
            struct((2, *own.shape), BF16),
            (token,),
        )
        column = [near] + [swap(near, "dp", k) for k in (1, 2, 3)]
        first = call(join_kernel, "join_columns", column[:2], struct((2, *near.shape), BF16))
        column = [first, *column[2:]]
        across = [swap(part, "mp", 1) for part in column]
        kernel, params = call(
            kernels_kernel,
            "kernels",
            [sel, *column, *across],
            [struct((4 * rows, OUT), BF16), struct((8, OUT), F32)],
        )
        return kernel, params, near
    own = lax.dynamic_index_in_dim(conv_weight, s, 0, keepdims=False)
    full = lax.all_gather(lax.all_gather(own, "dp", axis=0), "mp", axis=2, tiled=True)
    kernel = relative(full.reshape(9, 4, BLK, OUT), m, 1)
    last = kernel[:, 3].reshape(9, 3, 32, OUT)
    kernel = jnp.concatenate([kernel[:, :3], last], 2).reshape(36 * BLK, OUT)
    params = jnp.concatenate([conv_bias, conv_stitch.reshape(4, 64), jnp.zeros((2, 64), F32)], 0)
    params = lax.all_gather(params, "mp", axis=1, tiled=True)
    return kernel, params, jnp.zeros((8, 128), F32)


def split_kernel(sel, grad, small, keep, send):
    d, m = sel[D], sel[M]
    odd = lax.rem(m, 2) == 1
    lane = lane_index(32)

    def write(rows, place):
        count = rows.shape[0]
        t0, t1 = rows[:, 0:128], rows[:, 128:256]
        low = jnp.where(lane[:count] < 64, t0, pltpu.roll(t1, 64, 1)).astype(BF16)
        high = jnp.where(lane[:count] < 64, pltpu.roll(t0, 64, 1), t1).astype(BF16)
        here = pl.ds(pl.multiple_of(place, 16), count)
        keep[here, :] = jnp.where(odd, high, low)
        send[here, :] = jnp.where(odd, low, high)

    for tap in range(9):
        for block in range(4):
            index = tap * 4 + (block ^ m)
            part = lax.div(index, 9)
            place = (part ^ d) * (ROWS + 16) + (index - part * 9) * BLK
            for piece in range(3):
                start = tap * 4 * BLK + (128 * piece + BLK if block == 3 else 128 * block + 32 * piece)
                write(grad[start : start + 32, :], place + 32 * piece)
    sums = jnp.concatenate([small[...], jnp.zeros((16 - small.shape[0], OUT), F32)], 0)
    for part in range(4):
        write(sums, part * (ROWS + 16) + ROWS)


def pair_kernel(keep, arrived, own, *sends):
    size = ROWS + 16
    for k in range(4):
        here = slice(k * size, (k + 1) * size)
        total = keep[here, :].astype(F32) + arrived[here, :].astype(F32)
        if k == 0:
            own[...] = total
        else:
            sends[k - 1][...] = total.astype(BF16)


def turn_kernel(sel, own, a, b, c, mine, send):
    total = own[...] + a[...].astype(F32) + b[...].astype(F32) + c[...].astype(F32)
    total = jnp.concatenate([total, jnp.zeros((16, 128), F32)], 0).T
    low = sel[M] < 2
    mine[...] = jnp.where(low, total[:64], total[64:])
    send[...] = jnp.where(low, total[64:], total[:64]).astype(BF16)


def finish_kernel(sel, mine, arrived, rows, bias, stitch):
    rows[...] = mine[:, :ROWS] + arrived[:, :ROWS].astype(F32)
    last = slice(ROWS - BLK, ROWS + 32)
    small = (mine[:, last] + arrived[:, last].astype(F32)).T
    stitch[pl.ds(sel[S], 1), :] = small[BLK : BLK + 1]
    stitch[pl.ds(1 - sel[S], 1), :] = small[BLK + 1 : BLK + 2]
    bias[...] = small[BLK + 2 : BLK + 3]


def scatter_kernels(grad, small, sel, s, m, meanwhile, finish_fc):
    rows = grad.shape[0] // lax.axis_size("dp")
    small_shapes = [struct((1, 64), F32), struct((2, 64), F32)]
    if lax.axis_size("dp") == 4:
        size = ROWS + 16
        keep, send = call(
            split_kernel, "split_kernels", [sel, grad, small], [struct((4 * size, 128), BF16)] * 2
        )
        own, *sends = call(
            pair_kernel,
            "pair_kernels",
            [keep, swap(send, "mp", 1)],
            [struct((size, 128), F32)] + [struct((size, 128), BF16)] * 3,
            meanwhile(),
        )
        last = call(
            copy_kernel, "last_kernels", sends[2:], struct((size, 128), BF16), finish_fc(own)
        )
        arrived = [swap(part, "dp", k) for k, part in zip((1, 2, 3), (*sends[:2], last))]
        mine, other = call(
            turn_kernel,
            "turn_kernels",
            [sel, own, *arrived],
            [struct((64, ROWS + 32), F32), struct((64, ROWS + 32), BF16)],
        )
        result, bias, stitch = call(
            finish_kernel,
            "finish_kernels",
            [sel, mine, swap(other, "mp", 2)],
            [struct((64, ROWS), F32), *small_shapes],
        )
        return result.T, bias, stitch, own
    grad = grad.reshape(9, 3, 128, OUT)
    last = grad[:, :, BLK:].reshape(9, 1, BLK, OUT)
    grad = jnp.concatenate([grad[:, :, :BLK], last], 1)
    grad = relative(grad, m, 1).reshape(36 * BLK, OUT).astype(BF16)
    grad = lax.psum_scatter(grad, "mp", scatter_dimension=1, tiled=True)
    grad = lax.psum_scatter(grad, "dp", scatter_dimension=0, tiled=True).astype(F32)
    small = sum_over(sum_over(small, "dp"), "mp")
    small = lax.dynamic_slice_in_dim(small, m * 64, 64, 1)
    stitch = jnp.stack([jnp.where(s == 0, small[0], small[1]), jnp.where(s == 0, small[1], small[0])])
    meanwhile()
    finish_fc(small)
    return grad, small[2:3], stitch, small


def gelu_parts(value):
    scale = 0.7978845608028654
    square = value * value
    curve = jnp.tanh(scale * value * (1.0 + 0.044715 * square))
    return curve, square, scale


def gelu(value):
    curve, _, _ = gelu_parts(value)
    return 0.5 * value * (1.0 + curve)


def gelu_slope(value):
    curve, square, scale = gelu_parts(value)
    bend = (0.5 * scale) * value * (1.0 - curve * curve) * (1.0 + 0.134145 * square)
    return 0.5 * (1.0 + curve) + bend


def place_of(sel, k, p):
    return 9 * (lax.rem(sel[D], 4) ^ k) + p


def half_kernel(first, sel, pooled, out):
    for k in range(2):
        for p in range(9):
            out[k, p] = pooled[place_of(sel, first + k, p)].astype(BF16)


def pool_kernel(sel, conv_out, params, pooled, far):
    extent = jnp.where(is_low(sel), POOL_LOW, POOLED)
    shift = params[pl.ds(sel[S], 1), :]
    lines = []
    for i in range(SIDE):
        cells = [gelu(conv_out[i, j] + shift) for j in range(SIDE)]
        lines.append([cells[2 * q] + cells[2 * q + 1] + cells[2 * q + 2] for q in range(POOLED)])
        if i >= 2 and i % 2 == 0:
            p = i // 2 - 1
            for q in range(POOLED):
                total = lines[i - 2][q] + lines[i - 1][q] + lines[i][q]
                keep = jnp.logical_and(p < extent, q < extent).astype(F32) / 9.0
                total = total * keep
                pooled[POOLED * p + q] = total
    half_kernel(2, sel, pooled, far)


def slope_kernel(sel, conv_out, params, slope):
    shift = params[pl.ds(sel[S], 1), :]
    for i in range(SIDE):
        for j in range(SIDE):
            slope[SIDE * i + j] = gelu_slope(conv_out[i, j] + shift)


def entry(params, t, u):
    return params[pl.ds(2 + 2 * t + u, 1), :]


def stitch_kernel(first, sel, pooled, other, params, *chunks):
    s = sel[S]
    by_own, by_other = entry(params, s, s), entry(params, s, 1 - s)
    for k, chunk in enumerate(chunks):
        for p in range(9):
            mixed = by_own * pooled[place_of(sel, first + k, p)] + by_other * other[k, p].astype(F32)
            chunk[p] = mixed.astype(BF16)


def conv_grad_kernel(
    sel, near, far, near_other, far_other, slope, pooled, near_pooled, far_pooled, params, out, sums, mixed
):
    extent, s = jnp.where(is_low(sel), POOL_LOW, POOLED), sel[S]
    by_own, by_other = entry(params, s, s), entry(params, 1 - s, s)
    own_sum = other_sum = jnp.zeros((IMG, OUT), F32)
    for k in range(4):
        grad = near.at[k] if k < 3 else far
        grad_other = near_other.at[k] if k < 3 else far_other
        pooled_other = (near_pooled, far_pooled)[k // 2]
        for p in range(9):
            place = place_of(sel, k, p)
            mine = grad[p].astype(F32)
            mixed[place] = by_own * mine + by_other * grad_other[p].astype(F32)
            own_sum = own_sum + mine * pooled[place]
            other_sum = other_sum + mine * pooled_other[k % 2, p].astype(F32)
    spread = []
    for p in range(POOLED):
        line = []
        for q in range(POOLED):
            keep = jnp.logical_and(p < extent, q < extent).astype(F32) / 9.0
            line.append(mixed[POOLED * p + q] * keep)
        spread.append(line)
    bias_sum = jnp.zeros((IMG, OUT), F32)

    def over(values, index):
        near, far = index // 2, index // 2 - 1
        if index % 2 == 1 or index == 0:
            return values[near]
        if near >= POOLED:
            return values[far]
        return values[near] + values[far]

    for i in range(SIDE):
        line = [over([spread[p][q] for p in range(POOLED)], i) for q in range(POOLED)]
        for j in range(SIDE):
            cell = SIDE * i + j
            value = (slope[cell] * over(line, j)).astype(BF16)
            out[cell] = value
            bias_sum = bias_sum + value.astype(F32)
    for row, total in enumerate((own_sum, other_sum, bias_sum)):
        sums[row : row + 1, :] = jnp.sum(total, 0, keepdims=True)


def all_acts(acts, place):
    return jnp.concatenate([a[:, place].reshape(4 * IMG, OUT) for a in acts], 0)


def all_grads(grads):
    return jnp.concatenate([g[r] for r in range(4) for g in grads], 0)


def load_kernel(sel, weight, out, token, done):
    token[...] = jnp.zeros(token.shape, F32)
    count = done.shape[0]
    size = weight.shape[1] // count
    copies = []
    for part in range(count):
        here = pl.ds(part * size, size)
        copies.append(pltpu.make_async_copy(weight.at[sel[S], here], out.at[here], done.at[part]))
        copies[-1].start()
    for copy in copies:
        copy.wait()


def load_matrix(weight, sel, s, after):
    if lax.axis_size("dp") != 4:
        return lax.dynamic_index_in_dim(weight, s, 0, keepdims=False), ()
    matrix, token = call(
        load_kernel,
        "load_matrix",
        [sel, pltpu.with_memory_space_constraint(weight, pltpu.HBM)],
        [struct(weight.shape[1:], BF16), struct((8, 128), F32)],
        after,
        scratch=[pltpu.SemaphoreType.DMA((9,))],
        specs=[SMEM, HBM],
    )
    return matrix, (token,)


def fc_forward_kernel(a0, a1, a2, a3, weight, own, *sends):
    rows = jnp.concatenate([all_acts((a0, a1, a2, a3), p) for p in range(9)], 1)
    for n in range(weight.shape[1] // 256):
        here = slice(n * 256, (n + 1) * 256)
        term = jnp.dot(rows, weight[:, here], preferred_element_type=F32)
        for r in range(4):
            for k in range(4):
                part = term[(4 * r + k) * IMG : (4 * r + k + 1) * IMG]
                if k == 0:
                    own[r, :, here] = part
                else:
                    sends[k - 1][r, :, here] = part.astype(BF16)


def fc_active_kernel(sel, own, a, b, c, bias, stitch, cot, grad, active, sent, sums):
    s, m = sel[S], sel[M]
    for n in range(own.shape[2] // 256):
        here = slice(n * 256, (n + 1) * 256)
        shift = bias[pl.ds(s, 1), here]
        w0, w1 = stitch[0, pl.ds(s, 1), here], stitch[1, pl.ds(s, 1), here]
        sum0 = sum1 = jnp.zeros((IMG, 256), F32)
        for r in range(4):
            value = own[r, :, here] + a[r, :, here].astype(F32)
            value = value + (b[r, :, here].astype(F32) + c[r, :, here].astype(F32)) + shift
            curve, square, scale = gelu_parts(value)
            half = 0.5 * (1.0 + curve)
            bend = (0.5 * scale) * value * (1.0 - curve * curve) * (1.0 + 0.134145 * square)
            result = value * half
            c0, c1 = cot[0, m ^ r, :, here].astype(F32), cot[1, m ^ r, :, here].astype(F32)
            grad[r, :, here] = ((half + bend) * (w0 * c0 + w1 * c1)).astype(BF16)
            active[r, :, here] = result
            sent[r, :, here] = result.astype(BF16)
            sum0 = sum0 + c0 * result
            sum1 = sum1 + c1 * result
        for t, total in enumerate((sum0, sum1)):
            sums[4 * t + n : 4 * t + n + 1, :] = jnp.sum(total, 0, keepdims=True)


def fc_rows_kernel(*refs):
    grads, (weight, keep, send) = refs[:-3], refs[-3:]
    rows = all_grads(grads)
    for p in range(9):
        term = lax.dot_general(
            rows,
            weight[p * 256 : (p + 1) * 256, :],
            (((1,), (1,)), ((), ())),
            preferred_element_type=F32,
        )
        term = term.reshape(4, len(grads), IMG, 256)
        for r in range(4):
            if r % 2 == 0:
                keep[r // 2, :, p] = term[r]
            else:
                send[r // 2, :, p] = term[r].astype(BF16)


def cross_kernel(keep, arrived, out):
    out[...] = (keep[1] + arrived[1].astype(F32)).astype(BF16)


def home_kernel(keep, arrived, crossed, sums, *chunks):
    high = sums[...].astype(BF16).astype(F32)
    small = jnp.concatenate([high, sums[...] - high], 0).astype(BF16)
    for k in range(len(chunks)):
        total = keep[0, k] + arrived[0, k].astype(F32) + crossed[k].astype(F32)
        chunks[k][0:9] = total.astype(BF16)
        chunks[k][9] = small


def fc_matrix_kernel(a0, a1, a2, a3, g0, g1, g2, g3, out, bias, token, part, sent):
    token[...] = jnp.zeros(token.shape, F32)
    grads = all_grads((g0, g1, g2, g3))

    def copy(p):
        return pltpu.make_async_copy(part.at[p % 3], out.at[pl.ds(p * 256, 256)], sent.at[p % 3])

    for p in range(9):
        rows = all_acts((a0, a1, a2, a3), p).T
        if p >= 3:
            copy(p - 3).wait()
        part[p % 3] = jnp.dot(rows, grads, preferred_element_type=F32)
        copy(p).start()
    bias[...] = jnp.sum(grads.astype(F32), 0, keepdims=True)
    for p in range(6, 9):
        copy(p).wait()


def copy_kernel(value, out):
    out[...] = value[...]


def outputs_kernel(sel, active, arrived, stitch, out):
    s, m = sel[S], sel[M]
    for n in range(active.shape[2] // 256):
        here = slice(n * 256, (n + 1) * 256)
        by_own = jnp.where(s == 0, stitch[0, 0:1, here], stitch[1, 1:2, here])
        by_other = jnp.where(s == 0, stitch[0, 1:2, here], stitch[1, 0:1, here])
        for r in range(4):
            mixed = by_own * active[r, :, here] + by_other * arrived[r, :, here].astype(F32)
            out[m ^ r, :, here] = mixed.astype(BF16)


def plane_sum(near, far):
    total = jnp.zeros((8, OUT), F32)
    for plane in (near[0, 9], near[1, 9], near[2, 9], far[9]):
        plane = plane.astype(F32)
        total = total + (plane[0:8] + plane[8:16])
    return total


def stitch_sums_kernel(sel, near, far, near_other, far_other, out, own, other):
    s = sel[S]
    own[...] = plane_sum(near, far)
    other[...] = plane_sum(near_other, far_other)
    for n in range(4):
        here = slice(n * OUT, (n + 1) * OUT)
        out[pl.ds(s, 1), here] = own[pl.ds(4 * s + n, 1), :]
        out[pl.ds(1 - s, 1), here] = other[pl.ds(4 * s + n, 1), :]


def fc_section(pooled, near, far, params, weight, bias, stitch, cot, sel, s, d, m):
    count = lax.axis_size("dp")
    hid = weight.shape[2]
    plane = struct((9, IMG, OUT), BF16)
    block = struct((4, IMG, hid), BF16)
    token = struct((8, 128), F32)
    chunks = [None] * 4
    chunks[2:] = call(
        partial(stitch_kernel, 2), "stitch_far", [sel, pooled, far, params], [plane] * 2
    )
    chunks[:2] = call(
        partial(stitch_kernel, 0), "stitch_near", [sel, pooled, near, params], [plane] * 2, chunks[2:3]
    )
    own_weight, after = load_matrix(weight, sel, s, chunks[:1])
    if count == 4:
        moved = [chunks[0]] + [swap(chunks[k], "dp", k) for k in (1, 2, 3)]
        own_acts = call(join_kernel, "join_acts", moved, struct((4, 9, IMG, OUT), BF16), after)
        far_acts = swap(own_acts, "mp", 2)
        acts = [own_acts, swap(own_acts, "mp", 1), far_acts, swap(far_acts, "mp", 1)]
        pre, *sends = call(
            fc_forward_kernel,
            "fc_forward",
            [*acts, own_weight],
            [struct((4, IMG, hid), F32)] + [block] * 3,
        )
        arrived = [swap(part, "dp", k) for k, part in zip((1, 2, 3), sends)]
    else:
        shared = by_position(chunks, d)
        flat = shared.transpose(1, 0, 2).reshape(IMG, count, -1).transpose(1, 0, 2)
        flat = lax.all_to_all(flat, "dp", 0, 0, tiled=True)
        flat = lax.all_gather(flat, "mp", axis=0)
        flat = relative(flat, m)
        pre = jnp.einsum("rdnf,fk->drnk", flat, own_weight, preferred_element_type=F32)
        pre = lax.psum_scatter(pre.astype(BF16), "dp", scatter_dimension=0, tiled=True)
        pre = pre.reshape(4, IMG, hid).astype(F32)
        arrived = [jnp.zeros(block.shape, BF16)] * 3
    pre_grad, active, sent, sums = call(
        fc_active_kernel,
        "fc_active",
        [sel, pre, *arrived, bias, stitch, cot],
        [block, struct(block.shape, F32), block, struct((8, OUT), F32)],
    )
    if count == 4:
        grads = gather4(pre_grad)
        ten = struct((10, IMG, OUT), BF16)

        marks = []

        def home(ks, name, after=()):
            shape = (2, len(ks), 9, IMG, OUT)
            keep, send = call(
                fc_rows_kernel,
                "fc_rows_" + name,
                [*[grads[k] for k in ks], own_weight],
                [struct(shape, F32), struct(shape, BF16)],
                after,
            )
            arrived = swap(send, "mp", 1)
            crossing = call(cross_kernel, "cross_" + name, [keep, arrived], struct(shape[1:], BF16))
            crossed = swap(crossing, "mp", 2)
            inputs = [keep, arrived, crossed, sums]
            marks.append(crossing)
            return call(home_kernel, "home_" + name, inputs, [ten] * len(ks))

        chunks = home((0, 1, 2), "near")
        moved = [chunks[0], swap(chunks[1], "dp", 1), swap(chunks[2], "dp", 2)]
        (chunk,) = home((3,), "far", marks[:1])
        def matrix_gradient(after, grads=tuple(grads)):
            return call(
                fc_matrix_kernel,
                "fc_matrix",
                [*acts, *grads],
                [struct(own_weight.shape, F32), struct((1, hid), F32), token],
                after,
                scratch=[pltpu.VMEM((3, 256, hid), F32), pltpu.SemaphoreType.DMA((3,))],
                limit=10 << 20,
                out_specs=[HBM, VMEM, VMEM],
            )

        near_grad = call(join_kernel, "join_near", moved, struct((3, *ten.shape), BF16), (chunk,))
        near_back = (near_grad, swap(near_grad, "section", 1))
        far_grad = swap(chunk, "dp", 3)
        far_back = (far_grad, swap(far_grad, "section", 1))
    else:
        grads = lax.all_gather(pre_grad, "dp", axis=0)
        rows = jnp.einsum("drnk,fk->rdnf", grads, own_weight, preferred_element_type=F32)
        rows = relative(rows, m).astype(BF16)
        rows = lax.psum_scatter(rows, "mp", scatter_dimension=0, tiled=True)[0]
        rows = lax.all_to_all(rows, "dp", 0, 0, tiled=True)
        back = rows.transpose(1, 0, 2).reshape(IMG, 4, 9, OUT).transpose(1, 2, 0, 3)
        matrix_grad = jnp.einsum("rdnf,drnk->fk", flat, grads, preferred_element_type=F32)
        bias_sum = jnp.sum(grads.astype(F32), (0, 1, 2))[None]

        def matrix_gradient(after):
            return matrix_grad, bias_sum, sums

        total = sum_over(sums, "dp")
        high = lax.reduce_precision(total, 8, 7)
        small = jnp.concatenate([high, total - high], 0).astype(BF16)
        small = jnp.stack([small] + [jnp.zeros_like(small)] * 3)
        back = jnp.concatenate([relative(back, lax.rem(d, 4)), small[:, None]], 1)
        near_back, far_back = [(part, swap(part, "section", 1)) for part in (back[:3], back[3])]
    stitch_sum = call(
        stitch_sums_kernel,
        "stitch_sums",
        [sel, near_back[0], far_back[0], near_back[1], far_back[1]],
        struct((2, hid), F32),
        scratch=[pltpu.VMEM((8, OUT), F32)] * 2,
    )
    grads = [near_back[0], far_back[0], near_back[1], far_back[1]]
    return grads, (active, sent), matrix_gradient, stitch_sum


def by_position(chunks, d):
    return relative(jnp.stack(chunks), lax.rem(d, 4)).reshape(PLACES, IMG, OUT)


def conv(maps, taps, rows, form, kind=F32):
    return lax.conv_general_dilated(
        maps,
        taps,
        (1, 1),
        (rows, (1, 1)),
        dimension_numbers=form,
        preferred_element_type=F32,
    ).astype(kind)


def on_device(
    conv_input,
    group_ids,
    conv_weight,
    conv_bias,
    conv_stitch,
    fc_weight,
    fc_bias,
    fc_stitch,
    cotangent,
):
    s = lax.axis_index("section")
    d = lax.axis_index("dp")
    m = lax.axis_index("mp")
    assert conv_input.shape == (4, IMG, 2, SIDE, SIDE, BLK) and lax.axis_size("mp") == 4
    sel = jnp.concatenate([scalars(s, d, m), group_ids])

    by_row = conv_input.transpose(0, 1, 3, 4, 2, 5).reshape(4, IMG * CELLS * 2, BLK)
    by_row = pltpu.with_memory_space_constraint(by_row, pltpu.HBM)
    far3, far2, token = pack_maps(by_row, sel, 3)
    kernel, params, early = gather_kernels(conv_weight, conv_bias, conv_stitch, sel, s, m, token)
    cot = lax.dynamic_slice_in_dim(cotangent, d * IMG, IMG, 1).transpose(2, 0, 1, 3)
    near1, near0, token = pack_maps(by_row, sel, 1, (token, early, cot))
    wires = [near0, swap(near1, "mp", 1), swap(far2, "mp", 2), swap(far3, "mp", 3)]

    taps = kernel.reshape(3, 3, 4 * BLK, OUT)
    maps = call(
        unpack_kernel,
        "unpack_maps",
        [sel, *wires],
        struct((CELLS * IMG, 4 * BLK), BF16),
    )
    maps = maps.reshape(SIDE, SIDE, IMG, 4 * BLK)
    conv_out = conv(maps, taps, (1, 1), ("HWNC", "HWIO", "HWNC"))
    half = struct((2, 9, IMG, OUT), BF16)
    pooled, far = call(
        pool_kernel, "pool", [sel, conv_out, params], [struct((PLACES, IMG, OUT), F32), half]
    )
    near = call(partial(half_kernel, 0), "pool_near", [sel, pooled], half)
    far = swap(far, "section", 1)
    near = swap(near, "section", 1)

    back, outputs, matrix_gradient, fc_stitch_sum = fc_section(
        pooled, near, far, params, fc_weight, fc_bias, fc_stitch, cot, sel, s, d, m
    )
    slope = call(
        slope_kernel,
        "slope",
        [sel, conv_out, params],
        struct((CELLS, IMG, OUT), F32),
        (back[0],),
    )
    conv_grad, sums = call(
        conv_grad_kernel,
        "conv_gradient",
        [sel, *back, slope, pooled, near, far, params],
        [struct((CELLS, IMG, OUT), BF16), struct((3, OUT), F32)],
        scratch=[pltpu.VMEM((PLACES, IMG, OUT), F32)],
    )
    conv_grad = conv_grad.reshape(SIDE, SIDE, IMG, OUT)

    back_taps = taps[::-1, ::-1]
    wires = []

    def send_input_grad(after=()):
        chunk = len(wires)
        low, high = HALVES[chunk]
        padding = (1 - low, 1 - SIDE + high)
        part = conv(conv_grad, back_taps, padding, ("HWNC", "HWOI", "HWNC"), BF16)
        sends = pack_grad(part.reshape(-1, 4 * BLK), sel, HALVES[chunk], after)
        wires.append([sends[0]] + [swap(sends[k], "mp", k) for k in (1, 2, 3)])
        return (sends[0],)

    maps = pass_on(maps, send_input_grad())
    kernel_grad = conv(maps, conv_grad, (1, 1), ("HWCN", "HWIO", "HWNC"))
    results = []

    def finish_fc(begun):
        results.extend(matrix_gradient((begun,)))
        return results[-1:]

    kernel_rows, conv_bias_sum, conv_stitch_sum, begun = scatter_kernels(
        kernel_grad.reshape(36 * BLK, OUT), sums, sel, s, m, lambda: (), finish_fc
    )
    matrix_grad, fc_bias_sum, _ = results
    mark = send_input_grad((*wires[0][2:], begun))
    active, sent = outputs
    sent = call(copy_kernel, "outputs_send", [sent], struct(sent.shape, BF16), mark)
    outputs = call(
        outputs_kernel,
        "outputs",
        [sel, active, swap(sent, "section", 1), fc_stitch],
        struct(sent.shape, BF16),
    )
    input_grad = place_grad(wires[0], sel, HALVES[0], (0, 1, 2, 3), None)
    input_grad = place_grad(wires[1][:2], sel, HALVES[1], (0, 1), input_grad)
    input_grad = place_grad(wires[1][2:], sel, HALVES[1], (2, 3), input_grad)
    input_grad = input_grad.reshape(4, 1, SIDE, SIDE, IMG, BLK).transpose(0, 4, 1, 2, 3, 5)
    return (
        outputs[:, :, None],
        input_grad,
        kernel_rows[None],
        conv_bias_sum,
        conv_stitch_sum[None],
        matrix_grad[None],
        fc_bias_sum,
        fc_stitch_sum[None],
    )


def solution(mesh):
    placed = (
        P(None, "dp", None, None, None, "mp"),
        P(),
        P(None, "dp", "mp"),
        P(None, "mp"),
        P(None, None, "mp"),
        P(None, "dp", "mp"),
        P(None, "mp"),
        P(None, None, "mp"),
        P(None, None, None, "mp"),
    )
    return jax.shard_map(
        on_device,
        mesh=mesh,
        in_specs=placed,
        out_specs=(
            P(None, "dp", "section", "mp"),
            P(None, "dp", "section", None, None, "mp"),
            P("section", "dp", "mp"),
            P("section", "mp"),
            P("section", None, "mp"),
            P("section", "dp", "mp"),
            P("section", "mp"),
            P("section", None, "mp"),
        ),
        check_vma=False,
    )
```

```python
from functools import partial

import jax
import jax.numpy as jnp
from jax import lax
from jax.experimental import pallas as pl
from jax.experimental.pallas import tpu as pltpu
from jax.sharding import PartitionSpec as P


MAP_LOW = 11
POOL_LOW = 5
SIDE = 13
POOLED = 6
CELLS = SIDE * SIDE
PLACES = POOLED * POOLED
IMG = 16
BLK = 96
OUT = 256
ROWS = 9 * BLK
WHOLE = (0, 13)
HALVES = ((0, 7), (7, 13))
SCOPE = 4 << 20
F32 = jnp.float32
BF16 = jnp.bfloat16
VMEM = pl.BlockSpec(memory_space=pltpu.VMEM)
SMEM = pl.BlockSpec(memory_space=pltpu.SMEM)
ANY = pl.BlockSpec(memory_space=pl.ANY)
HBM = pl.BlockSpec(memory_space=pltpu.HBM)


def swap(value, axis, bit):
    count = lax.axis_size(axis)
    return lax.ppermute(value, axis, [(i, i ^ bit) for i in range(count)])


def gather4(value):
    near = swap(value, "dp", 1)
    far = swap(value, "dp", 2)
    return [value, near, far, swap(far, "dp", 1)]


def sum_over(value, axis):
    bit = 1
    while bit < lax.axis_size(axis):
        value = value + swap(value, axis, bit)
        bit *= 2
    return value


def relative(value, index, axis=0):
    return jnp.concatenate(
        [lax.dynamic_slice_in_dim(value, index ^ k, 1, axis) for k in range(4)], axis
    )


def scalars(*values):
    return jnp.stack(values).astype(jnp.int32)


S, D, M, GROUPS = range(4)
COST = pl.CostEstimate(flops=1, bytes_accessed=1, transcendentals=0)


def is_low(sel):
    return sel[GROUPS + sel[M]] == 1


def struct(shape, dtype):
    return jax.ShapeDtypeStruct(shape, dtype)


def call(body, name, inputs, outs, after=(), scratch=(), limit=SCOPE, specs=None, out_specs=None):
    if specs is None:
        specs = [SMEM if v.dtype == jnp.int32 else VMEM for v in inputs]
    count = len(inputs)

    def kernel(*refs):
        body(*refs[:count], *refs[count + len(after) :])

    single = not isinstance(outs, (list, tuple))
    if out_specs is None:
        out_specs = VMEM if single else [VMEM] * len(outs)
    return pl.pallas_call(
        kernel,
        in_specs=specs + [VMEM] * len(after),
        out_specs=out_specs,
        out_shape=outs if single else list(outs),
        scratch_shapes=list(scratch),
        compiler_params=pltpu.CompilerParams(vmem_limit_bytes=limit),
        cost_estimate=COST,
        name=name,
    )(*inputs, *after)


def pass_on(value, after):
    def kernel(*refs):
        pass

    return pl.pallas_call(
        kernel,
        in_specs=[ANY] + [VMEM] * len(after),
        out_specs=ANY,
        out_shape=struct(value.shape, value.dtype),
        input_output_aliases={0: 0},
        compiler_params=pltpu.CompilerParams(vmem_limit_bytes=SCOPE),
        cost_estimate=COST,
        name="pass_on",
    )(value, *after)


def lane_index(rows=IMG):
    return lax.broadcasted_iota(jnp.int32, (rows, 128), 1)


def join4(parts, lane):
    last = parts[3]
    return [jnp.where(lane < BLK, parts[j], pltpu.roll(last, 96 - 32 * j, 1)) for j in range(3)]


def last_part(tiles, lane):
    a, b, c = [pltpu.roll(tiles[j], 32 + 32 * j, 1) for j in range(3)]
    return jnp.where(lane < 32, a, jnp.where(lane < 64, b, c))


def tiles_of(row):
    return [row[:, 0:128], row[:, 128:256], row[:, 256:384]]


def exchange(rows, lane):
    rows = [tiles_of(row) for row in rows]
    out = []
    for k in range(3):
        last = rows[3][k]
        out.append(
            [
                jnp.where(lane < BLK, rows[j][k], pltpu.roll(last, 96 - 32 * j, 1))
                for j in range(3)
            ]
        )
    thirds = [last_part(rows[q], lane) for q in range(3)]
    out.append([jnp.where(lane < BLK, thirds[j], rows[3][j]) for j in range(3)])
    return [jnp.concatenate(tiles, 1) for tiles in out]


def chunk_cells(chunk):
    return SIDE * chunk[0], SIDE * (chunk[1] - chunk[0])


def chunk_group(chunk):
    return -(-chunk_cells(chunk)[1] // 4)


def wire_shape(chunk):
    return (chunk_group(chunk) * IMG, 4 * BLK)


def masked(row, cell, whole):
    if cell // SIDE >= MAP_LOW or cell % SIDE >= MAP_LOW:
        return row * whole
    return row


def whole_map(sel):
    return jnp.where(is_low(sel), 0.0, 1.0).astype(BF16)


def at(cell):
    return pl.ds(cell * IMG, IMG)


def pack_kernel(count, sel, maps, *refs):
    wires, token, rows = refs[count:-2], refs[-2], refs[-1]
    token[...] = jnp.zeros(token.shape, F32)
    tower = sel[S]

    def widen(step, _):
        rows[pl.ds(step * 208, 208), :BLK] = maps[0, pl.ds(step * 208, 208), :].astype(F32)
        return 0

    lax.fori_loop(0, 26, widen, 0, unroll=2)
    lane = lane_index()

    def cell(index):
        start = 2 * index + tower
        return jnp.concatenate(
            [
                rows[pl.ds(start, 8, stride=2 * CELLS), :],
                rows[pl.ds(start + 16 * CELLS, 8, stride=2 * CELLS), :],
            ],
            0,
        ).astype(BF16)

    def fill(wire):
        group = chunk_group(WHOLE)
        for step in range(group):
            parts = [cell(min(step + group * q, CELLS - 1)) for q in range(4)]
            wire[at(step), :] = jnp.concatenate(join4(parts, lane), 1)

    pl.when(pl.program_id(0) == 0)(partial(fill, wires[0]))
    pl.when(pl.program_id(0) == 1)(partial(fill, wires[1]))


def pack_maps(maps, sel, first, after=()):
    shape = wire_shape(WHOLE)
    return pl.pallas_call(
        partial(pack_kernel, len(after)),
        grid_spec=pltpu.PrefetchScalarGridSpec(
            num_scalar_prefetch=1,
            grid=(2,),
            in_specs=[pl.BlockSpec((1, IMG * CELLS * 2, BLK), lambda i, sel: (sel[M] ^ (first - i), 0, 0))]
            + [VMEM] * len(after),
            out_specs=[pl.BlockSpec(shape, lambda i, sel: (0, 0))] * 2
            + [pl.BlockSpec((8, 128), lambda i, sel: (0, 0))],
            scratch_shapes=[pltpu.VMEM((IMG * CELLS * 2 + 2 * CELLS + 14, 128), F32)],
        ),
        out_shape=[struct(shape, BF16)] * 2 + [struct((8, 128), F32)],
        compiler_params=pltpu.CompilerParams(vmem_limit_bytes=12 << 20),
        cost_estimate=COST,
        name="pack_maps",
    )(sel, maps, *after)


def unpack_kernel(sel, w0, w1, w2, w3, maps):
    lane = lane_index()
    whole = whole_map(sel)
    group = chunk_group(WHOLE)
    for step in range(group):
        rows = exchange([w[at(step), :] for w in (w0, w1, w2, w3)], lane)
        for q in range(4):
            cell = step + group * q
            if cell < CELLS:
                maps[at(cell), :] = masked(rows[q], cell, whole)


def pack_grad_kernel(chunk, sel, grad, *wires):
    lane = lane_index()
    whole = whole_map(sel)
    first, cells = chunk_cells(chunk)
    group = chunk_group(chunk)
    for step in range(group):
        rows = []
        for q in range(4):
            cell = min(step + group * q, cells - 1)
            rows.append(masked(grad[at(cell), :], first + cell, whole))
        for wire, row in zip(wires, exchange(rows, lane)):
            wire[at(step), :] = row


def pack_grad(grad, sel, chunk, after=()):
    shape = struct(wire_shape(chunk), BF16)
    return call(partial(pack_grad_kernel, chunk), "pack_grad", [sel, grad], [shape] * 4, after)


def place_grad_kernel(chunk, ks, sel, *refs):
    wires = refs[: len(ks)]
    out, parts, sent = refs[-3:]
    lane = lane_index()
    first, cells = chunk_cells(chunk)
    group = chunk_group(chunk)
    copies = []
    for index, (k, wire) in enumerate(zip(ks, wires)):
        for step in range(group):
            tiles = tiles_of(wire[at(step), :])
            tiles.append(last_part(tiles, lane))
            for q in range(4):
                if step + group * q < cells:
                    parts[index, at(step + group * q), :] = tiles[q][:, :BLK]
        place = out.at[sel[M] ^ k, pl.ds(first * IMG, cells * IMG)]
        copies.append(pltpu.make_async_copy(parts.at[index], place, sent.at[index]))
        copies[-1].start()
    for copy in copies:
        copy.wait()


def place_grad(wires, sel, chunk, ks, total):
    args = [sel, *wires]
    in_specs = [SMEM] + [VMEM] * len(wires)
    alias = {}
    if total is not None:
        alias = {len(args): 0}
        args.append(total)
        in_specs.append(ANY)
    cells = chunk_cells(chunk)[1]
    return pl.pallas_call(
        partial(place_grad_kernel, chunk, ks),
        in_specs=in_specs,
        out_specs=ANY,
        out_shape=struct((4, CELLS * IMG, BLK), BF16),
        scratch_shapes=[
            pltpu.VMEM((len(ks), cells * IMG, BLK), BF16),
            pltpu.SemaphoreType.DMA((len(ks),)),
        ],
        input_output_aliases=alias,
        compiler_params=pltpu.CompilerParams(vmem_limit_bytes=8 << 20),
        cost_estimate=COST,
        name="place_grad",
    )(*args)


def join_kernel(*refs):
    for k, part in enumerate(refs[:-1]):
        refs[-1][k] = part[...]


def own_kernel(sel, weight_in, bias_in, stitch_in, out, weight, bias, stitch, done):
    copies = [
        pltpu.make_async_copy(weight_in.at[sel[S]], weight, done.at[0]),
        pltpu.make_async_copy(bias_in, bias, done.at[1]),
        pltpu.make_async_copy(stitch_in, stitch, done.at[2]),
    ]
    for copy in copies:
        copy.start()
    for copy in copies:
        copy.wait()
    out[:, :ROWS] = weight[...]
    values = jnp.concatenate([bias[...], stitch[0], stitch[1], jnp.zeros((2, 64), F32)], 0)
    pieces = []
    for _ in range(3):
        pieces.append(values.astype(BF16).astype(F32))
        values = values - pieces[-1]
    zeros = jnp.zeros((BLK, 64), F32)
    rows = jnp.concatenate([zeros, *pieces, jnp.zeros((8, 64), F32)], 0)
    last = slice(ROWS - BLK, ROWS + 32)
    tile = jnp.where(lane_index(64) < BLK, out[:, last].astype(F32), rows.T)
    out[:, last] = tile.astype(BF16)


def kernels_kernel(sel, *refs):
    rows_out, params = refs[6:]
    blocks = []
    for first, second, third in (refs[:3], refs[3:6]):
        blocks += [first.at[0], first.at[1], second, third]
    d, m = sel[D], sel[M]
    odd = lax.rem(m, 2) == 1
    for k in range(4):
        for x in range(2):
            own = blocks[k][x].astype(F32)
            other = blocks[4 + k][x].astype(F32)
            even_rows = jnp.where(odd, other, own)
            odd_rows = jnp.where(odd, own, other)
            turned = jnp.concatenate([even_rows, odd_rows], 0).T
            tile = pl.multiple_of((lax.div(m, 2) ^ x) * 128, 128)
            if k == 0:
                values = turned[ROWS : ROWS + 8] + turned[ROWS + 8 : ROWS + 16]
                params[:, pl.ds(tile, 128)] = values + turned[ROWS + 16 : ROWS + 24]
            turned = turned.astype(BF16)
            for part in range(9):
                index = 9 * (d ^ k) + part
                first = lax.div(index, 4) * (4 * BLK)
                block = lax.rem(index, 4) ^ m
                for piece in range(3):
                    place = first + jnp.where(
                        block == 3, 128 * piece + BLK, 128 * block + 32 * piece
                    )
                    start = part * BLK + 32 * piece
                    rows_out[pl.ds(pl.multiple_of(place, 32), 32), pl.ds(tile, 128)] = turned[
                        start : start + 32
                    ]


def gather_kernels(conv_weight, conv_bias, conv_stitch, sel, s, m, token):
    turned = conv_weight.transpose(0, 2, 1)
    rows = turned.shape[2]
    if lax.axis_size("dp") == 4:
        shape = struct((64, rows + 32), BF16)
        inputs = [turned, conv_bias, conv_stitch]
        own = call(
            own_kernel,
            "own_kernels",
            [sel] + [pltpu.with_memory_space_constraint(v, pltpu.HBM) for v in inputs],
            shape,
            scratch=[pltpu.VMEM((64, rows), BF16)]
            + [pltpu.VMEM(v.shape, F32) for v in inputs[1:]]
            + [pltpu.SemaphoreType.DMA((3,))],
            specs=[SMEM] + [HBM] * 3,
        )
        near = call(
            join_kernel,
            "join_kernels",
            [own, swap(own, "mp", 2)],
            struct((2, *own.shape), BF16),
            (token,),
        )
        column = {k: swap(near, "dp", k) for k in (3, 2, 1)}
        column = [near, column[1], column[2], column[3]]
        first = call(join_kernel, "join_columns", column[:2], struct((2, *near.shape), BF16))
        column = [first, *column[2:]]
        across = [swap(part, "mp", 1) for part in column]
        kernel, params = call(
            kernels_kernel,
            "kernels",
            [sel, *column, *across],
            [struct((4 * rows, OUT), BF16), struct((8, OUT), F32)],
        )
        return kernel, params, near
    own = lax.dynamic_index_in_dim(conv_weight, s, 0, keepdims=False)
    full = lax.all_gather(lax.all_gather(own, "dp", axis=0), "mp", axis=2, tiled=True)
    kernel = relative(full.reshape(9, 4, BLK, OUT), m, 1)
    last = kernel[:, 3].reshape(9, 3, 32, OUT)
    kernel = jnp.concatenate([kernel[:, :3], last], 2).reshape(36 * BLK, OUT)
    params = jnp.concatenate([conv_bias, conv_stitch.reshape(4, 64), jnp.zeros((2, 64), F32)], 0)
    params = lax.all_gather(params, "mp", axis=1, tiled=True)
    return kernel, params, jnp.zeros((8, 128), F32)


def split_kernel(sel, grad, small, keep, send):
    d, m = sel[D], sel[M]
    odd = lax.rem(m, 2) == 1
    lane = lane_index(32)

    def write(rows, place):
        count = rows.shape[0]
        t0, t1 = rows[:, 0:128], rows[:, 128:256]
        low = jnp.where(lane[:count] < 64, t0, pltpu.roll(t1, 64, 1)).astype(BF16)
        high = jnp.where(lane[:count] < 64, pltpu.roll(t0, 64, 1), t1).astype(BF16)
        here = pl.ds(pl.multiple_of(place, 16), count)
        keep[here, :] = jnp.where(odd, high, low)
        send[here, :] = jnp.where(odd, low, high)

    for tap in range(9):
        for block in range(4):
            index = tap * 4 + (block ^ m)
            part = lax.div(index, 9)
            place = (part ^ d) * (ROWS + 16) + (index - part * 9) * BLK
            for piece in range(3):
                start = tap * 4 * BLK + (128 * piece + BLK if block == 3 else 128 * block + 32 * piece)
                write(grad[start : start + 32, :], place + 32 * piece)
    sums = jnp.concatenate([small[...], jnp.zeros((16 - small.shape[0], OUT), F32)], 0)
    for part in range(4):
        write(sums, part * (ROWS + 16) + ROWS)


def pair_kernel(keep, arrived, own, *sends):
    size = ROWS + 16
    for k in range(4):
        here = slice(k * size, (k + 1) * size)
        total = keep[here, :].astype(F32) + arrived[here, :].astype(F32)
        if k == 0:
            own[...] = total
        else:
            sends[k - 1][...] = total.astype(BF16)


def turn_kernel(sel, own, a, b, c, mine, send):
    total = own[...] + a[...].astype(F32) + b[...].astype(F32) + c[...].astype(F32)
    total = jnp.concatenate([total, jnp.zeros((16, 128), F32)], 0).T
    low = sel[M] < 2
    mine[...] = jnp.where(low, total[:64], total[64:])
    send[...] = jnp.where(low, total[64:], total[:64]).astype(BF16)


def finish_kernel(sel, mine, arrived, rows, bias, stitch):
    rows[...] = mine[:, :ROWS] + arrived[:, :ROWS].astype(F32)
    last = slice(ROWS - BLK, ROWS + 32)
    small = (mine[:, last] + arrived[:, last].astype(F32)).T
    stitch[pl.ds(sel[S], 1), :] = small[BLK : BLK + 1]
    stitch[pl.ds(1 - sel[S], 1), :] = small[BLK + 1 : BLK + 2]
    bias[...] = small[BLK + 2 : BLK + 3]


def scatter_kernels(grad, small, sel, s, m, meanwhile, finish_fc):
    rows = grad.shape[0] // lax.axis_size("dp")
    small_shapes = [struct((1, 64), F32), struct((2, 64), F32)]
    if lax.axis_size("dp") == 4:
        size = ROWS + 16
        keep, send = call(
            split_kernel, "split_kernels", [sel, grad, small], [struct((4 * size, 128), BF16)] * 2
        )
        own, *sends = call(
            pair_kernel,
            "pair_kernels",
            [keep, swap(send, "mp", 1)],
            [struct((size, 128), F32)] + [struct((size, 128), BF16)] * 3,
            meanwhile(),
        )
        last = call(
            copy_kernel, "last_kernels", sends[2:], struct((size, 128), BF16), finish_fc(own)
        )
        arrived = [swap(part, "dp", k) for k, part in zip((1, 2, 3), (*sends[:2], last))]
        mine, other = call(
            turn_kernel,
            "turn_kernels",
            [sel, own, *arrived],
            [struct((64, ROWS + 32), F32), struct((64, ROWS + 32), BF16)],
        )
        result, bias, stitch = call(
            finish_kernel,
            "finish_kernels",
            [sel, mine, swap(other, "mp", 2)],
            [struct((64, ROWS), F32), *small_shapes],
        )
        return result.T, bias, stitch, own
    grad = grad.reshape(9, 3, 128, OUT)
    last = grad[:, :, BLK:].reshape(9, 1, BLK, OUT)
    grad = jnp.concatenate([grad[:, :, :BLK], last], 1)
    grad = relative(grad, m, 1).reshape(36 * BLK, OUT).astype(BF16)
    grad = lax.psum_scatter(grad, "mp", scatter_dimension=1, tiled=True)
    grad = lax.psum_scatter(grad, "dp", scatter_dimension=0, tiled=True).astype(F32)
    small = sum_over(sum_over(small, "dp"), "mp")
    small = lax.dynamic_slice_in_dim(small, m * 64, 64, 1)
    stitch = jnp.stack([jnp.where(s == 0, small[0], small[1]), jnp.where(s == 0, small[1], small[0])])
    meanwhile()
    finish_fc(small)
    return grad, small[2:3], stitch, small


def gelu_parts(value):
    scale = 0.7978845608028654
    square = value * value
    curve = jnp.tanh(scale * value * (1.0 + 0.044715 * square))
    return curve, square, scale


def gelu(value):
    curve, _, _ = gelu_parts(value)
    return 0.5 * value * (1.0 + curve)


def gelu_slope(value):
    curve, square, scale = gelu_parts(value)
    bend = (0.5 * scale) * value * (1.0 - curve * curve) * (1.0 + 0.134145 * square)
    return 0.5 * (1.0 + curve) + bend


def place_of(sel, k, p):
    return 9 * (lax.rem(sel[D], 4) ^ k) + p


def half_kernel(first, sel, pooled, out):
    for k in range(2):
        for p in range(9):
            out[k, p] = pooled[place_of(sel, first + k, p)].astype(BF16)


def pool_kernel(sel, conv_out, params, pooled, far):
    extent = jnp.where(is_low(sel), POOL_LOW, POOLED)
    shift = params[pl.ds(sel[S], 1), :]
    lines = []
    for i in range(SIDE):
        cells = [gelu(conv_out[i, j] + shift) for j in range(SIDE)]
        lines.append([cells[2 * q] + cells[2 * q + 1] + cells[2 * q + 2] for q in range(POOLED)])
        if i >= 2 and i % 2 == 0:
            p = i // 2 - 1
            for q in range(POOLED):
                total = lines[i - 2][q] + lines[i - 1][q] + lines[i][q]
                keep = jnp.logical_and(p < extent, q < extent).astype(F32) / 9.0
                total = total * keep
                pooled[POOLED * p + q] = total
    half_kernel(2, sel, pooled, far)


def slope_kernel(sel, conv_out, params, slope):
    shift = params[pl.ds(sel[S], 1), :]
    for i in range(SIDE):
        for j in range(SIDE):
            slope[SIDE * i + j] = gelu_slope(conv_out[i, j] + shift)


def entry(params, t, u):
    return params[pl.ds(2 + 2 * t + u, 1), :]


def stitch_kernel(first, sel, pooled, other, params, *chunks):
    s = sel[S]
    by_own, by_other = entry(params, s, s), entry(params, s, 1 - s)
    for k, chunk in enumerate(chunks):
        for p in range(9):
            mixed = by_own * pooled[place_of(sel, first + k, p)] + by_other * other[k, p].astype(F32)
            chunk[p] = mixed.astype(BF16)


def conv_grad_kernel(
    sel, near, far, near_other, far_other, slope, pooled, near_pooled, far_pooled, params, out, sums, mixed
):
    extent, s = jnp.where(is_low(sel), POOL_LOW, POOLED), sel[S]
    by_own, by_other = entry(params, s, s), entry(params, 1 - s, s)
    own_sum = other_sum = jnp.zeros((IMG, OUT), F32)
    for k in range(4):
        grad = near.at[k] if k < 3 else far
        grad_other = near_other.at[k] if k < 3 else far_other
        pooled_other = (near_pooled, far_pooled)[k // 2]
        for p in range(9):
            place = place_of(sel, k, p)
            mine = grad[p].astype(F32)
            mixed[place] = by_own * mine + by_other * grad_other[p].astype(F32)
            own_sum = own_sum + mine * pooled[place]
            other_sum = other_sum + mine * pooled_other[k % 2, p].astype(F32)
    spread = []
    for p in range(POOLED):
        line = []
        for q in range(POOLED):
            keep = jnp.logical_and(p < extent, q < extent).astype(F32) / 9.0
            line.append(mixed[POOLED * p + q] * keep)
        spread.append(line)
    bias_sum = jnp.zeros((IMG, OUT), F32)

    def over(values, index):
        near, far = index // 2, index // 2 - 1
        if index % 2 == 1 or index == 0:
            return values[near]
        if near >= POOLED:
            return values[far]
        return values[near] + values[far]

    for i in range(SIDE):
        line = [over([spread[p][q] for p in range(POOLED)], i) for q in range(POOLED)]
        for j in range(SIDE):
            cell = SIDE * i + j
            value = (slope[cell] * over(line, j)).astype(BF16)
            out[cell] = value
            bias_sum = bias_sum + value.astype(F32)
    for row, total in enumerate((own_sum, other_sum, bias_sum)):
        sums[row : row + 1, :] = jnp.sum(total, 0, keepdims=True)


def all_acts(acts, place):
    return jnp.concatenate([a[:, place].reshape(-1, OUT) for a in acts], 0)


def all_grads(grads):
    return jnp.concatenate([g[r] for r in range(4) for g in grads], 0)


def load_kernel(sel, weight, out, token, done):
    token[...] = jnp.zeros(token.shape, F32)
    count = done.shape[0]
    size = weight.shape[1] // count
    copies = []
    for part in range(count):
        here = pl.ds(part * size, size)
        copies.append(pltpu.make_async_copy(weight.at[sel[S], here], out.at[here], done.at[part]))
        copies[-1].start()
    for copy in copies:
        copy.wait()


def load_matrix(weight, sel, s, after):
    if lax.axis_size("dp") != 4:
        return lax.dynamic_index_in_dim(weight, s, 0, keepdims=False), ()
    matrix, token = call(
        load_kernel,
        "load_matrix",
        [sel, pltpu.with_memory_space_constraint(weight, pltpu.HBM)],
        [struct(weight.shape[1:], BF16), struct((8, 128), F32)],
        after,
        scratch=[pltpu.SemaphoreType.DMA((9,))],
        specs=[SMEM, HBM],
    )
    return matrix, (token,)


def fc_forward_kernel(*refs):
    acts, (weight, own, *sends) = refs[:8], refs[8:]
    rows = jnp.concatenate([all_acts(acts, p) for p in range(9)], 1)
    for n in range(weight.shape[1] // 256):
        here = slice(n * 256, (n + 1) * 256)
        term = jnp.dot(rows, weight[:, here], preferred_element_type=F32)
        for r in range(4):
            for k in range(4):
                part = term[(4 * r + k) * IMG : (4 * r + k + 1) * IMG]
                if k == 0:
                    own[r, :, here] = part
                else:
                    sends[k - 1][r, :, here] = part.astype(BF16)


def fc_active_kernel(sel, own, a, b, c, bias, stitch, cot, grad, active, sent, sums):
    s, m = sel[S], sel[M]
    for n in range(own.shape[2] // 256):
        here = slice(n * 256, (n + 1) * 256)
        shift = bias[pl.ds(s, 1), here]
        w0, w1 = stitch[0, pl.ds(s, 1), here], stitch[1, pl.ds(s, 1), here]
        sum0 = sum1 = jnp.zeros((IMG, 256), F32)
        for r in range(4):
            value = own[r, :, here] + a[r, :, here].astype(F32)
            value = value + (b[r, :, here].astype(F32) + c[r, :, here].astype(F32)) + shift
            curve, square, scale = gelu_parts(value)
            half = 0.5 * (1.0 + curve)
            bend = (0.5 * scale) * value * (1.0 - curve * curve) * (1.0 + 0.134145 * square)
            result = value * half
            c0, c1 = cot[0, m ^ r, :, here].astype(F32), cot[1, m ^ r, :, here].astype(F32)
            grad[r, :, here] = ((half + bend) * (w0 * c0 + w1 * c1)).astype(BF16)
            active[r, :, here] = result
            sent[r, :, here] = result.astype(BF16)
            sum0 = sum0 + c0 * result
            sum1 = sum1 + c1 * result
        for t, total in enumerate((sum0, sum1)):
            sums[4 * t + n : 4 * t + n + 1, :] = jnp.sum(total, 0, keepdims=True)


def fc_rows_kernel(*refs):
    grads, (weight, keep, send) = refs[:-3], refs[-3:]
    rows = all_grads(grads)
    for p in range(9):
        term = lax.dot_general(
            rows,
            weight[p * 256 : (p + 1) * 256, :],
            (((1,), (1,)), ((), ())),
            preferred_element_type=F32,
        )
        term = term.reshape(4, len(grads), IMG, 256)
        for r in range(4):
            if r % 2 == 0:
                keep[r // 2, :, p] = term[r]
            else:
                send[r // 2, :, p] = term[r].astype(BF16)


def cross_kernel(keep, arrived, out):
    out[...] = (keep[1] + arrived[1].astype(F32)).astype(BF16)


def home_kernel(keep, arrived, crossed, sums, *chunks):
    high = sums[...].astype(BF16).astype(F32)
    small = jnp.concatenate([high, sums[...] - high], 0).astype(BF16)
    for k in range(len(chunks)):
        total = keep[0, k] + arrived[0, k].astype(F32) + crossed[k].astype(F32)
        chunks[k][0:9] = total.astype(BF16)
        chunks[k][9] = small


def fc_matrix_kernel(*refs):
    acts, refs = refs[:8], refs[8:]
    g0, g1, g2, g3, out, bias, token, part, sent = refs
    token[...] = jnp.zeros(token.shape, F32)
    grads = all_grads((g0, g1, g2, g3))

    def copy(p):
        return pltpu.make_async_copy(part.at[p % 3], out.at[pl.ds(p * 256, 256)], sent.at[p % 3])

    for p in range(9):
        rows = all_acts(acts, p).T
        if p >= 3:
            copy(p - 3).wait()
        part[p % 3] = jnp.dot(rows, grads, preferred_element_type=F32)
        copy(p).start()
    bias[...] = jnp.sum(grads.astype(F32), 0, keepdims=True)
    for p in range(6, 9):
        copy(p).wait()


def copy_kernel(value, out):
    out[...] = value[...]


def outputs_kernel(sel, active, arrived, stitch, out):
    s, m = sel[S], sel[M]
    for n in range(active.shape[2] // 256):
        here = slice(n * 256, (n + 1) * 256)
        by_own = jnp.where(s == 0, stitch[0, 0:1, here], stitch[1, 1:2, here])
        by_other = jnp.where(s == 0, stitch[0, 1:2, here], stitch[1, 0:1, here])
        for r in range(4):
            mixed = by_own * active[r, :, here] + by_other * arrived[r, :, here].astype(F32)
            out[m ^ r, :, here] = mixed.astype(BF16)


def plane_sum(near, far):
    total = jnp.zeros((8, OUT), F32)
    for plane in (near[0, 9], near[1, 9], near[2, 9], far[9]):
        plane = plane.astype(F32)
        total = total + (plane[0:8] + plane[8:16])
    return total


def stitch_sums_kernel(sel, near, far, near_other, far_other, out, own, other):
    s = sel[S]
    own[...] = plane_sum(near, far)
    other[...] = plane_sum(near_other, far_other)
    for n in range(4):
        here = slice(n * OUT, (n + 1) * OUT)
        out[pl.ds(s, 1), here] = own[pl.ds(4 * s + n, 1), :]
        out[pl.ds(1 - s, 1), here] = other[pl.ds(4 * s + n, 1), :]


def fc_section(pooled, near, far, params, own_weight, bias, stitch, cot, sel, s, d, m):
    count = lax.axis_size("dp")
    hid = own_weight.shape[1]
    plane = struct((9, IMG, OUT), BF16)
    block = struct((4, IMG, hid), BF16)
    token = struct((8, 128), F32)
    chunks = [None] * 4
    chunks[2:] = call(
        partial(stitch_kernel, 2), "stitch_far", [sel, pooled, far, params], [plane] * 2
    )
    chunks[:2] = call(
        partial(stitch_kernel, 0), "stitch_near", [sel, pooled, near, params], [plane] * 2, chunks[2:3]
    )
    if count == 4:
        def over_mp(acts):
            far = swap(acts, "mp", 2)
            return [acts, swap(acts, "mp", 1), far, swap(far, "mp", 1)]

        two = struct((2, 9, IMG, OUT), BF16)
        moved = [swap(chunks[2], "dp", 2), swap(chunks[3], "dp", 3)]
        far_acts = call(join_kernel, "join_acts_far", moved, two)
        moved = [chunks[0], swap(chunks[1], "dp", 1)]
        near_acts = call(join_kernel, "join_acts_near", moved, two, (far_acts,))
        acts = [a for pair in zip(over_mp(near_acts), over_mp(far_acts)) for a in pair]
        pre, *sends = call(
            fc_forward_kernel,
            "fc_forward",
            [*acts, own_weight],
            [struct((4, IMG, hid), F32)] + [block] * 3,
        )
        arrived = [swap(part, "dp", k) for k, part in zip((1, 2, 3), sends)]
    else:
        shared = by_position(chunks, d)
        flat = shared.transpose(1, 0, 2).reshape(IMG, count, -1).transpose(1, 0, 2)
        flat = lax.all_to_all(flat, "dp", 0, 0, tiled=True)
        flat = lax.all_gather(flat, "mp", axis=0)
        flat = relative(flat, m)
        pre = jnp.einsum("rdnf,fk->drnk", flat, own_weight, preferred_element_type=F32)
        pre = lax.psum_scatter(pre.astype(BF16), "dp", scatter_dimension=0, tiled=True)
        pre = pre.reshape(4, IMG, hid).astype(F32)
        arrived = [jnp.zeros(block.shape, BF16)] * 3
    pre_grad, active, sent, sums = call(
        fc_active_kernel,
        "fc_active",
        [sel, pre, *arrived, bias, stitch, cot],
        [block, struct(block.shape, F32), block, struct((8, OUT), F32)],
    )
    if count == 4:
        grads = gather4(pre_grad)
        ten = struct((10, IMG, OUT), BF16)

        marks = []

        def home(ks, name, after=()):
            shape = (2, len(ks), 9, IMG, OUT)
            keep, send = call(
                fc_rows_kernel,
                "fc_rows_" + name,
                [*[grads[k] for k in ks], own_weight],
                [struct(shape, F32), struct(shape, BF16)],
                after,
            )
            arrived = swap(send, "mp", 1)
            crossing = call(cross_kernel, "cross_" + name, [keep, arrived], struct(shape[1:], BF16))
            crossed = swap(crossing, "mp", 2)
            inputs = [keep, arrived, crossed, sums]
            marks.append(crossing)
            return call(home_kernel, "home_" + name, inputs, [ten] * len(ks))

        chunks = home((0, 1, 2), "near")
        moved = [chunks[0], swap(chunks[1], "dp", 1), swap(chunks[2], "dp", 2)]
        (chunk,) = home((3,), "far", marks[:1])
        def matrix_gradient(after, grads=tuple(grads)):
            return call(
                fc_matrix_kernel,
                "fc_matrix",
                [*acts, *grads],
                [struct(own_weight.shape, F32), struct((1, hid), F32), token],
                after,
                scratch=[pltpu.VMEM((3, 256, hid), F32), pltpu.SemaphoreType.DMA((3,))],
                limit=10 << 20,
                out_specs=[HBM, VMEM, VMEM],
            )

        near_grad = call(join_kernel, "join_near", moved, struct((3, *ten.shape), BF16), (chunk,))
        near_back = (near_grad, swap(near_grad, "section", 1))
        far_grad = swap(chunk, "dp", 3)
        far_back = (far_grad, swap(far_grad, "section", 1))
    else:
        grads = lax.all_gather(pre_grad, "dp", axis=0)
        rows = jnp.einsum("drnk,fk->rdnf", grads, own_weight, preferred_element_type=F32)
        rows = relative(rows, m).astype(BF16)
        rows = lax.psum_scatter(rows, "mp", scatter_dimension=0, tiled=True)[0]
        rows = lax.all_to_all(rows, "dp", 0, 0, tiled=True)
        back = rows.transpose(1, 0, 2).reshape(IMG, 4, 9, OUT).transpose(1, 2, 0, 3)
        matrix_grad = jnp.einsum("rdnf,drnk->fk", flat, grads, preferred_element_type=F32)
        bias_sum = jnp.sum(grads.astype(F32), (0, 1, 2))[None]

        def matrix_gradient(after):
            return matrix_grad, bias_sum, sums

        total = sum_over(sums, "dp")
        high = lax.reduce_precision(total, 8, 7)
        small = jnp.concatenate([high, total - high], 0).astype(BF16)
        small = jnp.stack([small] + [jnp.zeros_like(small)] * 3)
        back = jnp.concatenate([relative(back, lax.rem(d, 4)), small[:, None]], 1)
        near_back, far_back = [(part, swap(part, "section", 1)) for part in (back[:3], back[3])]
    stitch_sum = call(
        stitch_sums_kernel,
        "stitch_sums",
        [sel, near_back[0], far_back[0], near_back[1], far_back[1]],
        struct((2, hid), F32),
        scratch=[pltpu.VMEM((8, OUT), F32)] * 2,
    )
    grads = [near_back[0], far_back[0], near_back[1], far_back[1]]
    return grads, (active, sent), matrix_gradient, stitch_sum


def by_position(chunks, d):
    return relative(jnp.stack(chunks), lax.rem(d, 4)).reshape(PLACES, IMG, OUT)


def conv(maps, taps, rows, form, kind=F32):
    return lax.conv_general_dilated(
        maps,
        taps,
        (1, 1),
        (rows, (1, 1)),
        dimension_numbers=form,
        preferred_element_type=F32,
    ).astype(kind)


def on_device(
    conv_input,
    group_ids,
    conv_weight,
    conv_bias,
    conv_stitch,
    fc_weight,
    fc_bias,
    fc_stitch,
    cotangent,
):
    s = lax.axis_index("section")
    d = lax.axis_index("dp")
    m = lax.axis_index("mp")
    assert conv_input.shape == (4, IMG, 2, SIDE, SIDE, BLK) and lax.axis_size("mp") == 4
    sel = jnp.concatenate([scalars(s, d, m), group_ids])

    by_row = conv_input.transpose(0, 1, 3, 4, 2, 5).reshape(4, IMG * CELLS * 2, BLK)
    by_row = pltpu.with_memory_space_constraint(by_row, pltpu.HBM)
    far3, far2, token = pack_maps(by_row, sel, 3)
    kernel, params, early = gather_kernels(conv_weight, conv_bias, conv_stitch, sel, s, m, token)
    cot = lax.dynamic_slice_in_dim(cotangent, d * IMG, IMG, 1).transpose(2, 0, 1, 3)
    matrix, loaded = load_matrix(fc_weight, sel, s, (token,))
    near1, near0, token = pack_maps(by_row, sel, 1, (token, early, cot, *loaded))
    wires = [near0, swap(near1, "mp", 1), swap(far2, "mp", 2), swap(far3, "mp", 3)]

    taps = kernel.reshape(3, 3, 4 * BLK, OUT)
    maps = call(
        unpack_kernel,
        "unpack_maps",
        [sel, *wires],
        struct((CELLS * IMG, 4 * BLK), BF16),
    )
    maps = maps.reshape(SIDE, SIDE, IMG, 4 * BLK)
    conv_out = conv(maps, taps, (1, 1), ("HWNC", "HWIO", "HWNC"))
    half = struct((2, 9, IMG, OUT), BF16)
    pooled, far = call(
        pool_kernel, "pool", [sel, conv_out, params], [struct((PLACES, IMG, OUT), F32), half]
    )
    near = call(partial(half_kernel, 0), "pool_near", [sel, pooled], half)
    far = swap(far, "section", 1)
    near = swap(near, "section", 1)

    back, outputs, matrix_gradient, fc_stitch_sum = fc_section(
        pooled, near, far, params, matrix, fc_bias, fc_stitch, cot, sel, s, d, m
    )
    slope = call(
        slope_kernel,
        "slope",
        [sel, conv_out, params],
        struct((CELLS, IMG, OUT), F32),
        (back[0],),
    )
    conv_grad, sums = call(
        conv_grad_kernel,
        "conv_gradient",
        [sel, *back, slope, pooled, near, far, params],
        [struct((CELLS, IMG, OUT), BF16), struct((3, OUT), F32)],
        scratch=[pltpu.VMEM((PLACES, IMG, OUT), F32)],
    )
    conv_grad = conv_grad.reshape(SIDE, SIDE, IMG, OUT)

    back_taps = taps[::-1, ::-1]
    wires = []

    def send_input_grad(after=()):
        chunk = len(wires)
        low, high = HALVES[chunk]
        padding = (1 - low, 1 - SIDE + high)
        part = conv(conv_grad, back_taps, padding, ("HWNC", "HWOI", "HWNC"), BF16)
        sends = pack_grad(part.reshape(-1, 4 * BLK), sel, HALVES[chunk], after)
        wires.append([sends[0]] + [swap(sends[k], "mp", k) for k in (1, 2, 3)])
        return (sends[0],)

    maps = pass_on(maps, send_input_grad())
    kernel_grad = conv(maps, conv_grad, (1, 1), ("HWCN", "HWIO", "HWNC"))
    results = []

    def finish_fc(begun):
        results.extend(matrix_gradient((begun,)))
        return results[-1:]

    kernel_rows, conv_bias_sum, conv_stitch_sum, begun = scatter_kernels(
        kernel_grad.reshape(36 * BLK, OUT), sums, sel, s, m, lambda: (), finish_fc
    )
    matrix_grad, fc_bias_sum, _ = results
    mark = send_input_grad((*wires[0][2:], begun))
    active, sent = outputs
    sent = call(copy_kernel, "outputs_send", [sent], struct(sent.shape, BF16), mark)
    outputs = call(
        outputs_kernel,
        "outputs",
        [sel, active, swap(sent, "section", 1), fc_stitch],
        struct(sent.shape, BF16),
    )
    input_grad = place_grad(wires[0], sel, HALVES[0], (0, 1, 2, 3), None)
    input_grad = place_grad(wires[1][:2], sel, HALVES[1], (0, 1), input_grad)
    input_grad = place_grad(wires[1][2:], sel, HALVES[1], (2, 3), input_grad)
    input_grad = input_grad.reshape(4, 1, SIDE, SIDE, IMG, BLK).transpose(0, 4, 1, 2, 3, 5)
    return (
        outputs[:, :, None],
        input_grad,
        kernel_rows[None],
        conv_bias_sum,
        conv_stitch_sum[None],
        matrix_grad[None],
        fc_bias_sum,
        fc_stitch_sum[None],
    )


def solution(mesh):
    placed = (
        P(None, "dp", None, None, None, "mp"),
        P(),
        P(None, "dp", "mp"),
        P(None, "mp"),
        P(None, None, "mp"),
        P(None, "dp", "mp"),
        P(None, "mp"),
        P(None, None, "mp"),
        P(None, None, None, "mp"),
    )
    return jax.shard_map(
        on_device,
        mesh=mesh,
        in_specs=placed,
        out_specs=(
            P(None, "dp", "section", "mp"),
            P(None, "dp", "section", None, None, "mp"),
            P("section", "dp", "mp"),
            P("section", "mp"),
            P("section", None, "mp"),
            P("section", "dp", "mp"),
            P("section", "mp"),
            P("section", None, "mp"),
        ),
        check_vma=False,
    )
```

```python
from functools import partial

import jax
import jax.numpy as jnp
from jax import lax
from jax.experimental import pallas as pl
from jax.experimental.pallas import tpu as pltpu
from jax.sharding import PartitionSpec as P


MAP_LOW = 11
POOL_LOW = 5
SIDE = 13
POOLED = 6
CELLS = SIDE * SIDE
PLACES = POOLED * POOLED
IMG = 16
BLK = 96
OUT = 256
ROWS = 9 * BLK
WHOLE = (0, 13)
HALVES = ((0, 7), (7, 13))
SCOPE = 4 << 20
F32 = jnp.float32
BF16 = jnp.bfloat16
VMEM = pl.BlockSpec(memory_space=pltpu.VMEM)
SMEM = pl.BlockSpec(memory_space=pltpu.SMEM)
ANY = pl.BlockSpec(memory_space=pl.ANY)
HBM = pl.BlockSpec(memory_space=pltpu.HBM)


def swap(value, axis, bit):
    count = lax.axis_size(axis)
    return lax.ppermute(value, axis, [(i, i ^ bit) for i in range(count)])


def gather4(value):
    near = swap(value, "dp", 1)
    far = swap(value, "dp", 2)
    return [value, near, far, swap(far, "dp", 1)]


def sum_over(value, axis):
    bit = 1
    while bit < lax.axis_size(axis):
        value = value + swap(value, axis, bit)
        bit *= 2
    return value


def relative(value, index, axis=0):
    return jnp.concatenate(
        [lax.dynamic_slice_in_dim(value, index ^ k, 1, axis) for k in range(4)], axis
    )


def scalars(*values):
    return jnp.stack(values).astype(jnp.int32)


S, D, M, GROUPS = range(4)
COST = pl.CostEstimate(flops=1, bytes_accessed=1, transcendentals=0)


def is_low(sel):
    return sel[GROUPS + sel[M]] == 1


def struct(shape, dtype):
    return jax.ShapeDtypeStruct(shape, dtype)


def call(body, name, inputs, outs, after=(), scratch=(), limit=SCOPE, specs=None, out_specs=None):
    if specs is None:
        specs = [SMEM if v.dtype == jnp.int32 else VMEM for v in inputs]
    count = len(inputs)

    def kernel(*refs):
        body(*refs[:count], *refs[count + len(after) :])

    single = not isinstance(outs, (list, tuple))
    if out_specs is None:
        out_specs = VMEM if single else [VMEM] * len(outs)
    return pl.pallas_call(
        kernel,
        in_specs=specs + [VMEM] * len(after),
        out_specs=out_specs,
        out_shape=outs if single else list(outs),
        scratch_shapes=list(scratch),
        compiler_params=pltpu.CompilerParams(vmem_limit_bytes=limit),
        cost_estimate=COST,
        name=name,
    )(*inputs, *after)


def pass_on(value, after):
    def kernel(*refs):
        pass

    return pl.pallas_call(
        kernel,
        in_specs=[ANY] + [VMEM] * len(after),
        out_specs=ANY,
        out_shape=struct(value.shape, value.dtype),
        input_output_aliases={0: 0},
        compiler_params=pltpu.CompilerParams(vmem_limit_bytes=SCOPE),
        cost_estimate=COST,
        name="pass_on",
    )(value, *after)


def lane_index(rows=IMG):
    return lax.broadcasted_iota(jnp.int32, (rows, 128), 1)


def join4(parts, lane):
    last = parts[3]
    return [jnp.where(lane < BLK, parts[j], pltpu.roll(last, 96 - 32 * j, 1)) for j in range(3)]


def last_part(tiles, lane):
    a, b, c = [pltpu.roll(tiles[j], 32 + 32 * j, 1) for j in range(3)]
    return jnp.where(lane < 32, a, jnp.where(lane < 64, b, c))


def tiles_of(row):
    return [row[:, 0:128], row[:, 128:256], row[:, 256:384]]


def exchange(rows, lane):
    rows = [tiles_of(row) for row in rows]
    out = []
    for k in range(3):
        last = rows[3][k]
        out.append(
            [
                jnp.where(lane < BLK, rows[j][k], pltpu.roll(last, 96 - 32 * j, 1))
                for j in range(3)
            ]
        )
    thirds = [last_part(rows[q], lane) for q in range(3)]
    out.append([jnp.where(lane < BLK, thirds[j], rows[3][j]) for j in range(3)])
    return [jnp.concatenate(tiles, 1) for tiles in out]


def chunk_cells(chunk):
    return SIDE * chunk[0], SIDE * (chunk[1] - chunk[0])


def chunk_group(chunk):
    return -(-chunk_cells(chunk)[1] // 4)


def wire_shape(chunk):
    return (chunk_group(chunk) * IMG, 4 * BLK)


def masked(row, cell, whole):
    if cell // SIDE >= MAP_LOW or cell % SIDE >= MAP_LOW:
        return row * whole
    return row


def whole_map(sel):
    return jnp.where(is_low(sel), 0.0, 1.0).astype(BF16)


def at(cell):
    return pl.ds(cell * IMG, IMG)


def pack_kernel(count, sel, maps, *refs):
    wires, token, rows = refs[count:-2], refs[-2], refs[-1]
    token[...] = jnp.zeros(token.shape, F32)
    tower = sel[S]

    def widen(step, _):
        rows[pl.ds(step * 208, 208), :BLK] = maps[0, pl.ds(step * 208, 208), :].astype(F32)
        return 0

    lax.fori_loop(0, 26, widen, 0, unroll=2)
    lane = lane_index()

    def cell(index):
        start = 2 * index + tower
        return jnp.concatenate(
            [
                rows[pl.ds(start, 8, stride=2 * CELLS), :],
                rows[pl.ds(start + 16 * CELLS, 8, stride=2 * CELLS), :],
            ],
            0,
        ).astype(BF16)

    def fill(wire):
        group = chunk_group(WHOLE)
        for step in range(group):
            parts = [cell(min(step + group * q, CELLS - 1)) for q in range(4)]
            wire[at(step), :] = jnp.concatenate(join4(parts, lane), 1)

    pl.when(pl.program_id(0) == 0)(partial(fill, wires[0]))
    pl.when(pl.program_id(0) == 1)(partial(fill, wires[1]))


def pack_maps(maps, sel, first, after=()):
    shape = wire_shape(WHOLE)
    return pl.pallas_call(
        partial(pack_kernel, len(after)),
        grid_spec=pltpu.PrefetchScalarGridSpec(
            num_scalar_prefetch=1,
            grid=(2,),
            in_specs=[pl.BlockSpec((1, IMG * CELLS * 2, BLK), lambda i, sel: (sel[M] ^ (first - i), 0, 0))]
            + [VMEM] * len(after),
            out_specs=[pl.BlockSpec(shape, lambda i, sel: (0, 0))] * 2
            + [pl.BlockSpec((8, 128), lambda i, sel: (0, 0))],
            scratch_shapes=[pltpu.VMEM((IMG * CELLS * 2 + 2 * CELLS + 14, 128), F32)],
        ),
        out_shape=[struct(shape, BF16)] * 2 + [struct((8, 128), F32)],
        compiler_params=pltpu.CompilerParams(vmem_limit_bytes=12 << 20),
        cost_estimate=COST,
        name="pack_maps",
    )(sel, maps, *after)


def unpack_kernel(sel, w0, w1, w2, w3, maps):
    lane = lane_index()
    whole = whole_map(sel)
    group = chunk_group(WHOLE)
    for step in range(group):
        rows = exchange([w[at(step), :] for w in (w0, w1, w2, w3)], lane)
        for q in range(4):
            cell = step + group * q
            if cell < CELLS:
                maps[at(cell), :] = masked(rows[q], cell, whole)


def pack_grad_kernel(chunk, sel, grad, *wires):
    lane = lane_index()
    whole = whole_map(sel)
    first, cells = chunk_cells(chunk)
    group = chunk_group(chunk)
    for step in range(group):
        rows = []
        for q in range(4):
            cell = min(step + group * q, cells - 1)
            rows.append(masked(grad[at(cell), :], first + cell, whole))
        for wire, row in zip(wires, exchange(rows, lane)):
            wire[at(step), :] = row


def pack_grad(grad, sel, chunk, after=()):
    shape = struct(wire_shape(chunk), BF16)
    return call(partial(pack_grad_kernel, chunk), "pack_grad", [sel, grad], [shape] * 4, after)


def place_grad_kernel(chunk, ks, sel, *refs):
    wires = refs[: len(ks)]
    out, parts, sent = refs[-3:]
    lane = lane_index()
    first, cells = chunk_cells(chunk)
    group = chunk_group(chunk)
    copies = []
    for index, (k, wire) in enumerate(zip(ks, wires)):
        for step in range(group):
            tiles = tiles_of(wire[at(step), :])
            tiles.append(last_part(tiles, lane))
            for q in range(4):
                if step + group * q < cells:
                    parts[index, at(step + group * q), :] = tiles[q][:, :BLK]
        place = out.at[sel[M] ^ k, pl.ds(first * IMG, cells * IMG)]
        copies.append(pltpu.make_async_copy(parts.at[index], place, sent.at[index]))
        copies[-1].start()
    for copy in copies:
        copy.wait()


def place_grad(wires, sel, chunk, ks, total):
    args = [sel, *wires]
    in_specs = [SMEM] + [VMEM] * len(wires)
    alias = {}
    if total is not None:
        alias = {len(args): 0}
        args.append(total)
        in_specs.append(ANY)
    cells = chunk_cells(chunk)[1]
    return pl.pallas_call(
        partial(place_grad_kernel, chunk, ks),
        in_specs=in_specs,
        out_specs=ANY,
        out_shape=struct((4, CELLS * IMG, BLK), BF16),
        scratch_shapes=[
            pltpu.VMEM((len(ks), cells * IMG, BLK), BF16),
            pltpu.SemaphoreType.DMA((len(ks),)),
        ],
        input_output_aliases=alias,
        compiler_params=pltpu.CompilerParams(vmem_limit_bytes=8 << 20),
        cost_estimate=COST,
        name="place_grad",
    )(*args)


def join_kernel(*refs):
    for k, part in enumerate(refs[:-1]):
        refs[-1][k] = part[...]


def own_kernel(sel, weight_in, bias_in, stitch_in, out, weight, bias, stitch, done):
    copies = [
        pltpu.make_async_copy(weight_in.at[sel[S]], weight, done.at[0]),
        pltpu.make_async_copy(bias_in, bias, done.at[1]),
        pltpu.make_async_copy(stitch_in, stitch, done.at[2]),
    ]
    for copy in copies:
        copy.start()
    for copy in copies:
        copy.wait()
    out[:, :ROWS] = weight[...]
    values = jnp.concatenate([bias[...], stitch[0], stitch[1], jnp.zeros((2, 64), F32)], 0)
    pieces = []
    for _ in range(3):
        pieces.append(values.astype(BF16).astype(F32))
        values = values - pieces[-1]
    zeros = jnp.zeros((BLK, 64), F32)
    rows = jnp.concatenate([zeros, *pieces, jnp.zeros((8, 64), F32)], 0)
    last = slice(ROWS - BLK, ROWS + 32)
    tile = jnp.where(lane_index(64) < BLK, out[:, last].astype(F32), rows.T)
    out[:, last] = tile.astype(BF16)


def kernels_kernel(sel, *refs):
    rows_out, params = refs[6:]
    blocks = []
    for first, second, third in (refs[:3], refs[3:6]):
        blocks += [first.at[0], first.at[1], second, third]
    d, m = sel[D], sel[M]
    odd = lax.rem(m, 2) == 1
    for k in range(4):
        for x in range(2):
            own = blocks[k][x].astype(F32)
            other = blocks[4 + k][x].astype(F32)
            even_rows = jnp.where(odd, other, own)
            odd_rows = jnp.where(odd, own, other)
            turned = jnp.concatenate([even_rows, odd_rows], 0).T
            tile = pl.multiple_of((lax.div(m, 2) ^ x) * 128, 128)
            if k == 0:
                values = turned[ROWS : ROWS + 8] + turned[ROWS + 8 : ROWS + 16]
                params[:, pl.ds(tile, 128)] = values + turned[ROWS + 16 : ROWS + 24]
            turned = turned.astype(BF16)
            for part in range(9):
                index = 9 * (d ^ k) + part
                first = lax.div(index, 4) * (4 * BLK)
                block = lax.rem(index, 4) ^ m
                for piece in range(3):
                    place = first + jnp.where(
                        block == 3, 128 * piece + BLK, 128 * block + 32 * piece
                    )
                    start = part * BLK + 32 * piece
                    rows_out[pl.ds(pl.multiple_of(place, 32), 32), pl.ds(tile, 128)] = turned[
                        start : start + 32
                    ]


def gather_kernels(conv_weight, conv_bias, conv_stitch, sel, s, m, token):
    turned = conv_weight.transpose(0, 2, 1)
    rows = turned.shape[2]
    if lax.axis_size("dp") == 4:
        shape = struct((64, rows + 32), BF16)
        inputs = [turned, conv_bias, conv_stitch]
        own = call(
            own_kernel,
            "own_kernels",
            [sel] + [pltpu.with_memory_space_constraint(v, pltpu.HBM) for v in inputs],
            shape,
            scratch=[pltpu.VMEM((64, rows), BF16)]
            + [pltpu.VMEM(v.shape, F32) for v in inputs[1:]]
            + [pltpu.SemaphoreType.DMA((3,))],
            specs=[SMEM] + [HBM] * 3,
        )
        near = call(
            join_kernel,
            "join_kernels",
            [own, swap(own, "mp", 2)],
            struct((2, *own.shape), BF16),
            (token,),
        )
        column = {k: swap(near, "dp", k) for k in (3, 2, 1)}
        column = [near, column[1], column[2], column[3]]
        first = call(join_kernel, "join_columns", column[:2], struct((2, *near.shape), BF16))
        column = [first, *column[2:]]
        across = [swap(part, "mp", 1) for part in column]
        kernel, params = call(
            kernels_kernel,
            "kernels",
            [sel, *column, *across],
            [struct((4 * rows, OUT), BF16), struct((8, OUT), F32)],
        )
        return kernel, params, near
    own = lax.dynamic_index_in_dim(conv_weight, s, 0, keepdims=False)
    full = lax.all_gather(lax.all_gather(own, "dp", axis=0), "mp", axis=2, tiled=True)
    kernel = relative(full.reshape(9, 4, BLK, OUT), m, 1)
    last = kernel[:, 3].reshape(9, 3, 32, OUT)
    kernel = jnp.concatenate([kernel[:, :3], last], 2).reshape(36 * BLK, OUT)
    params = jnp.concatenate([conv_bias, conv_stitch.reshape(4, 64), jnp.zeros((2, 64), F32)], 0)
    params = lax.all_gather(params, "mp", axis=1, tiled=True)
    return kernel, params, jnp.zeros((8, 128), F32)


def split_kernel(sel, grad, small, keep, send):
    d, m = sel[D], sel[M]
    odd = lax.rem(m, 2) == 1
    lane = lane_index(32)

    def write(rows, place):
        count = rows.shape[0]
        t0, t1 = rows[:, 0:128], rows[:, 128:256]
        low = jnp.where(lane[:count] < 64, t0, pltpu.roll(t1, 64, 1)).astype(BF16)
        high = jnp.where(lane[:count] < 64, pltpu.roll(t0, 64, 1), t1).astype(BF16)
        here = pl.ds(pl.multiple_of(place, 16), count)
        keep[here, :] = jnp.where(odd, high, low)
        send[here, :] = jnp.where(odd, low, high)

    for tap in range(9):
        for block in range(4):
            index = tap * 4 + (block ^ m)
            part = lax.div(index, 9)
            place = (part ^ d) * (ROWS + 16) + (index - part * 9) * BLK
            for piece in range(3):
                start = tap * 4 * BLK + (128 * piece + BLK if block == 3 else 128 * block + 32 * piece)
                write(grad[start : start + 32, :], place + 32 * piece)
    sums = jnp.concatenate([small[...], jnp.zeros((16 - small.shape[0], OUT), F32)], 0)
    for part in range(4):
        write(sums, part * (ROWS + 16) + ROWS)


def pair_kernel(keep, arrived, own, *sends):
    size = ROWS + 16
    for k in range(4):
        here = slice(k * size, (k + 1) * size)
        total = keep[here, :].astype(F32) + arrived[here, :].astype(F32)
        if k == 0:
            own[...] = total
        else:
            sends[k - 1][...] = total.astype(BF16)


def turn_kernel(sel, own, a, b, c, mine, send):
    total = own[...] + a[...].astype(F32) + b[...].astype(F32) + c[...].astype(F32)
    total = jnp.concatenate([total, jnp.zeros((16, 128), F32)], 0).T
    low = sel[M] < 2
    mine[...] = jnp.where(low, total[:64], total[64:])
    send[...] = jnp.where(low, total[64:], total[:64]).astype(BF16)


def finish_kernel(sel, mine, arrived, rows, bias, stitch):
    rows[...] = mine[:, :ROWS] + arrived[:, :ROWS].astype(F32)
    last = slice(ROWS - BLK, ROWS + 32)
    small = (mine[:, last] + arrived[:, last].astype(F32)).T
    stitch[pl.ds(sel[S], 1), :] = small[BLK : BLK + 1]
    stitch[pl.ds(1 - sel[S], 1), :] = small[BLK + 1 : BLK + 2]
    bias[...] = small[BLK + 2 : BLK + 3]


def scatter_kernels(grad, small, sel, s, m, meanwhile, finish_fc):
    rows = grad.shape[0] // lax.axis_size("dp")
    small_shapes = [struct((1, 64), F32), struct((2, 64), F32)]
    if lax.axis_size("dp") == 4:
        size = ROWS + 16
        keep, send = call(
            split_kernel, "split_kernels", [sel, grad, small], [struct((4 * size, 128), BF16)] * 2
        )
        own, *sends = call(
            pair_kernel,
            "pair_kernels",
            [keep, swap(send, "mp", 1)],
            [struct((size, 128), F32)] + [struct((size, 128), BF16)] * 3,
            meanwhile(),
        )
        last = call(
            copy_kernel, "last_kernels", sends[2:], struct((size, 128), BF16), finish_fc(own)
        )
        arrived = [swap(part, "dp", k) for k, part in zip((1, 2, 3), (*sends[:2], last))]
        mine, other = call(
            turn_kernel,
            "turn_kernels",
            [sel, own, *arrived],
            [struct((64, ROWS + 32), F32), struct((64, ROWS + 32), BF16)],
        )
        result, bias, stitch = call(
            finish_kernel,
            "finish_kernels",
            [sel, mine, swap(other, "mp", 2)],
            [struct((64, ROWS), F32), *small_shapes],
        )
        return result.T, bias, stitch, own
    grad = grad.reshape(9, 3, 128, OUT)
    last = grad[:, :, BLK:].reshape(9, 1, BLK, OUT)
    grad = jnp.concatenate([grad[:, :, :BLK], last], 1)
    grad = relative(grad, m, 1).reshape(36 * BLK, OUT).astype(BF16)
    grad = lax.psum_scatter(grad, "mp", scatter_dimension=1, tiled=True)
    grad = lax.psum_scatter(grad, "dp", scatter_dimension=0, tiled=True).astype(F32)
    small = sum_over(sum_over(small, "dp"), "mp")
    small = lax.dynamic_slice_in_dim(small, m * 64, 64, 1)
    stitch = jnp.stack([jnp.where(s == 0, small[0], small[1]), jnp.where(s == 0, small[1], small[0])])
    meanwhile()
    finish_fc(small)
    return grad, small[2:3], stitch, small


def gelu_parts(value):
    scale = 0.7978845608028654
    square = value * value
    curve = jnp.tanh(scale * value * (1.0 + 0.044715 * square))
    return curve, square, scale


def gelu(value):
    curve, _, _ = gelu_parts(value)
    return 0.5 * value * (1.0 + curve)


def gelu_slope(value):
    curve, square, scale = gelu_parts(value)
    bend = (0.5 * scale) * value * (1.0 - curve * curve) * (1.0 + 0.134145 * square)
    return 0.5 * (1.0 + curve) + bend


def place_of(sel, k, p):
    return 9 * (lax.rem(sel[D], 4) ^ k) + p


def half_kernel(first, sel, pooled, out):
    for k in range(2):
        for p in range(9):
            out[k, p] = pooled[place_of(sel, first + k, p)].astype(BF16)


def pool_kernel(sel, conv_out, params, pooled, far):
    extent = jnp.where(is_low(sel), POOL_LOW, POOLED)
    shift = params[pl.ds(sel[S], 1), :]
    lines = []
    for i in range(SIDE):
        cells = [gelu(conv_out[i, j] + shift) for j in range(SIDE)]
        lines.append([cells[2 * q] + cells[2 * q + 1] + cells[2 * q + 2] for q in range(POOLED)])
        if i >= 2 and i % 2 == 0:
            p = i // 2 - 1
            for q in range(POOLED):
                total = lines[i - 2][q] + lines[i - 1][q] + lines[i][q]
                keep = jnp.logical_and(p < extent, q < extent).astype(F32) / 9.0
                total = total * keep
                pooled[POOLED * p + q] = total
    half_kernel(2, sel, pooled, far)


def slope_kernel(sel, conv_out, params, slope):
    shift = params[pl.ds(sel[S], 1), :]
    for i in range(SIDE):
        for j in range(SIDE):
            slope[SIDE * i + j] = gelu_slope(conv_out[i, j] + shift)


def entry(params, t, u):
    return params[pl.ds(2 + 2 * t + u, 1), :]


def stitch_kernel(first, sel, pooled, other, params, *chunks):
    s = sel[S]
    by_own, by_other = entry(params, s, s), entry(params, s, 1 - s)
    for k, chunk in enumerate(chunks):
        for p in range(9):
            mixed = by_own * pooled[place_of(sel, first + k, p)] + by_other * other[k, p].astype(F32)
            chunk[p] = mixed.astype(BF16)


def conv_grad_kernel(
    sel, near, far, near_other, far_other, slope, pooled, near_pooled, far_pooled, params, out, sums, mixed
):
    extent, s = jnp.where(is_low(sel), POOL_LOW, POOLED), sel[S]
    by_own, by_other = entry(params, s, s), entry(params, 1 - s, s)
    own_sum = other_sum = jnp.zeros((IMG, OUT), F32)
    for k in range(4):
        grad = near.at[k] if k < 3 else far
        grad_other = near_other.at[k] if k < 3 else far_other
        pooled_other = (near_pooled, far_pooled)[k // 2]
        for p in range(9):
            place = place_of(sel, k, p)
            mine = grad[p].astype(F32)
            mixed[place] = by_own * mine + by_other * grad_other[p].astype(F32)
            own_sum = own_sum + mine * pooled[place]
            other_sum = other_sum + mine * pooled_other[k % 2, p].astype(F32)
    spread = []
    for p in range(POOLED):
        line = []
        for q in range(POOLED):
            keep = jnp.logical_and(p < extent, q < extent).astype(F32) / 9.0
            line.append(mixed[POOLED * p + q] * keep)
        spread.append(line)
    bias_sum = jnp.zeros((IMG, OUT), F32)

    def over(values, index):
        near, far = index // 2, index // 2 - 1
        if index % 2 == 1 or index == 0:
            return values[near]
        if near >= POOLED:
            return values[far]
        return values[near] + values[far]

    for i in range(SIDE):
        line = [over([spread[p][q] for p in range(POOLED)], i) for q in range(POOLED)]
        for j in range(SIDE):
            cell = SIDE * i + j
            value = (slope[cell] * over(line, j)).astype(BF16)
            out[cell] = value
            bias_sum = bias_sum + value.astype(F32)
    for row, total in enumerate((own_sum, other_sum, bias_sum)):
        sums[row : row + 1, :] = jnp.sum(total, 0, keepdims=True)


def all_acts(acts, place):
    return jnp.concatenate([a[:, place].reshape(-1, OUT) for a in acts], 0)


def all_grads(grads):
    return jnp.concatenate([g[r] for r in range(4) for g in grads], 0)


def load_kernel(sel, weight, out, token, done):
    token[...] = jnp.zeros(token.shape, F32)
    count = done.shape[0]
    size = weight.shape[1] // count
    copies = []
    for part in range(count):
        here = pl.ds(part * size, size)
        copies.append(pltpu.make_async_copy(weight.at[sel[S], here], out.at[here], done.at[part]))
        copies[-1].start()
    for copy in copies:
        copy.wait()


def load_matrix(weight, sel, s, after):
    if lax.axis_size("dp") != 4:
        return lax.dynamic_index_in_dim(weight, s, 0, keepdims=False), ()
    matrix, token = call(
        load_kernel,
        "load_matrix",
        [sel, pltpu.with_memory_space_constraint(weight, pltpu.HBM)],
        [struct(weight.shape[1:], BF16), struct((8, 128), F32)],
        after,
        scratch=[pltpu.SemaphoreType.DMA((9,))],
        specs=[SMEM, HBM],
    )
    return matrix, (token,)


def fc_forward_kernel(*refs):
    acts, (weight, own, *sends) = refs[:8], refs[8:]
    rows = jnp.concatenate([all_acts(acts, p) for p in range(9)], 1)
    for n in range(weight.shape[1] // 256):
        here = slice(n * 256, (n + 1) * 256)
        term = jnp.dot(rows, weight[:, here], preferred_element_type=F32)
        for r in range(4):
            for k in range(4):
                part = term[(4 * r + k) * IMG : (4 * r + k + 1) * IMG]
                if k == 0:
                    own[r, :, here] = part
                else:
                    sends[k - 1][r, :, here] = part.astype(BF16)


def fc_active_kernel(sel, own, a, b, c, bias, stitch, cot, grad, active, sent, sums):
    s, m = sel[S], sel[M]
    for n in range(own.shape[2] // 256):
        here = slice(n * 256, (n + 1) * 256)
        shift = bias[pl.ds(s, 1), here]
        w0, w1 = stitch[0, pl.ds(s, 1), here], stitch[1, pl.ds(s, 1), here]
        sum0 = sum1 = jnp.zeros((IMG, 256), F32)
        for r in range(4):
            value = own[r, :, here] + a[r, :, here].astype(F32)
            value = value + (b[r, :, here].astype(F32) + c[r, :, here].astype(F32)) + shift
            curve, square, scale = gelu_parts(value)
            half = 0.5 * (1.0 + curve)
            bend = (0.5 * scale) * value * (1.0 - curve * curve) * (1.0 + 0.134145 * square)
            result = value * half
            c0, c1 = cot[0, m ^ r, :, here].astype(F32), cot[1, m ^ r, :, here].astype(F32)
            grad[r, :, here] = ((half + bend) * (w0 * c0 + w1 * c1)).astype(BF16)
            active[r, :, here] = result
            sent[r, :, here] = result.astype(BF16)
            sum0 = sum0 + c0 * result
            sum1 = sum1 + c1 * result
        for t, total in enumerate((sum0, sum1)):
            sums[4 * t + n : 4 * t + n + 1, :] = jnp.sum(total, 0, keepdims=True)


def fc_rows_kernel(*refs):
    grads, (weight, keep, send) = refs[:-3], refs[-3:]
    rows = all_grads(grads)
    for p in range(9):
        term = lax.dot_general(
            rows,
            weight[p * 256 : (p + 1) * 256, :],
            (((1,), (1,)), ((), ())),
            preferred_element_type=F32,
        )
        term = term.reshape(4, len(grads), IMG, 256)
        for r in range(4):
            if r % 2 == 0:
                keep[r // 2, :, p] = term[r]
            else:
                send[r // 2, :, p] = term[r].astype(BF16)


def cross_kernel(keep, arrived, out):
    out[...] = (keep[1] + arrived[1].astype(F32)).astype(BF16)


def home_kernel(keep, arrived, crossed, sums, *chunks):
    high = sums[...].astype(BF16).astype(F32)
    small = jnp.concatenate([high, sums[...] - high], 0).astype(BF16)
    for k in range(len(chunks)):
        total = keep[0, k] + arrived[0, k].astype(F32) + crossed[k].astype(F32)
        chunks[k][0:9] = total.astype(BF16)
        chunks[k][9] = small


def fc_matrix_kernel(*refs):
    acts, refs = refs[:8], refs[8:]
    g0, g1, g2, g3, out, bias, token, part, sent = refs
    token[...] = jnp.zeros(token.shape, F32)
    grads = all_grads((g0, g1, g2, g3))

    def copy(p):
        return pltpu.make_async_copy(part.at[p % 3], out.at[pl.ds(p * 256, 256)], sent.at[p % 3])

    for p in range(9):
        rows = all_acts(acts, p).T
        if p >= 3:
            copy(p - 3).wait()
        part[p % 3] = jnp.dot(rows, grads, preferred_element_type=F32)
        copy(p).start()
    bias[...] = jnp.sum(grads.astype(F32), 0, keepdims=True)
    for p in range(6, 9):
        copy(p).wait()


def copy_kernel(value, out):
    out[...] = value[...]


def outputs_kernel(sel, active, arrived, stitch, out):
    s, m = sel[S], sel[M]
    for n in range(active.shape[2] // 256):
        here = slice(n * 256, (n + 1) * 256)
        by_own = jnp.where(s == 0, stitch[0, 0:1, here], stitch[1, 1:2, here])
        by_other = jnp.where(s == 0, stitch[0, 1:2, here], stitch[1, 0:1, here])
        for r in range(4):
            mixed = by_own * active[r, :, here] + by_other * arrived[r, :, here].astype(F32)
            out[m ^ r, :, here] = mixed.astype(BF16)


def plane_sum(near, far):
    total = jnp.zeros((8, OUT), F32)
    for plane in (near[0, 9], near[1, 9], near[2, 9], far[9]):
        plane = plane.astype(F32)
        total = total + (plane[0:8] + plane[8:16])
    return total


def stitch_sums_kernel(sel, near, far, near_other, far_other, out, own, other):
    s = sel[S]
    own[...] = plane_sum(near, far)
    other[...] = plane_sum(near_other, far_other)
    for n in range(4):
        here = slice(n * OUT, (n + 1) * OUT)
        out[pl.ds(s, 1), here] = own[pl.ds(4 * s + n, 1), :]
        out[pl.ds(1 - s, 1), here] = other[pl.ds(4 * s + n, 1), :]


def fc_section(pooled, near, far, params, own_weight, bias, stitch, cot, sel, s, d, m):
    count = lax.axis_size("dp")
    hid = own_weight.shape[1]
    plane = struct((9, IMG, OUT), BF16)
    block = struct((4, IMG, hid), BF16)
    token = struct((8, 128), F32)
    chunks = [None] * 4
    chunks[2:] = call(
        partial(stitch_kernel, 2), "stitch_far", [sel, pooled, far, params], [plane] * 2
    )
    chunks[:2] = call(
        partial(stitch_kernel, 0), "stitch_near", [sel, pooled, near, params], [plane] * 2, chunks[2:3]
    )
    if count == 4:
        def over_mp(acts):
            far = swap(acts, "mp", 2)
            return [acts, swap(acts, "mp", 1), far, swap(far, "mp", 1)]

        two = struct((2, 9, IMG, OUT), BF16)
        moved = [swap(chunks[2], "dp", 2), swap(chunks[3], "dp", 3)]
        far_acts = call(join_kernel, "join_acts_far", moved, two)
        moved = [chunks[0], swap(chunks[1], "dp", 1)]
        near_acts = call(join_kernel, "join_acts_near", moved, two, (far_acts,))
        acts = [a for pair in zip(over_mp(near_acts), over_mp(far_acts)) for a in pair]
        pre, *sends = call(
            fc_forward_kernel,
            "fc_forward",
            [*acts, own_weight],
            [struct((4, IMG, hid), F32)] + [block] * 3,
        )
        arrived = [swap(part, "dp", k) for k, part in zip((1, 2, 3), sends)]
    else:
        shared = by_position(chunks, d)
        flat = shared.transpose(1, 0, 2).reshape(IMG, count, -1).transpose(1, 0, 2)
        flat = lax.all_to_all(flat, "dp", 0, 0, tiled=True)
        flat = lax.all_gather(flat, "mp", axis=0)
        flat = relative(flat, m)
        pre = jnp.einsum("rdnf,fk->drnk", flat, own_weight, preferred_element_type=F32)
        pre = lax.psum_scatter(pre.astype(BF16), "dp", scatter_dimension=0, tiled=True)
        pre = pre.reshape(4, IMG, hid).astype(F32)
        arrived = [jnp.zeros(block.shape, BF16)] * 3
    pre_grad, active, sent, sums = call(
        fc_active_kernel,
        "fc_active",
        [sel, pre, *arrived, bias, stitch, cot],
        [block, struct(block.shape, F32), block, struct((8, OUT), F32)],
    )
    if count == 4:
        grads = gather4(pre_grad)
        ten = struct((10, IMG, OUT), BF16)

        def home(ks, name, after=()):
            shape = (2, len(ks), 9, IMG, OUT)
            keep, send = call(
                fc_rows_kernel,
                "fc_rows_" + name,
                [*[grads[k] for k in ks], own_weight],
                [struct(shape, F32), struct(shape, BF16)],
                after,
            )
            arrived = swap(send, "mp", 1)
            crossing = call(cross_kernel, "cross_" + name, [keep, arrived], struct(shape[1:], BF16))
            crossed = swap(crossing, "mp", 2)
            inputs = [keep, arrived, crossed, sums]
            return call(home_kernel, "home_" + name, inputs, [ten] * len(ks))

        chunks = home((0, 1, 2), "near")
        moved = [chunks[0], swap(chunks[1], "dp", 1), swap(chunks[2], "dp", 2)]
        (chunk,) = home((3,), "far")
        def matrix_gradient(after, grads=tuple(grads)):
            return call(
                fc_matrix_kernel,
                "fc_matrix",
                [*acts, *grads],
                [struct(own_weight.shape, F32), struct((1, hid), F32), token],
                after,
                scratch=[pltpu.VMEM((3, 256, hid), F32), pltpu.SemaphoreType.DMA((3,))],
                limit=10 << 20,
                out_specs=[HBM, VMEM, VMEM],
            )

        near_grad = call(join_kernel, "join_near", moved, struct((3, *ten.shape), BF16), (chunk,))
        near_back = (near_grad, swap(near_grad, "section", 1))
        far_grad = swap(chunk, "dp", 3)
        far_back = (far_grad, swap(far_grad, "section", 1))
    else:
        grads = lax.all_gather(pre_grad, "dp", axis=0)
        rows = jnp.einsum("drnk,fk->rdnf", grads, own_weight, preferred_element_type=F32)
        rows = relative(rows, m).astype(BF16)
        rows = lax.psum_scatter(rows, "mp", scatter_dimension=0, tiled=True)[0]
        rows = lax.all_to_all(rows, "dp", 0, 0, tiled=True)
        back = rows.transpose(1, 0, 2).reshape(IMG, 4, 9, OUT).transpose(1, 2, 0, 3)
        matrix_grad = jnp.einsum("rdnf,drnk->fk", flat, grads, preferred_element_type=F32)
        bias_sum = jnp.sum(grads.astype(F32), (0, 1, 2))[None]

        def matrix_gradient(after):
            return matrix_grad, bias_sum, sums

        total = sum_over(sums, "dp")
        high = lax.reduce_precision(total, 8, 7)
        small = jnp.concatenate([high, total - high], 0).astype(BF16)
        small = jnp.stack([small] + [jnp.zeros_like(small)] * 3)
        back = jnp.concatenate([relative(back, lax.rem(d, 4)), small[:, None]], 1)
        near_back, far_back = [(part, swap(part, "section", 1)) for part in (back[:3], back[3])]
    stitch_sum = call(
        stitch_sums_kernel,
        "stitch_sums",
        [sel, near_back[0], far_back[0], near_back[1], far_back[1]],
        struct((2, hid), F32),
        scratch=[pltpu.VMEM((8, OUT), F32)] * 2,
    )
    grads = [near_back[0], far_back[0], near_back[1], far_back[1]]
    return grads, (active, sent), matrix_gradient, stitch_sum


def by_position(chunks, d):
    return relative(jnp.stack(chunks), lax.rem(d, 4)).reshape(PLACES, IMG, OUT)


def conv(maps, taps, rows, form, kind=F32):
    return lax.conv_general_dilated(
        maps,
        taps,
        (1, 1),
        (rows, (1, 1)),
        dimension_numbers=form,
        preferred_element_type=F32,
    ).astype(kind)


def on_device(
    conv_input,
    group_ids,
    conv_weight,
    conv_bias,
    conv_stitch,
    fc_weight,
    fc_bias,
    fc_stitch,
    cotangent,
):
    s = lax.axis_index("section")
    d = lax.axis_index("dp")
    m = lax.axis_index("mp")
    assert conv_input.shape == (4, IMG, 2, SIDE, SIDE, BLK) and lax.axis_size("mp") == 4
    sel = jnp.concatenate([scalars(s, d, m), group_ids])

    by_row = conv_input.transpose(0, 1, 3, 4, 2, 5).reshape(4, IMG * CELLS * 2, BLK)
    by_row = pltpu.with_memory_space_constraint(by_row, pltpu.HBM)
    far3, far2, token = pack_maps(by_row, sel, 3)
    kernel, params, early = gather_kernels(conv_weight, conv_bias, conv_stitch, sel, s, m, token)
    cot = lax.dynamic_slice_in_dim(cotangent, d * IMG, IMG, 1).transpose(2, 0, 1, 3)
    matrix, loaded = load_matrix(fc_weight, sel, s, (token,))
    near1, near0, token = pack_maps(by_row, sel, 1, (token, early, cot, *loaded))
    wires = [near0, swap(near1, "mp", 1), swap(far2, "mp", 2), swap(far3, "mp", 3)]

    taps = kernel.reshape(3, 3, 4 * BLK, OUT)
    maps = call(
        unpack_kernel,
        "unpack_maps",
        [sel, *wires],
        struct((CELLS * IMG, 4 * BLK), BF16),
    )
    maps = maps.reshape(SIDE, SIDE, IMG, 4 * BLK)
    conv_out = conv(maps, taps, (1, 1), ("HWNC", "HWIO", "HWNC"))
    half = struct((2, 9, IMG, OUT), BF16)
    pooled, far = call(
        pool_kernel, "pool", [sel, conv_out, params], [struct((PLACES, IMG, OUT), F32), half]
    )
    near = call(partial(half_kernel, 0), "pool_near", [sel, pooled], half)
    far = swap(far, "section", 1)
    near = swap(near, "section", 1)

    back, outputs, matrix_gradient, fc_stitch_sum = fc_section(
        pooled, near, far, params, matrix, fc_bias, fc_stitch, cot, sel, s, d, m
    )
    slope = call(
        slope_kernel,
        "slope",
        [sel, conv_out, params],
        struct((CELLS, IMG, OUT), F32),
        (back[0],),
    )
    conv_grad, sums = call(
        conv_grad_kernel,
        "conv_gradient",
        [sel, *back, slope, pooled, near, far, params],
        [struct((CELLS, IMG, OUT), BF16), struct((3, OUT), F32)],
        scratch=[pltpu.VMEM((PLACES, IMG, OUT), F32)],
    )
    conv_grad = conv_grad.reshape(SIDE, SIDE, IMG, OUT)

    back_taps = taps[::-1, ::-1]
    wires = []

    def send_input_grad(after=()):
        chunk = len(wires)
        low, high = HALVES[chunk]
        padding = (1 - low, 1 - SIDE + high)
        part = conv(conv_grad, back_taps, padding, ("HWNC", "HWOI", "HWNC"), BF16)
        sends = pack_grad(part.reshape(-1, 4 * BLK), sel, HALVES[chunk], after)
        wires.append([sends[0]] + [swap(sends[k], "mp", k) for k in (1, 2, 3)])
        return (sends[0],)

    maps = pass_on(maps, send_input_grad())
    kernel_grad = conv(maps, conv_grad, (1, 1), ("HWCN", "HWIO", "HWNC"))
    results = []

    def finish_fc(begun):
        results.extend(matrix_gradient((begun,)))
        return results[-1:]

    kernel_rows, conv_bias_sum, conv_stitch_sum, begun = scatter_kernels(
        kernel_grad.reshape(36 * BLK, OUT), sums, sel, s, m, lambda: (), finish_fc
    )
    matrix_grad, fc_bias_sum, _ = results
    mark = send_input_grad((*wires[0][2:], begun))
    active, sent = outputs
    sent = call(copy_kernel, "outputs_send", [sent], struct(sent.shape, BF16), mark)
    outputs = call(
        outputs_kernel,
        "outputs",
        [sel, active, swap(sent, "section", 1), fc_stitch],
        struct(sent.shape, BF16),
    )
    input_grad = place_grad(wires[0], sel, HALVES[0], (0, 1, 2, 3), None)
    input_grad = place_grad(wires[1][:2], sel, HALVES[1], (0, 1), input_grad)
    input_grad = place_grad(wires[1][2:], sel, HALVES[1], (2, 3), input_grad)
    input_grad = input_grad.reshape(4, 1, SIDE, SIDE, IMG, BLK).transpose(0, 4, 1, 2, 3, 5)
    return (
        outputs[:, :, None],
        input_grad,
        kernel_rows[None],
        conv_bias_sum,
        conv_stitch_sum[None],
        matrix_grad[None],
        fc_bias_sum,
        fc_stitch_sum[None],
    )


def solution(mesh):
    placed = (
        P(None, "dp", None, None, None, "mp"),
        P(),
        P(None, "dp", "mp"),
        P(None, "mp"),
        P(None, None, "mp"),
        P(None, "dp", "mp"),
        P(None, "mp"),
        P(None, None, "mp"),
        P(None, None, None, "mp"),
    )
    return jax.shard_map(
        on_device,
        mesh=mesh,
        in_specs=placed,
        out_specs=(
            P(None, "dp", "section", "mp"),
            P(None, "dp", "section", None, None, "mp"),
            P("section", "dp", "mp"),
            P("section", "mp"),
            P("section", None, "mp"),
            P("section", "dp", "mp"),
            P("section", "mp"),
            P("section", None, "mp"),
        ),
        check_vma=False,
    )
```
